32 devices in a mesh: dp: 16 (over z, x, core), fsdp: 2 (over y).
Axes of the slice: x: 2, y: 2, z: 4, core: 2. Of those that a mesh axis runs over, the one named last changes fastest.
Arguments:
- tokens: bfloat16 [32768, 1024], P(('dp', 'fsdp')), may hold values from -6 to 6
- incoming: bfloat16 [32, 512, 1024], P(('dp', 'fsdp')), may hold values from -6 to 6
- document_lengths: int32 [8], replicated, may hold values from 1 to 17408, as said below
- output_grad: bfloat16 [32768, 1024], P(('dp', 'fsdp')), may hold values from -12 to 12
- token_proj: bfloat16 [1024, 4096], P('dp', 'fsdp'), may hold values from -0.1875 to 0.1875
- state_proj: bfloat16 [1024, 4096], P('dp', 'fsdp'), may hold values from -0.1875 to 0.1875
- token_out: bfloat16 [2048, 1024], P('dp', 'fsdp'), may hold values from -1 to 1
- state_out: bfloat16 [2048, 1024], P('dp', 'fsdp'), may hold values from -1 to 1
- gate_weight: bfloat16 [1024, 1024], P('dp', 'fsdp'), may hold values from -0.1875 to 0.1875
- init_state: bfloat16 [512, 1024], P('dp', 'fsdp'), may hold values from -6 to 6
- hidden_in: bfloat16 [1024, 4096], P('dp', 'fsdp'), may hold values from -0.1875 to 0.1875
- hidden_out: bfloat16 [4096, 1024], P('dp', 'fsdp'), may hold values from -0.09375 to 0.09375
- token_gain: bfloat16 [1024], P('fsdp'), may hold values from 0.5 to 1.5
- state_gain: bfloat16 [1024], P('fsdp'), may hold values from 0.5 to 1.5
- hidden_gain: bfloat16 [1024], P('fsdp'), may hold values from 0.5 to 1.5
- gate_bias: bfloat16 [1024], P('fsdp'), may hold values from -4 to 4
Outputs:
- result: bfloat16 [32768, 1024], P(('dp', 'fsdp'))
- final_states: bfloat16 [32, 512, 1024], P(('dp', 'fsdp'))
- tokens_grad: bfloat16 [32768, 1024], P(('dp', 'fsdp'))
- token_proj_grad: float32 [1024, 4096], P('dp', 'fsdp')
- state_proj_grad: float32 [1024, 4096], P('dp', 'fsdp')
- token_out_grad: float32 [2048, 1024], P('dp', 'fsdp')
- state_out_grad: float32 [2048, 1024], P('dp', 'fsdp')
- gate_weight_grad: float32 [1024, 1024], P('dp', 'fsdp')
- init_state_grad: float32 [512, 1024], P('dp', 'fsdp')
- hidden_in_grad: float32 [1024, 4096], P('dp', 'fsdp')
- hidden_out_grad: float32 [4096, 1024], P('dp', 'fsdp')
- token_gain_grad: float32 [1024], P('fsdp')
- state_gain_grad: float32 [1024], P('fsdp')
- hidden_gain_grad: float32 [1024], P('fsdp')
- gate_bias_grad: float32 [1024], P('fsdp')
The draws below stay inside these ranges and needn't reach their ends.
Inputs may be any that keep to these rules, and one draw needn't show every extreme that they name: `document_lengths`: the documents fill exactly 32 segments: the sum over documents of ceil(length / 1024) is 32. Exactly one document has the largest length; every other one has at most (9) * 1024 tokens.
All inputs are finite; a program needn't handle non-finite values.
Results may differ from the reference program's by a relative error of at most 0.019.
Values may be sent and summed in bfloat16 or wider, within the bound.
No kernel may reach another device: no remote copies, remote signals or barrier semaphores. Data moves between devices by JAX's collectives and lax.ppermute only.
A program may use at most 448 MiB of HBM per device.

```python
import math
import jax
import jax.numpy as jnp
from jax import lax

D = 1024
HD = 128
FF = 4096
NS = 512
WINDOW = 512
SEG_LEN = 1024
BLOCKS = 2
SEGS = 32
DOCS = 8
TOKENS = 32768


def draw_document_lengths(key, part):
    key = jax.random.fold_in(key, 7)
    order_key, tail_key, place_key = jax.random.split(key, 3)
    longest = SEGS // 2 + 1
    rest = SEGS - longest
    picks = jax.random.permutation(order_key, rest - 1)[:DOCS - 2] + 1
    bounds = jnp.concatenate([jnp.zeros((1,), jnp.int32), jnp.sort(picks).astype(jnp.int32), jnp.full((1,), rest, jnp.int32)])
    others = bounds[1:] - bounds[:-1]
    place = jax.random.randint(place_key, (), 0, DOCS)
    index = jnp.arange(DOCS, dtype=jnp.int32)
    source = jnp.clip(index - (index > place).astype(jnp.int32), 0, DOCS - 2)
    counts = jnp.where(index == place, longest, others[source])
    tails = jax.random.randint(tail_key, (DOCS,), 1, SEG_LEN + 1)
    tails = jnp.where(index == place, SEG_LEN, tails)
    return ((counts - 1) * SEG_LEN + tails).astype(jnp.int32)


def strengthened(values, stream_key, source, target, shards_of, factor):
    owner, partner = [(jnp.arange(values.shape[axis_at]) // (values.shape[axis_at] // shards_of)).reshape([-1 if axis == axis_at else 1 for axis in range(values.ndim)]) for axis_at in (source, target)]
    chosen = jax.random.permutation(stream_key, shards_of)[partner]
    strong = (owner == chosen) | (owner == (partner + shards_of // 2) % shards_of)
    return jnp.where(strong, factor * values, values)


def block_scale(stream_key, extent, cuts, least, high):
    loudness = 1.0
    for axis_at, blocks in cuts:
        steps = jax.random.uniform(jax.random.fold_in(jax.random.fold_in(stream_key, 6), axis_at), (blocks,), jnp.float32, least / len(cuts), high / len(cuts))
        loudness = loudness * jnp.repeat(jnp.exp(steps), extent[axis_at] // blocks).reshape((-1,) + (1,) * (len(extent) - 1 - axis_at))
    return loudness


def normal_values(stream_key, dims, scale, limit, cuts=(), kind=jnp.bfloat16):
    level = block_scale(stream_key, dims, cuts, -0.22, 0.18) if cuts else 1.0
    entries = jax.random.normal(stream_key, dims, jnp.float32) * scale * level
    return jnp.minimum(jnp.maximum(entries, -limit), limit).astype(kind)


def gaussian_with(key, dims, spread, limit, cuts, heavy, kind=jnp.bfloat16):
    values = spread * jax.random.normal(key, dims, jnp.float32)
    if cuts:
        values = values * block_scale(key, dims, cuts, -0.22, 0.18)
    return jnp.clip(strengthened(values, jax.random.fold_in(key, 3), *heavy), -limit, limit).astype(kind)


def setup_inputs(seed: int = 0) -> dict:
    streams_of = jax.random.split(jax.random.key(seed), 17)
    tokens = normal_values(streams_of[0], (TOKENS, D), 1.0, 6.0, ((0, 32),))
    incoming = normal_values(streams_of[1], (SEGS, NS, D), 1.0, 6.0, ((0, 32),))
    document_lengths = draw_document_lengths(jax.random.fold_in(streams_of[16], 71), 0)
    output_grad = gaussian_with(streams_of[3], (TOKENS, D), 1.0, 12.0, ((0, 32),), (0, 1, 32, 2.75))
    token_proj = normal_values(streams_of[4], (D, 4 * D), D ** -0.5, 0.1875, ((0, 16), (1, 2)))
    state_proj = normal_values(streams_of[5], (D, 4 * D), D ** -0.5, 0.1875, ((0, 16), (1, 2)))
    token_out = normal_values(streams_of[6], (2 * D, D), (2 * D // 64) ** -0.5, 1.0, ((0, 16), (1, 2)))
    state_out = normal_values(streams_of[7], (2 * D, D), (2 * D // 64) ** -0.5, 1.0, ((0, 16), (1, 2)))
    gate_weight = normal_values(streams_of[8], (D, D), D ** -0.5, 0.1875, ((0, 16), (1, 2)))
    init_state = normal_values(streams_of[9], (NS, D), 1.0, 6.0, ((0, 16), (1, 2)))
    hidden_in = normal_values(streams_of[10], (D, FF), D ** -0.5, 0.1875, ((0, 16), (1, 2)))
    hidden_out = normal_values(streams_of[11], (FF, D), FF ** -0.5, 0.09375, ((0, 16), (1, 2)))
    token_gain = jnp.clip(1.0 + 0.1 * jax.random.normal(streams_of[12], (D,), jnp.float32), 0.5, 1.5).astype(jnp.bfloat16)
    state_gain = jnp.clip(1.0 + 0.1 * jax.random.normal(streams_of[13], (D,), jnp.float32), 0.5, 1.5).astype(jnp.bfloat16)
    hidden_gain = jnp.clip(1.0 + 0.1 * jax.random.normal(streams_of[14], (D,), jnp.float32), 0.5, 1.5).astype(jnp.bfloat16)
    gate_bias = normal_values(streams_of[15], (D,), 1.0, 4.0, ((0, 2),))
    return {"tokens": tokens, "incoming": incoming, "document_lengths": document_lengths, "output_grad": output_grad, "token_proj": token_proj, "state_proj": state_proj, "token_out": token_out, "state_out": state_out, "gate_weight": gate_weight, "init_state": init_state, "hidden_in": hidden_in, "hidden_out": hidden_out, "token_gain": token_gain, "state_gain": state_gain, "hidden_gain": hidden_gain, "gate_bias": gate_bias}


@jax.custom_vjp
def low(v):
    return lax.optimization_barrier(v.astype(jnp.bfloat16)).astype(jnp.float32)

@jax.custom_vjp
def low_back(v):
    return v

def low_keep(v):
    return (low(v), None)

def low_pass(kept, grad):
    return (grad,)

def back_keep(v):
    return (v, None)

def back_low(kept, grad):
    return (low(grad),)
low.defvjp(low_keep, low_pass)
low_back.defvjp(back_keep, back_low)
norm_eps = 1e-06
masked_score = -1e+30

def round_both(values):
    return low(low_back(values))

def layer_norm(values, gain):
    centered = values - lax.optimization_barrier(jnp.mean(values, axis=-1, keepdims=True))
    inverse = lax.rsqrt(lax.optimization_barrier(jnp.mean(centered * centered, axis=-1, keepdims=True)) + norm_eps)
    return centered * inverse * gain

def product(left, right):
    return jnp.dot(left, right, precision=lax.Precision.HIGHEST)

def split_heads(values):
    return values.reshape(values.shape[0], values.shape[1] // HD, HD)

def attention(query, keys, values, allowed):
    raw = low_back(jnp.einsum('rhd,khd->hrk', split_heads(query), split_heads(keys), precision=lax.Precision.HIGHEST))
    scores = raw * (1.0 / math.sqrt(HD))
    if allowed is not None:
        scores = jnp.where(allowed[None], scores, masked_score)
    top = lax.optimization_barrier(jnp.max(scores, axis=-1, keepdims=True))
    weights = jnp.exp(scores - top)
    probs = weights / lax.optimization_barrier(jnp.sum(weights, axis=-1, keepdims=True))
    mixed = jnp.einsum('hrk,khd->rhd', low(probs), split_heads(values), precision=lax.Precision.HIGHEST)
    return round_both(mixed.reshape(query.shape[0], query.shape[1]))

def window_allowed(start):
    query_pos = start + jnp.arange(WINDOW)
    key_pos = start - WINDOW + jnp.arange(2 * WINDOW)
    later = key_pos[None, :] <= query_pos[:, None]
    near = key_pos[None, :] > query_pos[:, None] - WINDOW
    return later & near & (key_pos[None, :] >= 0)

def segment(params, piece, start_state, valid_len):
    token_proj, state_proj, token_out, state_out, gate_weight, init_state, hidden_in, hidden_out, token_gain, state_gain, hidden_gain, gate_bias = params
    width = piece.shape[1]
    normed = low(layer_norm(piece, token_gain))
    projected = round_both(product(normed, token_proj))
    self_query = projected[:, :width]
    cross_query = projected[:, width:2 * width]
    token_keys = projected[:, 2 * width:3 * width]
    token_values = projected[:, 3 * width:]
    padding = jnp.zeros((WINDOW, width), projected.dtype)
    padded_keys = jnp.concatenate([padding, token_keys], axis=0)
    padded_values = jnp.concatenate([padding, token_values], axis=0)
    state = start_state
    parts = []
    for block_idx in range(BLOCKS):
        start = block_idx * WINDOW
        state_normed = low(layer_norm(state, state_gain))
        state_side = round_both(product(state_normed, state_proj))
        state_keys = state_side[:, 2 * width:3 * width]
        state_values = state_side[:, 3 * width:]
        self_part = attention(self_query[start:start + WINDOW], padded_keys[start:start + 2 * WINDOW], padded_values[start:start + 2 * WINDOW], window_allowed(start))
        cross_part = attention(cross_query[start:start + WINDOW], state_keys, state_values, None)
        parts.append(jnp.concatenate([self_part, cross_part], axis=1))
        live_keys = start + jnp.arange(WINDOW) < valid_len
        key_allowed = jnp.broadcast_to(live_keys[None, :], (state.shape[0], WINDOW))
        inner_self = attention(state_side[:, :width], state_keys, state_values, None)
        inner_cross = attention(state_side[:, width:2 * width], token_keys[start:start + WINDOW], token_values[start:start + WINDOW], key_allowed)
        mixed_state = round_both(product(jnp.concatenate([inner_self, inner_cross], axis=1), state_out))
        gate = jax.nn.sigmoid(low_back(product(mixed_state, gate_weight)) + gate_bias)
        updated = gate * state + (1.0 - gate) * jnp.tanh(mixed_state)
        live = jnp.where(start < valid_len, 1.0, 0.0).astype(state.dtype)
        state = state + live * (updated - state)
    attended = jnp.concatenate(parts, axis=0)
    middle = piece + low_back(product(attended, token_out))
    hidden_pre = low_back(product(low(layer_norm(middle, hidden_gain)), hidden_in))
    activated = low(jax.nn.gelu(hidden_pre, approximate=True))
    result = middle + low_back(product(activated, hidden_out))
    return (result, state)

def segment_table(document_lengths):
    counts = (document_lengths + SEG_LEN - 1) // SEG_LEN
    ends = jnp.cumsum(counts).astype(jnp.int32)
    starts = ends - counts
    index = jnp.arange(SEGS, dtype=jnp.int32)
    inside = (index[:, None] >= starts[None, :]) & (index[:, None] < ends[None, :])
    offset = (index[:, None] - starts[None, :]) * SEG_LEN
    remaining = jnp.minimum(SEG_LEN, document_lengths[None, :] - offset)
    valid_len = lax.optimization_barrier(jnp.sum(jnp.where(inside, remaining, 0), axis=1)).astype(jnp.int32)
    first = jnp.any(index[:, None] == starts[None, :], axis=1)
    return (valid_len, first)

def reference(tokens, incoming, document_lengths, output_grad, token_proj, state_proj, token_out, state_out, gate_weight, init_state, hidden_in, hidden_out, token_gain, state_gain, hidden_gain, gate_bias):
    valid_len, first = segment_table(document_lengths)
    params = tuple((item.astype(jnp.float32) for item in (token_proj, state_proj, token_out, state_out, gate_weight, init_state, hidden_in, hidden_out, token_gain, state_gain, hidden_gain, gate_bias)))
    pieces = tokens.astype(jnp.float32).reshape(SEGS, SEG_LEN, D)
    carried = incoming.astype(jnp.float32)
    checked = jax.checkpoint(segment)

    def forward(params, pieces):

        def one_segment(items):
            piece, prior, length, opening = items
            start_state = jnp.where(opening, params[5], prior)
            return checked(params, piece, start_state, length)
        return lax.map(one_segment, (pieces, carried, valid_len, first))
    (results, states), pullback = jax.vjp(forward, params, pieces)
    grads, grad_pieces = pullback((output_grad.astype(jnp.float32).reshape(SEGS, SEG_LEN, D), jnp.zeros_like(states)))
    return (results.reshape(TOKENS, D).astype(jnp.bfloat16), states.astype(jnp.bfloat16), grad_pieces.reshape(TOKENS, D).astype(jnp.bfloat16), grads[0], grads[1], grads[2], grads[3], grads[4], grads[5], grads[6], grads[7], grads[8], grads[9], grads[10], grads[11])
```

```python
from functools import partial
import math

import jax
import jax.numpy as jnp
from jax import lax
from jax.experimental import pallas as pl
from jax.experimental.pallas import tpu as pltpu
from jax.sharding import PartitionSpec as P

HD = 128
WINDOW = 512


norm_eps = 1e-06
masked_score = -1e30


def layer_norm(values, gain):
    centered = values - jnp.mean(values, axis=-1, keepdims=True)
    inverse = lax.rsqrt(jnp.mean(centered * centered, axis=-1, keepdims=True) + norm_eps)
    return centered * inverse * gain


def norm_back(values, gain, grad_out):
    _, pullback = jax.vjp(layer_norm, values, gain)
    return pullback(grad_out)


def narrow(values):
    return values.astype(jnp.bfloat16)


def matmul(left, right):
    return jnp.dot(left, right, preferred_element_type=jnp.float32)


def matmul_left_t(left, right):
    return lax.dot_general(
        left, right, (((0,), (0,)), ((), ())), preferred_element_type=jnp.float32
    )


def matmul_right_t(left, right):
    return lax.dot_general(
        left, right, (((1,), (1,)), ((), ())), preferred_element_type=jnp.float32
    )


EXP_SCALE = math.log2(math.e) / math.sqrt(HD)
RAW_SCALE = 1.0 / math.sqrt(HD)
NT = (((1,), (1,)), ((), ()))
TN = (((0,), (0,)), ((), ()))
NN = (((1,), (0,)), ((), ()))
MIB = 1 << 20


def dot(a, b, dims):
    return lax.dot_general(a, b, dims, preferred_element_type=jnp.float32)


def attend_tile(q, k, v, mask):
    scores = dot(k, q, NT)
    if mask is not None:
        scores = jnp.where(mask, scores, masked_score)
    top = jnp.max(scores, axis=0, keepdims=True)
    weights = jnp.exp2((scores - top) * EXP_SCALE)
    total = jnp.sum(weights, axis=0, keepdims=True)
    mixed = dot(v, weights.astype(jnp.bfloat16), TN) / total
    return mixed.T.astype(jnp.bfloat16), top * EXP_SCALE + jnp.log2(total)


def attend_back_tile(q, k, v, mask, log_total, grad_out, delta):
    probs = jnp.exp2(dot(k, q, NT) * EXP_SCALE - log_total)
    if mask is not None:
        probs = jnp.where(mask, probs, 0.0)
    grad_probs = dot(v, grad_out, NT)
    grad_raw = (probs * (grad_probs - delta)).astype(jnp.bfloat16)
    grad_v = dot(probs.astype(jnp.bfloat16), grad_out, NN)
    grad_k = dot(grad_raw, q, NN)
    grad_q = dot(k, grad_raw, TN)
    return grad_q, grad_k, grad_v


def row_delta(out, grad_out):
    both = out.astype(jnp.float32) * grad_out.astype(jnp.float32)
    return jnp.sum(both.T, axis=0, keepdims=True)


def band_mask(rows, cols, key_start, query_start, window):
    key = lax.broadcasted_iota(jnp.int32, (rows, cols), 0) + key_start
    query = lax.broadcasted_iota(jnp.int32, (rows, cols), 1) + query_start
    return (key <= query) & (key > query - window)


TILE = 256


def self_kernel(window, q_ref, k_ref, v_ref, out_ref, log_ref):
    rows = q_ref.shape[0]
    for start in range(0, rows, TILE):
        low = max(0, start - window)
        size = start + TILE - low
        mask = band_mask(size, TILE, low, start, window)
        out, log = attend_tile(
            q_ref[start : start + TILE, :], k_ref[low : low + size, :], v_ref[low : low + size, :], mask
        )
        out_ref[start : start + TILE, :] = out
        log_ref[0, :, start : start + TILE] = log


def column(rows, offset):
    return pl.BlockSpec((rows, HD), lambda h: (0, h + offset))


def stat(rows):
    return pl.BlockSpec((1, 1, rows), lambda h: (h, 0, 0))


def self_attention(projected, window):
    rows, width = projected.shape
    heads = width // 4 // HD
    return pl.pallas_call(
        partial(self_kernel, window),
        grid=(heads,),
        in_specs=[column(rows, 0), column(rows, 2 * heads), column(rows, 3 * heads)],
        out_specs=[column(rows, 0), stat(rows)],
        out_shape=[
            jax.ShapeDtypeStruct((rows, width // 4), jnp.bfloat16),
            jax.ShapeDtypeStruct((heads, 1, rows), jnp.float32),
        ],
        compiler_params=pltpu.CompilerParams(vmem_limit_bytes=40 * MIB),
        cost_estimate=pl.CostEstimate(
            flops=heads * 4 * 2304 * 256 * HD, bytes_accessed=8 * MIB, transcendentals=heads * 2304 * 256
        ),
        name="self_attention",
    )(projected, projected, projected)


def state_kernel(live_ref, cq_ref, sq_ref, scq_ref, sk_ref, sv_ref, tk_ref, tv_ref,
                 cross_ref, inner_self_ref, inner_cross_ref, cross_log, self_log, inner_log):
    rows = cq_ref.shape[0]
    for start in range(0, rows, TILE):
        at = slice(start, start + TILE)
        cross_ref[at, :], cross_log[0, :, at] = attend_tile(cq_ref[at, :], sk_ref[...], sv_ref[...], None)
        inner_self_ref[at, :], self_log[0, :, at] = attend_tile(sq_ref[at, :], sk_ref[...], sv_ref[...], None)
        key = lax.broadcasted_iota(jnp.int32, (rows, TILE), 0)
        inner_cross_ref[at, :], inner_log[0, :, at] = attend_tile(
            scq_ref[at, :], tk_ref[...], tv_ref[...], key < live_ref[0]
        )


def state_attention(projected, state_side, live_keys, block):
    rows, width = state_side.shape
    heads = width // 4 // HD
    def piece(offset):
        return pl.BlockSpec((rows, HD), lambda h: (block, h + offset))
    out = jax.ShapeDtypeStruct((rows, width // 4), jnp.bfloat16)
    log = jax.ShapeDtypeStruct((heads, 1, rows), jnp.float32)
    return pl.pallas_call(
        state_kernel,
        grid=(heads,),
        in_specs=[pl.BlockSpec(memory_space=pltpu.SMEM),
                  piece(heads), column(rows, 0), column(rows, heads), column(rows, 2 * heads), column(rows, 3 * heads),
                  piece(2 * heads), piece(3 * heads)],
        out_specs=[column(rows, 0)] * 3 + [stat(rows)] * 3,
        out_shape=[out] * 3 + [log] * 3,
        compiler_params=pltpu.CompilerParams(vmem_limit_bytes=40 * MIB),
        cost_estimate=pl.CostEstimate(
            flops=heads * 3 * 4 * rows * rows * HD, bytes_accessed=8 * MIB, transcendentals=heads * 3 * rows * rows
        ),
        name="state_attention",
    )(live_keys, projected, state_side, state_side, state_side, state_side, projected, projected)


def self_back_kernel(window, q_ref, k_ref, v_ref, out_ref, log_ref, grad_ref, ek_ref, ev_ref, gq_ref, gk_ref, gv_ref, sk_ref, sv_ref):
    rows = q_ref.shape[0]
    extra = ek_ref.shape[0]
    sk_ref[...] = jnp.zeros_like(sk_ref)
    sv_ref[:extra, :] = ev_ref[...]
    sv_ref[extra:, :] = jnp.zeros((rows - extra, HD), jnp.float32)
    for start in range(0, rows, TILE):
        at = slice(start, start + TILE)
        low = max(0, start - window)
        size = start + TILE - low
        keys = slice(low, low + size)
        mask = band_mask(size, TILE, low, start, window)
        grad_out = grad_ref[at, :]
        grad_q, grad_k, grad_v = attend_back_tile(
            q_ref[at, :], k_ref[keys, :], v_ref[keys, :], mask, log_ref[0, :, at], grad_out,
            row_delta(out_ref[at, :], grad_out))
        gq_ref[at, :] = (grad_q * RAW_SCALE).T.astype(jnp.bfloat16)
        sk_ref[keys, :] += grad_k
        sv_ref[keys, :] += grad_v
    gk_ref[:extra, :] = (sk_ref[:extra, :] * RAW_SCALE + ek_ref[...]).astype(jnp.bfloat16)
    gk_ref[extra:, :] = (sk_ref[extra:, :] * RAW_SCALE).astype(jnp.bfloat16)
    gv_ref[...] = sv_ref[...].astype(jnp.bfloat16)


def self_attention_back(projected, out, log, grad_attended, extra_k, extra_v, window):
    rows, width = projected.shape
    heads = width // 4 // HD
    extra = extra_k.shape[0]
    grad = jax.ShapeDtypeStruct((rows, width // 4), jnp.bfloat16)
    return pl.pallas_call(
        partial(self_back_kernel, window),
        grid=(heads,),
        in_specs=[column(rows, 0), column(rows, 2 * heads), column(rows, 3 * heads), column(rows, 0), stat(rows),
                  column(rows, 0), column(extra, 0), column(extra, 0)],
        out_specs=[column(rows, 0)] * 3,
        out_shape=[grad] * 3,
        scratch_shapes=[pltpu.VMEM((rows, HD), jnp.float32)] * 2,
        compiler_params=pltpu.CompilerParams(vmem_limit_bytes=40 * MIB),
        cost_estimate=pl.CostEstimate(
            flops=heads * 10 * 2304 * 256 * HD, bytes_accessed=16 * MIB, transcendentals=heads * 2304 * 256
        ),
        name="self_attention_back",
    )(projected, projected, projected, out, log, grad_attended, extra_k, extra_v)


def cross_back_kernel(cq_ref, sk_ref, sv_ref, out_ref, log_ref, grad_ref, gq_ref, gk_ref, gv_ref):
    rows = cq_ref.shape[0]
    total_k = total_v = 0.0
    for start in range(0, rows, TILE):
        at = slice(start, start + TILE)
        grad_out = grad_ref[at, :]
        grad_q, grad_k, grad_v = attend_back_tile(
            cq_ref[at, :], sk_ref[...], sv_ref[...], None, log_ref[0, :, at], grad_out,
            row_delta(out_ref[at, :], grad_out))
        gq_ref[at, :] = (grad_q * RAW_SCALE).T.astype(jnp.bfloat16)
        total_k = total_k + grad_k
        total_v = total_v + grad_v
    gk_ref[...] = (total_k * RAW_SCALE).astype(jnp.bfloat16)
    gv_ref[...] = total_v.astype(jnp.bfloat16)


def cross_attention_back(projected, state_side, out, log, grad_attended, block):
    rows, width = state_side.shape
    heads = width // 4 // HD
    grad = jax.ShapeDtypeStruct((rows, width // 4), jnp.bfloat16)
    def piece(offset):
        return pl.BlockSpec((rows, HD), lambda h: (block, h + offset))
    return pl.pallas_call(
        cross_back_kernel,
        grid=(heads,),
        in_specs=[piece(heads), column(rows, 2 * heads), column(rows, 3 * heads), column(rows, 0), stat(rows), piece(heads)],
        out_specs=[column(rows, 0)] * 3,
        out_shape=[grad] * 3,
        compiler_params=pltpu.CompilerParams(vmem_limit_bytes=40 * MIB),
        cost_estimate=pl.CostEstimate(
            flops=heads * 10 * rows * rows * HD, bytes_accessed=8 * MIB, transcendentals=heads * rows * rows
        ),
        name="cross_attention_back",
    )(projected, state_side, state_side, out, log, grad_attended)


def state_back_kernel(live_ref, cq_ref, sq_ref, scq_ref, sk_ref, sv_ref, tk_ref, tv_ref,
                      co_ref, so_ref, io_ref, cl_ref, sl_ref, il_ref, cg_ref, sg_ref, ig_ref,
                      gcq_ref, gsq_ref, gscq_ref, gsk_ref, gsv_ref, gtk_ref, gtv_ref):
    rows = cq_ref.shape[0]
    sums = [0.0] * 4
    for start in range(0, rows, TILE):
        at = slice(start, start + TILE)
        key = lax.broadcasted_iota(jnp.int32, (rows, TILE), 0)
        for q_ref, k_ref, v_ref, o_ref, l_ref, g_ref, gq_ref, mask, slot in (
            (cq_ref, sk_ref, sv_ref, co_ref, cl_ref, cg_ref, gcq_ref, None, 0),
            (sq_ref, sk_ref, sv_ref, so_ref, sl_ref, sg_ref, gsq_ref, None, 0),
            (scq_ref, tk_ref, tv_ref, io_ref, il_ref, ig_ref, gscq_ref, key < live_ref[0], 2),
        ):
            grad_out = g_ref[at, :]
            grad_q, grad_k, grad_v = attend_back_tile(
                q_ref[at, :], k_ref[...], v_ref[...], mask, l_ref[0, :, at], grad_out,
                row_delta(o_ref[at, :], grad_out))
            gq_ref[at, :] = (grad_q * RAW_SCALE).T.astype(jnp.bfloat16)
            sums[slot] = sums[slot] + grad_k
            sums[slot + 1] = sums[slot + 1] + grad_v
    gsk_ref[...] = (sums[0] * RAW_SCALE).astype(jnp.bfloat16)
    gsv_ref[...] = sums[1].astype(jnp.bfloat16)
    gtk_ref[...] = sums[2] * RAW_SCALE
    gtv_ref[...] = sums[3]


def state_attention_back(projected, state_side, live_keys, outs, logs, grad_attended, grad_inner, block):
    rows, width = state_side.shape
    heads = width // 4 // HD
    def piece(offset):
        return pl.BlockSpec((rows, HD), lambda h: (block, h + offset))
    grad = jax.ShapeDtypeStruct((rows, width // 4), jnp.bfloat16)
    wide = jax.ShapeDtypeStruct((rows, width // 4), jnp.float32)
    return pl.pallas_call(
        state_back_kernel,
        grid=(heads,),
        in_specs=[pl.BlockSpec(memory_space=pltpu.SMEM),
                  piece(heads), column(rows, 0), column(rows, heads), column(rows, 2 * heads), column(rows, 3 * heads),
                  piece(2 * heads), piece(3 * heads)] + [column(rows, 0)] * 3 + [stat(rows)] * 3
                 + [piece(heads), column(rows, 0), column(rows, heads)],
        out_specs=[column(rows, 0)] * 7,
        out_shape=[grad] * 5 + [wide] * 2,
        compiler_params=pltpu.CompilerParams(vmem_limit_bytes=40 * MIB),
        cost_estimate=pl.CostEstimate(
            flops=heads * 30 * rows * rows * HD, bytes_accessed=16 * MIB, transcendentals=3 * heads * rows * rows
        ),
        name="state_attention_back",
    )(live_keys, projected, state_side, state_side, state_side, state_side, projected, projected,
      *outs, *logs, grad_attended, grad_inner, grad_inner)


def shards(
    tokens,
    incoming,
    document_lengths,
    output_grad,
    token_proj,
    state_proj,
    token_out,
    state_out,
    gate_weight,
    init_state,
    hidden_in,
    hidden_out,
    token_gain,
    state_gain,
    hidden_gain,
    gate_bias,
):
    columns = (
        lax.all_gather(token_proj, "fsdp", axis=1, tiled=True),
        lax.all_gather(state_proj, "fsdp", axis=1, tiled=True),
        lax.all_gather(token_out, "fsdp", axis=1, tiled=True),
        lax.all_gather(state_out, "fsdp", axis=1, tiled=True),
        lax.all_gather(gate_weight, "fsdp", axis=1, tiled=True),
        lax.all_gather(init_state, "fsdp", axis=1, tiled=True),
        lax.all_gather(hidden_in, "fsdp", axis=1, tiled=True),
        lax.all_gather(hidden_out, "fsdp", axis=1, tiled=True),
        lax.all_gather(token_gain, "fsdp", axis=0, tiled=True),
        lax.all_gather(state_gain, "fsdp", axis=0, tiled=True),
        lax.all_gather(hidden_gain, "fsdp", axis=0, tiled=True),
        lax.all_gather(gate_bias, "fsdp", axis=0, tiled=True),
    )
    weights = (
        lax.all_gather(columns[0], "dp", axis=0, tiled=True),
        lax.all_gather(columns[1], "dp", axis=0, tiled=True),
        lax.all_gather(columns[2], "dp", axis=0, tiled=True),
        lax.all_gather(columns[3], "dp", axis=0, tiled=True),
        lax.all_gather(columns[4], "dp", axis=0, tiled=True),
        lax.all_gather(columns[5], "dp", axis=0, tiled=True),
        lax.all_gather(columns[6], "dp", axis=0, tiled=True),
        lax.all_gather(columns[7], "dp", axis=0, tiled=True),
    )
    (
        full_token_proj,
        full_state_proj,
        full_token_out,
        full_state_out,
        full_gate_weight,
        full_init,
        full_hidden_in,
        full_hidden_out,
    ) = weights
    token_gain_f = columns[8].astype(jnp.float32)
    state_gain_f = columns[9].astype(jnp.float32)
    hidden_gain_f = columns[10].astype(jnp.float32)
    gate_bias_f = columns[11].astype(jnp.float32)
    seg_len, width = tokens.shape
    window = WINDOW
    blocks = seg_len // window
    segment_id = lax.axis_index(("dp", "fsdp"))
    counts = (document_lengths + seg_len - 1) // seg_len
    ends = jnp.cumsum(counts)
    starts = ends - counts
    inside = (segment_id >= starts) & (segment_id < ends)
    valid_len = jnp.sum(
        jnp.where(
            inside, jnp.minimum(seg_len, document_lengths - (segment_id - starts) * seg_len), 0
        )
    )
    first = jnp.any(segment_id == starts)
    piece = tokens.astype(jnp.float32)
    normed_low = narrow(layer_norm(piece, token_gain_f))
    projected = narrow(matmul(normed_low, full_token_proj))
    self_out, self_log = self_attention(projected, window)
    state = jnp.where(first, full_init.astype(jnp.float32), incoming[0].astype(jnp.float32))
    state_inputs, normed_states, sides, inner_cats, mixed_states, gates, lives, key_counts = (
        [],
        [],
        [],
        [],
        [],
        [],
        [],
        [],
    )
    state_outs, state_logs = ([], [])
    for block_idx in range(blocks):
        start = block_idx * window
        state_normed = narrow(layer_norm(state, state_gain_f))
        state_side = narrow(matmul(state_normed, full_state_proj))
        live_keys = jnp.clip(valid_len - start, 0, window).astype(jnp.int32).reshape(1)
        outs = state_attention(projected, state_side, live_keys, block_idx)
        inner_cat = jnp.concatenate([outs[1], outs[2]], axis=1)
        mixed_state = narrow(matmul(inner_cat, full_state_out))
        gate = jax.nn.sigmoid(matmul(mixed_state, full_gate_weight) + gate_bias_f)
        updated = gate * state + (1.0 - gate) * jnp.tanh(mixed_state.astype(jnp.float32))
        live = jnp.where(start < valid_len, 1.0, 0.0).astype(jnp.float32)
        state_inputs.append(state)
        normed_states.append(state_normed)
        sides.append(state_side)
        inner_cats.append(inner_cat)
        mixed_states.append(mixed_state)
        gates.append(gate)
        lives.append(live)
        key_counts.append(live_keys)
        state_outs.append(outs[:3])
        state_logs.append(outs[3:])
        state = state + live * (updated - state)
    cross_out = jnp.concatenate([outs[0] for outs in state_outs], axis=0)
    attended = jnp.concatenate([self_out, cross_out], axis=1)
    middle = piece + matmul(attended, full_token_out)
    hidden_normed = narrow(layer_norm(middle, hidden_gain_f))
    hidden_pre = matmul(hidden_normed, full_hidden_in)
    activated = narrow(jax.nn.gelu(hidden_pre, approximate=True))
    result = middle + matmul(activated, full_hidden_out)
    columns_back = (
        lax.all_gather(token_proj, "fsdp", axis=1, tiled=True),
        lax.all_gather(state_proj, "fsdp", axis=1, tiled=True),
        lax.all_gather(token_out, "fsdp", axis=1, tiled=True),
        lax.all_gather(state_out, "fsdp", axis=1, tiled=True),
        lax.all_gather(gate_weight, "fsdp", axis=1, tiled=True),
        lax.all_gather(init_state, "fsdp", axis=1, tiled=True),
        lax.all_gather(hidden_in, "fsdp", axis=1, tiled=True),
        lax.all_gather(hidden_out, "fsdp", axis=1, tiled=True),
    )
    weights_back = (
        lax.all_gather(columns_back[0], "dp", axis=0, tiled=True),
        lax.all_gather(columns_back[1], "dp", axis=0, tiled=True),
        lax.all_gather(columns_back[2], "dp", axis=0, tiled=True),
        lax.all_gather(columns_back[3], "dp", axis=0, tiled=True),
        lax.all_gather(columns_back[4], "dp", axis=0, tiled=True),
        lax.all_gather(columns_back[5], "dp", axis=0, tiled=True),
        lax.all_gather(columns_back[6], "dp", axis=0, tiled=True),
        lax.all_gather(columns_back[7], "dp", axis=0, tiled=True),
    )
    (
        back_token_proj,
        back_state_proj,
        back_token_out,
        back_state_out,
        back_gate_weight,
        back_init,
        back_hidden_in,
        back_hidden_out,
    ) = weights_back
    grad_result = output_grad.astype(jnp.float32)
    grad_hidden_out = matmul_left_t(activated, output_grad)
    grad_activated = matmul_right_t(output_grad, back_hidden_out)
    _, gelu_pull = jax.vjp(partial(jax.nn.gelu, approximate=True), hidden_pre)
    grad_pre = narrow(gelu_pull(grad_activated)[0])
    grad_hidden_in = matmul_left_t(hidden_normed, grad_pre)
    grad_middle_part, grad_hidden_gain = norm_back(
        middle, hidden_gain_f, matmul_right_t(grad_pre, back_hidden_in)
    )
    grad_middle = grad_result + grad_middle_part
    grad_branch = narrow(grad_middle)
    grad_token_out = matmul_left_t(attended, grad_branch)
    grad_attended = narrow(matmul_right_t(grad_branch, back_token_out))
    last = blocks - 1
    last_start = last * window
    cross_grad, last_keys_grad, last_values_grad = cross_attention_back(
        projected,
        sides[last],
        state_outs[last][0],
        state_logs[last][0],
        grad_attended,
        last,
    )
    cross_grads = [cross_grad]
    grad_side = jnp.concatenate([last_keys_grad, last_values_grad], axis=1)
    grad_state_proj = jnp.concatenate(
        [
            jnp.zeros((width, 2 * width), jnp.float32),
            matmul_left_t(normed_states[last], grad_side),
        ],
        axis=1,
    )
    grad_state, grad_state_gain = norm_back(
        state_inputs[last], state_gain_f, matmul_right_t(grad_side, back_state_proj[:, 2 * width :])
    )
    grad_state_out = jnp.zeros((2 * width, width), jnp.float32)
    grad_gate_weight = jnp.zeros((width, width), jnp.float32)
    grad_gate_bias = jnp.zeros((width,), jnp.float32)
    extra_keys, extra_values = ([], [])
    for block_idx in reversed(range(last)):
        state_side = sides[block_idx]
        gate = gates[block_idx]
        live = lives[block_idx]
        state_in = state_inputs[block_idx]
        tanh_mixed = jnp.tanh(mixed_states[block_idx].astype(jnp.float32))
        grad_updated = live * grad_state
        grad_direct = (1.0 - live) * grad_state + grad_updated * gate
        grad_gate_pre = gate * (1.0 - gate) * grad_updated * (state_in - tanh_mixed)
        grad_gate_bias = grad_gate_bias + jnp.sum(grad_gate_pre, axis=0)
        grad_gate_low = narrow(grad_gate_pre)
        grad_gate_weight = grad_gate_weight + matmul_left_t(mixed_states[block_idx], grad_gate_low)
        grad_mixed = narrow(
            matmul_right_t(grad_gate_low, back_gate_weight)
            + grad_updated * (1.0 - gate) * (1.0 - tanh_mixed * tanh_mixed)
        )
        grad_state_out = grad_state_out + matmul_left_t(inner_cats[block_idx], grad_mixed)
        grad_inner = narrow(matmul_right_t(grad_mixed, back_state_out))
        parts = state_attention_back(
            projected,
            state_side,
            key_counts[block_idx],
            state_outs[block_idx],
            state_logs[block_idx],
            grad_attended,
            grad_inner,
            block_idx,
        )
        cross_grads.insert(0, parts[0])
        grad_side = jnp.concatenate(parts[1:5], axis=1)
        extra_keys.insert(0, parts[5])
        extra_values.insert(0, parts[6])
        grad_state_proj = grad_state_proj + matmul_left_t(normed_states[block_idx], grad_side)
        grad_state_norm, grad_gain_part = norm_back(
            state_in, state_gain_f, matmul_right_t(grad_side, back_state_proj)
        )
        grad_state_gain = grad_state_gain + grad_gain_part
        grad_state = grad_direct + grad_state_norm
    self_grad, keys_grad, values_grad = self_attention_back(
        projected,
        self_out,
        self_log,
        grad_attended,
        jnp.concatenate(extra_keys, axis=0),
        jnp.concatenate(extra_values, axis=0),
        window,
    )
    grad_init = jnp.where(first, grad_state, 0.0)
    grad_projected = jnp.concatenate(
        [self_grad, jnp.concatenate(cross_grads, axis=0), keys_grad, values_grad], axis=1
    )
    grad_token_proj = matmul_left_t(normed_low, grad_projected)
    grad_piece, grad_token_gain = norm_back(
        piece, token_gain_f, matmul_right_t(grad_projected, back_token_proj)
    )
    tokens_grad = narrow(grad_middle + grad_piece)
    row_parts = (
        lax.psum_scatter(
            grad_token_proj.astype(jnp.bfloat16), "dp", scatter_dimension=0, tiled=True
        ).astype(jnp.float32),
        lax.psum_scatter(
            grad_state_proj.astype(jnp.bfloat16), "dp", scatter_dimension=0, tiled=True
        ).astype(jnp.float32),
        lax.psum_scatter(
            grad_token_out.astype(jnp.bfloat16), "dp", scatter_dimension=0, tiled=True
        ).astype(jnp.float32),
        lax.psum_scatter(
            grad_state_out.astype(jnp.bfloat16), "dp", scatter_dimension=0, tiled=True
        ).astype(jnp.float32),
        lax.psum_scatter(
            grad_gate_weight.astype(jnp.bfloat16), "dp", scatter_dimension=0, tiled=True
        ).astype(jnp.float32),
        lax.psum_scatter(
            grad_init.astype(jnp.bfloat16), "dp", scatter_dimension=0, tiled=True
        ).astype(jnp.float32),
        lax.psum_scatter(
            grad_hidden_in.astype(jnp.bfloat16), "dp", scatter_dimension=0, tiled=True
        ).astype(jnp.float32),
        lax.psum_scatter(
            grad_hidden_out.astype(jnp.bfloat16), "dp", scatter_dimension=0, tiled=True
        ).astype(jnp.float32),
    )
    summed = (
        lax.psum_scatter(
            row_parts[0].astype(jnp.bfloat16), "fsdp", scatter_dimension=1, tiled=True
        ).astype(jnp.float32),
        lax.psum_scatter(
            row_parts[1].astype(jnp.bfloat16), "fsdp", scatter_dimension=1, tiled=True
        ).astype(jnp.float32),
        lax.psum_scatter(
            row_parts[2].astype(jnp.bfloat16), "fsdp", scatter_dimension=1, tiled=True
        ).astype(jnp.float32),
        lax.psum_scatter(
            row_parts[3].astype(jnp.bfloat16), "fsdp", scatter_dimension=1, tiled=True
        ).astype(jnp.float32),
        lax.psum_scatter(
            row_parts[4].astype(jnp.bfloat16), "fsdp", scatter_dimension=1, tiled=True
        ).astype(jnp.float32),
        lax.psum_scatter(
            row_parts[5].astype(jnp.bfloat16), "fsdp", scatter_dimension=1, tiled=True
        ).astype(jnp.float32),
        lax.psum_scatter(
            row_parts[6].astype(jnp.bfloat16), "fsdp", scatter_dimension=1, tiled=True
        ).astype(jnp.float32),
        lax.psum_scatter(
            row_parts[7].astype(jnp.bfloat16), "fsdp", scatter_dimension=1, tiled=True
        ).astype(jnp.float32),
        lax.psum_scatter(
            grad_token_gain.astype(jnp.bfloat16), "fsdp", scatter_dimension=0, tiled=True
        ).astype(jnp.float32),
        lax.psum_scatter(
            grad_state_gain.astype(jnp.bfloat16), "fsdp", scatter_dimension=0, tiled=True
        ).astype(jnp.float32),
        lax.psum_scatter(
            grad_hidden_gain.astype(jnp.bfloat16), "fsdp", scatter_dimension=0, tiled=True
        ).astype(jnp.float32),
        lax.psum_scatter(
            grad_gate_bias.astype(jnp.bfloat16), "fsdp", scatter_dimension=0, tiled=True
        ).astype(jnp.float32),
    )
    matrix_grads = summed[:8]
    vector_parts = summed[8:]
    vector_grads = lax.psum(
        (vector_parts[0], vector_parts[1], vector_parts[2], vector_parts[3]), "dp"
    )
    return (
        narrow(result),
        narrow(state)[None],
        tokens_grad,
        matrix_grads[0],
        matrix_grads[1],
        matrix_grads[2],
        matrix_grads[3],
        matrix_grads[4],
        matrix_grads[5],
        matrix_grads[6],
        matrix_grads[7],
        vector_grads[0],
        vector_grads[1],
        vector_grads[2],
        vector_grads[3],
    )


def solution(mesh):
    return jax.shard_map(
        shards,
        mesh=mesh,
        in_specs=(
            P(("dp", "fsdp"), None),
            P(("dp", "fsdp"), None, None),
            P(),
            P(("dp", "fsdp"), None),
            P("dp", "fsdp"),
            P("dp", "fsdp"),
            P("dp", "fsdp"),
            P("dp", "fsdp"),
            P("dp", "fsdp"),
            P("dp", "fsdp"),
            P("dp", "fsdp"),
            P("dp", "fsdp"),
            P("fsdp"),
            P("fsdp"),
            P("fsdp"),
            P("fsdp"),
        ),
        out_specs=(
            P(("dp", "fsdp"), None),
            P(("dp", "fsdp"), None, None),
            P(("dp", "fsdp"), None),
            P("dp", "fsdp"),
            P("dp", "fsdp"),
            P("dp", "fsdp"),
            P("dp", "fsdp"),
            P("dp", "fsdp"),
            P("dp", "fsdp"),
            P("dp", "fsdp"),
            P("dp", "fsdp"),
            P("fsdp"),
            P("fsdp"),
            P("fsdp"),
            P("fsdp"),
        ),
        check_vma=False,
    )
```

```python
from functools import partial
import math

import jax
import jax.numpy as jnp
from jax import lax
from jax.experimental import pallas as pl
from jax.experimental.pallas import tpu as pltpu
from jax.sharding import PartitionSpec as P

HD = 128
WINDOW = 512


norm_eps = 1e-06
masked_score = -1e30


def layer_norm(values, gain):
    centered = values - jnp.mean(values, axis=-1, keepdims=True)
    inverse = lax.rsqrt(jnp.mean(centered * centered, axis=-1, keepdims=True) + norm_eps)
    return centered * inverse * gain


def norm_back(values, gain, grad_out):
    _, pullback = jax.vjp(layer_norm, values, gain)
    return pullback(grad_out)


def narrow(values):
    return values.astype(jnp.bfloat16)


def matmul(left, right):
    return jnp.dot(left, right, preferred_element_type=jnp.float32)


def matmul_left_t(left, right):
    return lax.dot_general(
        left, right, (((0,), (0,)), ((), ())), preferred_element_type=jnp.float32
    )


def matmul_right_t(left, right):
    return lax.dot_general(
        left, right, (((1,), (1,)), ((), ())), preferred_element_type=jnp.float32
    )


EXP_SCALE = math.log2(math.e) / math.sqrt(HD)
RAW_SCALE = 1.0 / math.sqrt(HD)
NT = (((1,), (1,)), ((), ()))
TN = (((0,), (0,)), ((), ()))
NN = (((1,), (0,)), ((), ()))
MIB = 1 << 20


def dot(a, b, dims):
    return lax.dot_general(a, b, dims, preferred_element_type=jnp.float32)


def attend_tile(q, k, v, mask):
    scores = dot(k, q, NT)
    if mask is not None:
        scores = jnp.where(mask, scores, masked_score)
    top = jnp.max(scores, axis=0, keepdims=True)
    weights = jnp.exp2((scores - top) * EXP_SCALE)
    total = jnp.sum(weights, axis=0, keepdims=True)
    mixed = dot(v, weights.astype(jnp.bfloat16), TN) / total
    return mixed.T.astype(jnp.bfloat16), top * EXP_SCALE + jnp.log2(total)


def attend_back_tile(q, k, v, mask, log_total, grad_out, delta):
    probs = jnp.exp2(dot(k, q, NT) * EXP_SCALE - log_total)
    if mask is not None:
        probs = jnp.where(mask, probs, 0.0)
    grad_probs = dot(v, grad_out, NT)
    grad_raw = (probs * (grad_probs - delta)).astype(jnp.bfloat16)
    grad_v = dot(probs.astype(jnp.bfloat16), grad_out, NN)
    grad_k = dot(grad_raw, q, NN)
    grad_q = dot(k, grad_raw, TN)
    return grad_q, grad_k, grad_v


def row_delta(out, grad_out):
    both = out.astype(jnp.float32) * grad_out.astype(jnp.float32)
    return jnp.sum(both.T, axis=0, keepdims=True)


def band_mask(rows, cols, key_start, query_start, window):
    key = lax.broadcasted_iota(jnp.int32, (rows, cols), 0) + key_start
    query = lax.broadcasted_iota(jnp.int32, (rows, cols), 1) + query_start
    return (key <= query) & (key > query - window)


TILE = 256


def self_kernel(window, q_ref, k_ref, v_ref, out_ref, log_ref):
    rows = q_ref.shape[0]
    for start in range(0, rows, TILE):
        low = max(0, start - window)
        size = start + TILE - low
        mask = band_mask(size, TILE, low, start, window)
        out, log = attend_tile(
            q_ref[start : start + TILE, :], k_ref[low : low + size, :], v_ref[low : low + size, :], mask
        )
        out_ref[start : start + TILE, :] = out
        log_ref[0, :, start : start + TILE] = log


def column(rows, offset):
    return pl.BlockSpec((rows, HD), lambda h: (0, h + offset))


def stat(rows):
    return pl.BlockSpec((1, 1, rows), lambda h: (h, 0, 0))


def self_attention(projected, window):
    rows, width = projected.shape
    heads = width // 4 // HD
    return pl.pallas_call(
        partial(self_kernel, window),
        grid=(heads,),
        in_specs=[column(rows, 0), column(rows, 2 * heads), column(rows, 3 * heads)],
        out_specs=[column(rows, 0), stat(rows)],
        out_shape=[
            jax.ShapeDtypeStruct((rows, width // 4), jnp.bfloat16),
            jax.ShapeDtypeStruct((heads, 1, rows), jnp.float32),
        ],
        compiler_params=pltpu.CompilerParams(vmem_limit_bytes=40 * MIB),
        cost_estimate=pl.CostEstimate(
            flops=heads * 4 * 2304 * 256 * HD, bytes_accessed=8 * MIB, transcendentals=heads * 2304 * 256
        ),
        name="self_attention",
    )(projected, projected, projected)


def state_kernel(live_ref, cq_ref, sq_ref, scq_ref, sk_ref, sv_ref, tk_ref, tv_ref,
                 cross_ref, inner_self_ref, inner_cross_ref, cross_log, self_log, inner_log):
    rows = cq_ref.shape[0]
    for start in range(0, rows, TILE):
        at = slice(start, start + TILE)
        cross_ref[at, :], cross_log[0, :, at] = attend_tile(cq_ref[at, :], sk_ref[...], sv_ref[...], None)
        inner_self_ref[at, :], self_log[0, :, at] = attend_tile(sq_ref[at, :], sk_ref[...], sv_ref[...], None)
        key = lax.broadcasted_iota(jnp.int32, (rows, TILE), 0)
        inner_cross_ref[at, :], inner_log[0, :, at] = attend_tile(
            scq_ref[at, :], tk_ref[...], tv_ref[...], key < live_ref[0]
        )


def state_attention(projected, state_side, live_keys, block):
    rows, width = state_side.shape
    heads = width // 4 // HD
    def piece(offset):
        return pl.BlockSpec((rows, HD), lambda h: (block, h + offset))
    out = jax.ShapeDtypeStruct((rows, width // 4), jnp.bfloat16)
    log = jax.ShapeDtypeStruct((heads, 1, rows), jnp.float32)
    return pl.pallas_call(
        state_kernel,
        grid=(heads,),
        in_specs=[pl.BlockSpec(memory_space=pltpu.SMEM),
                  piece(heads), column(rows, 0), column(rows, heads), column(rows, 2 * heads), column(rows, 3 * heads),
                  piece(2 * heads), piece(3 * heads)],
        out_specs=[column(rows, 0)] * 3 + [stat(rows)] * 3,
        out_shape=[out] * 3 + [log] * 3,
        compiler_params=pltpu.CompilerParams(vmem_limit_bytes=40 * MIB),
        cost_estimate=pl.CostEstimate(
            flops=heads * 3 * 4 * rows * rows * HD, bytes_accessed=8 * MIB, transcendentals=heads * 3 * rows * rows
        ),
        name="state_attention",
    )(live_keys, projected, state_side, state_side, state_side, state_side, projected, projected)


def self_back_kernel(window, q_ref, k_ref, v_ref, out_ref, log_ref, grad_ref, ek_ref, ev_ref, gq_ref, gk_ref, gv_ref, sk_ref, sv_ref):
    rows = q_ref.shape[0]
    extra = ek_ref.shape[0]
    sk_ref[...] = jnp.zeros_like(sk_ref)
    sv_ref[:extra, :] = ev_ref[...]
    sv_ref[extra:, :] = jnp.zeros((rows - extra, HD), jnp.float32)
    for start in range(0, rows, TILE):
        at = slice(start, start + TILE)
        low = max(0, start - window)
        size = start + TILE - low
        keys = slice(low, low + size)
        mask = band_mask(size, TILE, low, start, window)
        grad_out = grad_ref[at, :]
        grad_q, grad_k, grad_v = attend_back_tile(
            q_ref[at, :], k_ref[keys, :], v_ref[keys, :], mask, log_ref[0, :, at], grad_out,
            row_delta(out_ref[at, :], grad_out))
        gq_ref[at, :] = (grad_q * RAW_SCALE).T.astype(jnp.bfloat16)
        sk_ref[keys, :] += grad_k
        sv_ref[keys, :] += grad_v
    gk_ref[:extra, :] = (sk_ref[:extra, :] * RAW_SCALE + ek_ref[...]).astype(jnp.bfloat16)
    gk_ref[extra:, :] = (sk_ref[extra:, :] * RAW_SCALE).astype(jnp.bfloat16)
    gv_ref[...] = sv_ref[...].astype(jnp.bfloat16)


def self_attention_back(projected, out, log, grad_attended, extra_k, extra_v, window):
    rows, width = projected.shape
    heads = width // 4 // HD
    extra = extra_k.shape[0]
    grad = jax.ShapeDtypeStruct((rows, width // 4), jnp.bfloat16)
    return pl.pallas_call(
        partial(self_back_kernel, window),
        grid=(heads,),
        in_specs=[column(rows, 0), column(rows, 2 * heads), column(rows, 3 * heads), column(rows, 0), stat(rows),
                  column(rows, 0), column(extra, 0), column(extra, 0)],
        out_specs=[column(rows, 0)] * 3,
        out_shape=[grad] * 3,
        scratch_shapes=[pltpu.VMEM((rows, HD), jnp.float32)] * 2,
        compiler_params=pltpu.CompilerParams(vmem_limit_bytes=40 * MIB),
        cost_estimate=pl.CostEstimate(
            flops=heads * 10 * 2304 * 256 * HD, bytes_accessed=16 * MIB, transcendentals=heads * 2304 * 256
        ),
        name="self_attention_back",
    )(projected, projected, projected, out, log, grad_attended, extra_k, extra_v)


def cross_back_kernel(cq_ref, sk_ref, sv_ref, out_ref, log_ref, grad_ref, gq_ref, gk_ref, gv_ref):
    rows = cq_ref.shape[0]
    total_k = total_v = 0.0
    for start in range(0, rows, TILE):
        at = slice(start, start + TILE)
        grad_out = grad_ref[at, :]
        grad_q, grad_k, grad_v = attend_back_tile(
            cq_ref[at, :], sk_ref[...], sv_ref[...], None, log_ref[0, :, at], grad_out,
            row_delta(out_ref[at, :], grad_out))
        gq_ref[at, :] = (grad_q * RAW_SCALE).T.astype(jnp.bfloat16)
        total_k = total_k + grad_k
        total_v = total_v + grad_v
    gk_ref[...] = (total_k * RAW_SCALE).astype(jnp.bfloat16)
    gv_ref[...] = total_v.astype(jnp.bfloat16)


def cross_attention_back(projected, state_side, out, log, grad_attended, block):
    rows, width = state_side.shape
    heads = width // 4 // HD
    grad = jax.ShapeDtypeStruct((rows, width // 4), jnp.bfloat16)
    def piece(offset):
        return pl.BlockSpec((rows, HD), lambda h: (block, h + offset))
    return pl.pallas_call(
        cross_back_kernel,
        grid=(heads,),
        in_specs=[piece(heads), column(rows, 2 * heads), column(rows, 3 * heads), column(rows, 0), stat(rows), piece(heads)],
        out_specs=[column(rows, 0)] * 3,
        out_shape=[grad] * 3,
        compiler_params=pltpu.CompilerParams(vmem_limit_bytes=40 * MIB),
        cost_estimate=pl.CostEstimate(
            flops=heads * 10 * rows * rows * HD, bytes_accessed=8 * MIB, transcendentals=heads * rows * rows
        ),
        name="cross_attention_back",
    )(projected, state_side, state_side, out, log, grad_attended)


def state_back_kernel(live_ref, cq_ref, sq_ref, scq_ref, sk_ref, sv_ref, tk_ref, tv_ref,
                      co_ref, so_ref, io_ref, cl_ref, sl_ref, il_ref, cg_ref, sg_ref, ig_ref,
                      gcq_ref, gsq_ref, gscq_ref, gsk_ref, gsv_ref, gtk_ref, gtv_ref):
    rows = cq_ref.shape[0]
    sums = [0.0] * 4
    for start in range(0, rows, TILE):
        at = slice(start, start + TILE)
        key = lax.broadcasted_iota(jnp.int32, (rows, TILE), 0)
        for q_ref, k_ref, v_ref, o_ref, l_ref, g_ref, gq_ref, mask, slot in (
            (cq_ref, sk_ref, sv_ref, co_ref, cl_ref, cg_ref, gcq_ref, None, 0),
            (sq_ref, sk_ref, sv_ref, so_ref, sl_ref, sg_ref, gsq_ref, None, 0),
            (scq_ref, tk_ref, tv_ref, io_ref, il_ref, ig_ref, gscq_ref, key < live_ref[0], 2),
        ):
            grad_out = g_ref[at, :]
            grad_q, grad_k, grad_v = attend_back_tile(
                q_ref[at, :], k_ref[...], v_ref[...], mask, l_ref[0, :, at], grad_out,
                row_delta(o_ref[at, :], grad_out))
            gq_ref[at, :] = (grad_q * RAW_SCALE).T.astype(jnp.bfloat16)
            sums[slot] = sums[slot] + grad_k
            sums[slot + 1] = sums[slot + 1] + grad_v
    gsk_ref[...] = (sums[0] * RAW_SCALE).astype(jnp.bfloat16)
    gsv_ref[...] = sums[1].astype(jnp.bfloat16)
    gtk_ref[...] = sums[2] * RAW_SCALE
    gtv_ref[...] = sums[3]


def state_attention_back(projected, state_side, live_keys, outs, logs, grad_attended, grad_inner, block):
    rows, width = state_side.shape
    heads = width // 4 // HD
    def piece(offset):
        return pl.BlockSpec((rows, HD), lambda h: (block, h + offset))
    grad = jax.ShapeDtypeStruct((rows, width // 4), jnp.bfloat16)
    wide = jax.ShapeDtypeStruct((rows, width // 4), jnp.float32)
    return pl.pallas_call(
        state_back_kernel,
        grid=(heads,),
        in_specs=[pl.BlockSpec(memory_space=pltpu.SMEM),
                  piece(heads), column(rows, 0), column(rows, heads), column(rows, 2 * heads), column(rows, 3 * heads),
                  piece(2 * heads), piece(3 * heads)] + [column(rows, 0)] * 3 + [stat(rows)] * 3
                 + [piece(heads), column(rows, 0), column(rows, heads)],
        out_specs=[column(rows, 0)] * 7,
        out_shape=[grad] * 5 + [wide] * 2,
        compiler_params=pltpu.CompilerParams(vmem_limit_bytes=40 * MIB),
        cost_estimate=pl.CostEstimate(
            flops=heads * 30 * rows * rows * HD, bytes_accessed=16 * MIB, transcendentals=3 * heads * rows * rows
        ),
        name="state_attention_back",
    )(live_keys, projected, state_side, state_side, state_side, state_side, projected, projected,
      *outs, *logs, grad_attended, grad_inner, grad_inner)


def lines_along_z(dp):
    return [[line + 4 * z for z in range(dp // 4)] for line in range(4)]


def swap(values, axis):
    if axis == "y":
        return lax.ppermute(values, "fsdp", [(0, 1), (1, 0)])
    bit = {"x": 2, "core": 1}[axis]
    return lax.ppermute(values, "dp", [(d, d ^ bit) for d in range(16)])


def place():
    dp = lax.axis_index("dp")
    return jnp.stack([(dp // 2) % 2, dp % 2, lax.axis_index("fsdp")]).astype(jnp.int32)


def assemble_kernel(sizes, place_ref, *refs):
    x, core, y = place_ref[0], place_ref[1], place_ref[2]
    pieces, outs = refs[:8], refs[8:]
    half = pieces[0].shape[-1]
    for which, piece in enumerate(pieces):
        order, far, other = which // 4, (which // 2) % 2, which % 2
        for near in range(2):
            dx, dy = (near, far) if order == 0 else (far, near)
            line = (x ^ dx) * 2 + (core ^ other)
            at = pl.multiple_of((y ^ dy) * (2 * half) + order * half, 128)
            row = 0
            for size, out in zip(sizes, outs):
                out[0, line, :, pl.ds(at, half)] = piece[near, 0, row : row + size, :]
                row += size


def assemble(pieces, sizes, where):
    _, depth, rows, half = pieces[0].shape
    outs = pl.pallas_call(
        partial(assemble_kernel, sizes),
        grid_spec=pltpu.PrefetchScalarGridSpec(
            num_scalar_prefetch=1,
            grid=(depth,),
            in_specs=[pl.BlockSpec((2, 1, rows, half), lambda z, p: (0, z, 0, 0))] * 8,
            out_specs=[
                pl.BlockSpec((1, 4, size, 4 * half), lambda z, p: (z, 0, 0, 0)) for size in sizes
            ],
        ),
        out_shape=[
            jax.ShapeDtypeStruct((depth, 4, size, 4 * half), jnp.bfloat16) for size in sizes
        ],
        compiler_params=pltpu.CompilerParams(vmem_limit_bytes=40 * MIB),
        cost_estimate=pl.CostEstimate(
            flops=0, bytes_accessed=64 * depth * half * rows, transcendentals=0
        ),
        name="assemble",
    )(where, *pieces)
    return [out.reshape(-1, 4 * half) for out in outs]


def gather_group(blocks, where):
    packed = blocks[0] if len(blocks) == 1 else jnp.concatenate(blocks, axis=0)
    lanes = lax.all_gather(packed, "dp", axis=0, axis_index_groups=lines_along_z(16))
    half = packed.shape[1] // 2
    first, second = lanes[:, :, :half], lanes[:, :, half:]
    first = jnp.stack([first, swap(first, "x")])
    second = jnp.stack([second, swap(second, "y")])
    pieces = [first, swap(first, "core")]
    far = swap(first, "y")
    pieces += [far, swap(far, "core"), second, swap(second, "core")]
    far = swap(second, "x")
    pieces += [far, swap(far, "core")]
    return assemble(pieces, [block.shape[0] for block in blocks], where)


def add(left, right):
    return left.astype(jnp.float32) + right.astype(jnp.float32)


def fold_core_kernel(place_ref, keep_ref, come_ref, kx_ref, sx_ref, ky_ref, sy_ref):
    half = come_ref.shape[-1] // 4
    y = place_ref[2]

    def along_x(out):
        for z in range(out.shape[0]):
            for part in range(2):
                at = slice(2 * part * half, (2 * part + 1) * half)
                out[z, :, part * half : (part + 1) * half] = narrow(
                    add(keep_ref[z, 0, 0, :, at], come_ref[z, 0, :, at])
                )

    def along_y(out, side):
        at = pl.ds(pl.multiple_of(side * 2 * half + half, 128), half)
        for z in range(out.shape[0]):
            out[z, 0] = narrow(add(keep_ref[z, 0, 0, :, at], come_ref[z, 0, :, at]))

    @pl.when(pl.program_id(0) == 0)
    def _():
        along_x(kx_ref)

    @pl.when(pl.program_id(0) == 1)
    def _():
        along_x(sx_ref)

    along_y(ky_ref, y)
    along_y(sy_ref, 1 - y)


def fold_core(grad, come, where):
    depth, _, _, rows, cols = grad.shape
    half = cols // 4
    across_x = jax.ShapeDtypeStruct((depth, rows, 2 * half), jnp.bfloat16)
    across_y = jax.ShapeDtypeStruct((depth, 2, rows, half), jnp.bfloat16)
    whole = pl.BlockSpec((depth, rows, 2 * half), lambda d, p: (0, 0, 0))
    part = pl.BlockSpec((depth, 1, rows, half), lambda d, p: (0, p[0] ^ d, 0, 0))
    return pl.pallas_call(
        fold_core_kernel,
        grid_spec=pltpu.PrefetchScalarGridSpec(
            num_scalar_prefetch=1,
            grid=(2,),
            in_specs=[
                pl.BlockSpec((depth, 1, 1, rows, cols), lambda d, p: (0, p[0] ^ d, p[1], 0, 0)),
                pl.BlockSpec((depth, 1, rows, cols), lambda d, p: (0, p[0] ^ d, 0, 0)),
            ],
            out_specs=[whole, whole, part, part],
        ),
        out_shape=[across_x, across_x, across_y, across_y],
        compiler_params=pltpu.CompilerParams(vmem_limit_bytes=40 * MIB),
        cost_estimate=pl.CostEstimate(
            flops=grad.size // 2, bytes_accessed=3 * grad.size, transcendentals=0
        ),
        name="fold_core",
    )(where, grad, come)


def fold_far_kernel(place_ref, kx_ref, rx_ref, ky_ref, ry_ref, kxy_ref, sxy_ref, kyx_ref, syx_ref):
    half = kxy_ref.shape[-1]
    x, y = place_ref[0], place_ref[2]
    for z in range(kx_ref.shape[0]):
        for side, out in ((y, kxy_ref), (1 - y, sxy_ref)):
            at = pl.ds(pl.multiple_of(side * half, 128), half)
            out[z] = narrow(add(kx_ref[z, :, at], rx_ref[z, :, at]))
        for side, out in ((x, kyx_ref), (1 - x, syx_ref)):
            out[z] = narrow(add(ky_ref[z, side], ry_ref[z, side]))


def fold_far(kx, rx, ky, ry, where):
    depth, _, rows, half = ky.shape
    step = depth // 2
    out = jax.ShapeDtypeStruct((depth, rows, half), jnp.bfloat16)
    whole = pl.BlockSpec((step, rows, 2 * half), lambda z, p: (z, 0, 0))
    pair = pl.BlockSpec((step, 2, rows, half), lambda z, p: (z, 0, 0, 0))
    return pl.pallas_call(
        fold_far_kernel,
        grid_spec=pltpu.PrefetchScalarGridSpec(
            num_scalar_prefetch=1,
            grid=(2,),
            in_specs=[whole, whole, pair, pair],
            out_specs=[pl.BlockSpec((step, rows, half), lambda z, p: (z, 0, 0))] * 4,
        ),
        out_shape=[out] * 4,
        compiler_params=pltpu.CompilerParams(vmem_limit_bytes=40 * MIB),
        cost_estimate=pl.CostEstimate(
            flops=2 * kx.size, bytes_accessed=12 * kx.size, transcendentals=0
        ),
        name="fold_far",
    )(where, kx, rx, ky, ry)


def fold_last_kernel(kxy_ref, rxy_ref, kyx_ref, ryx_ref, out_ref):
    half = kxy_ref.shape[-1]
    out_ref[:, :, :half] = narrow(add(kxy_ref[...], rxy_ref[...]))
    out_ref[:, :, half:] = narrow(add(kyx_ref[...], ryx_ref[...]))


def fold_last(kxy, rxy, kyx, ryx):
    depth, rows, half = kxy.shape
    step = depth // 2
    return pl.pallas_call(
        fold_last_kernel,
        grid=(2,),
        in_specs=[pl.BlockSpec((step, rows, half), lambda z: (z, 0, 0))] * 4,
        out_specs=pl.BlockSpec((step, rows, 2 * half), lambda z: (z, 0, 0)),
        out_shape=jax.ShapeDtypeStruct((depth, rows, 2 * half), jnp.bfloat16),
        compiler_params=pltpu.CompilerParams(vmem_limit_bytes=40 * MIB),
        cost_estimate=pl.CostEstimate(
            flops=2 * kxy.size, bytes_accessed=12 * kxy.size, transcendentals=0
        ),
        name="fold_last",
    )(kxy, rxy, kyx, ryx)


def scatter_group(grad, where):
    rows, cols = grad.shape[0] // 16, grad.shape[1]
    grad = grad.reshape(4, 2, 2, rows, cols)
    come = swap(lax.dynamic_index_in_dim(grad, 1 - where[1], 2, keepdims=False), "core")
    kx, sx, ky, sy = fold_core(grad, come, where)
    kxy, sxy, kyx, syx = fold_far(kx, swap(sx, "x"), ky, swap(sy, "y"), where)
    line = fold_last(kxy, swap(sxy, "y"), kyx, swap(syx, "x"))
    return lax.psum_scatter(
        line.reshape(4 * rows, cols // 2),
        "dp",
        scatter_dimension=0,
        axis_index_groups=lines_along_z(16),
        tiled=True,
    )


def paired():
    return lax.axis_size("dp") == 16 and lax.axis_size("fsdp") == 2


def gather(blocks, where):
    if paired():
        return gather_group(blocks, where)
    rows = [lax.all_gather(block, "fsdp", axis=1, tiled=True) for block in blocks]
    return [lax.all_gather(block, "dp", axis=0, tiled=True) for block in rows]


def scatter(grad, where):
    if paired():
        return scatter_group(grad, where)
    rows = lax.psum_scatter(grad, "dp", scatter_dimension=0, tiled=True)
    return lax.psum_scatter(rows, "fsdp", scatter_dimension=1, tiled=True)


def gather_vectors(vectors):
    return lax.all_gather(vectors, "fsdp", axis=1, tiled=True).astype(jnp.float32)


def scatter_vectors(vectors):
    every = lax.all_gather(vectors, ("dp", "fsdp"), axis=0)
    part = vectors.shape[1] // lax.axis_size("fsdp")
    total = jnp.sum(every, axis=0)
    return lax.dynamic_slice_in_dim(total, lax.axis_index("fsdp") * part, part, axis=1)


def shards(
    tokens,
    incoming,
    document_lengths,
    output_grad,
    token_proj,
    state_proj,
    token_out,
    state_out,
    gate_weight,
    init_state,
    hidden_in,
    hidden_out,
    token_gain,
    state_gain,
    hidden_gain,
    gate_bias,
):
    where = place()
    gains = gather_vectors(jnp.stack([token_gain, state_gain, hidden_gain, gate_bias]))
    token_gain_f, state_gain_f, hidden_gain_f, gate_bias_f = gains
    (full_token_proj,) = gather([token_proj], where)
    (full_state_proj,) = gather([state_proj], where)
    full_state_out, full_gate_weight, full_token_out, full_init = gather(
        [state_out, gate_weight, token_out, init_state], where
    )
    (full_hidden_in,) = gather([hidden_in], where)
    (full_hidden_out,) = gather([hidden_out], where)
    seg_len, width = tokens.shape
    window = WINDOW
    blocks = seg_len // window
    segment_id = lax.axis_index(("dp", "fsdp"))
    counts = (document_lengths + seg_len - 1) // seg_len
    ends = jnp.cumsum(counts)
    starts = ends - counts
    inside = (segment_id >= starts) & (segment_id < ends)
    valid_len = jnp.sum(
        jnp.where(
            inside, jnp.minimum(seg_len, document_lengths - (segment_id - starts) * seg_len), 0
        )
    )
    first = jnp.any(segment_id == starts)
    piece = tokens.astype(jnp.float32)
    normed_low = narrow(layer_norm(piece, token_gain_f))
    projected = narrow(matmul(normed_low, full_token_proj))
    self_out, self_log = self_attention(projected, window)
    state = jnp.where(first, full_init.astype(jnp.float32), incoming[0].astype(jnp.float32))
    state_inputs, normed_states, sides, inner_cats, mixed_states, gates, lives, key_counts = (
        [],
        [],
        [],
        [],
        [],
        [],
        [],
        [],
    )
    state_outs, state_logs = ([], [])
    for block_idx in range(blocks):
        start = block_idx * window
        state_normed = narrow(layer_norm(state, state_gain_f))
        state_side = narrow(matmul(state_normed, full_state_proj))
        live_keys = jnp.clip(valid_len - start, 0, window).astype(jnp.int32).reshape(1)
        outs = state_attention(projected, state_side, live_keys, block_idx)
        inner_cat = jnp.concatenate([outs[1], outs[2]], axis=1)
        mixed_state = narrow(matmul(inner_cat, full_state_out))
        gate = jax.nn.sigmoid(matmul(mixed_state, full_gate_weight) + gate_bias_f)
        updated = gate * state + (1.0 - gate) * jnp.tanh(mixed_state.astype(jnp.float32))
        live = jnp.where(start < valid_len, 1.0, 0.0).astype(jnp.float32)
        state_inputs.append(state)
        normed_states.append(state_normed)
        sides.append(state_side)
        inner_cats.append(inner_cat)
        mixed_states.append(mixed_state)
        gates.append(gate)
        lives.append(live)
        key_counts.append(live_keys)
        state_outs.append(outs[:3])
        state_logs.append(outs[3:])
        state = state + live * (updated - state)
    cross_out = jnp.concatenate([outs[0] for outs in state_outs], axis=0)
    attended = jnp.concatenate([self_out, cross_out], axis=1)
    middle = piece + matmul(attended, full_token_out)
    hidden_normed = narrow(layer_norm(middle, hidden_gain_f))
    hidden_pre = matmul(hidden_normed, full_hidden_in)
    activated = narrow(jax.nn.gelu(hidden_pre, approximate=True))
    result = middle + matmul(activated, full_hidden_out)
    grad_result = output_grad.astype(jnp.float32)
    grad_hidden_out = matmul_left_t(activated, output_grad)
    grad_activated = matmul_right_t(output_grad, full_hidden_out)
    _, gelu_pull = jax.vjp(partial(jax.nn.gelu, approximate=True), hidden_pre)
    grad_pre = narrow(gelu_pull(grad_activated)[0])
    grad_hidden_in = matmul_left_t(hidden_normed, grad_pre)
    grad_middle_part, grad_hidden_gain = norm_back(
        middle, hidden_gain_f, matmul_right_t(grad_pre, full_hidden_in)
    )
    grad_middle = grad_result + grad_middle_part
    grad_branch = narrow(grad_middle)
    grad_token_out = matmul_left_t(attended, grad_branch)
    grad_attended = narrow(matmul_right_t(grad_branch, full_token_out))
    last = blocks - 1
    last_start = last * window
    cross_grad, last_keys_grad, last_values_grad = cross_attention_back(
        projected,
        sides[last],
        state_outs[last][0],
        state_logs[last][0],
        grad_attended,
        last,
    )
    cross_grads = [cross_grad]
    grad_side = jnp.concatenate([last_keys_grad, last_values_grad], axis=1)
    grad_state_proj = jnp.concatenate(
        [
            jnp.zeros((width, 2 * width), jnp.float32),
            matmul_left_t(normed_states[last], grad_side),
        ],
        axis=1,
    )
    grad_state, grad_state_gain = norm_back(
        state_inputs[last], state_gain_f, matmul_right_t(grad_side, full_state_proj[:, 2 * width :])
    )
    grad_state_out = jnp.zeros((2 * width, width), jnp.float32)
    grad_gate_weight = jnp.zeros((width, width), jnp.float32)
    grad_gate_bias = jnp.zeros((width,), jnp.float32)
    extra_keys, extra_values = ([], [])
    for block_idx in reversed(range(last)):
        state_side = sides[block_idx]
        gate = gates[block_idx]
        live = lives[block_idx]
        state_in = state_inputs[block_idx]
        tanh_mixed = jnp.tanh(mixed_states[block_idx].astype(jnp.float32))
        grad_updated = live * grad_state
        grad_direct = (1.0 - live) * grad_state + grad_updated * gate
        grad_gate_pre = gate * (1.0 - gate) * grad_updated * (state_in - tanh_mixed)
        grad_gate_bias = grad_gate_bias + jnp.sum(grad_gate_pre, axis=0)
        grad_gate_low = narrow(grad_gate_pre)
        grad_gate_weight = grad_gate_weight + matmul_left_t(mixed_states[block_idx], grad_gate_low)
        grad_mixed = narrow(
            matmul_right_t(grad_gate_low, full_gate_weight)
            + grad_updated * (1.0 - gate) * (1.0 - tanh_mixed * tanh_mixed)
        )
        grad_state_out = grad_state_out + matmul_left_t(inner_cats[block_idx], grad_mixed)
        grad_inner = narrow(matmul_right_t(grad_mixed, full_state_out))
        parts = state_attention_back(
            projected,
            state_side,
            key_counts[block_idx],
            state_outs[block_idx],
            state_logs[block_idx],
            grad_attended,
            grad_inner,
            block_idx,
        )
        cross_grads.insert(0, parts[0])
        grad_side = jnp.concatenate(parts[1:5], axis=1)
        extra_keys.insert(0, parts[5])
        extra_values.insert(0, parts[6])
        grad_state_proj = grad_state_proj + matmul_left_t(normed_states[block_idx], grad_side)
        grad_state_norm, grad_gain_part = norm_back(
            state_in, state_gain_f, matmul_right_t(grad_side, full_state_proj)
        )
        grad_state_gain = grad_state_gain + grad_gain_part
        grad_state = grad_direct + grad_state_norm
    self_grad, keys_grad, values_grad = self_attention_back(
        projected,
        self_out,
        self_log,
        grad_attended,
        jnp.concatenate(extra_keys, axis=0),
        jnp.concatenate(extra_values, axis=0),
        window,
    )
    grad_init = jnp.where(first, grad_state, 0.0)
    grad_projected = jnp.concatenate(
        [self_grad, jnp.concatenate(cross_grads, axis=0), keys_grad, values_grad], axis=1
    )
    grad_token_proj = matmul_left_t(normed_low, grad_projected)
    grad_piece, grad_token_gain = norm_back(
        piece, token_gain_f, matmul_right_t(grad_projected, full_token_proj)
    )
    tokens_grad = narrow(grad_middle + grad_piece)
    vectors = jnp.stack([grad_token_gain, grad_state_gain, grad_hidden_gain, grad_gate_bias])
    vector_grads = scatter_vectors(vectors)
    matrix_grads = [
        scatter(narrow(grad), where).astype(jnp.float32)
        for grad in (
            grad_token_proj,
            grad_state_proj,
            grad_token_out,
            grad_state_out,
            grad_gate_weight,
            grad_init,
            grad_hidden_in,
            grad_hidden_out,
        )
    ]
    return (
        narrow(result),
        narrow(state)[None],
        tokens_grad,
        matrix_grads[0],
        matrix_grads[1],
        matrix_grads[2],
        matrix_grads[3],
        matrix_grads[4],
        matrix_grads[5],
        matrix_grads[6],
        matrix_grads[7],
        vector_grads[0],
        vector_grads[1],
        vector_grads[2],
        vector_grads[3],
    )


def solution(mesh):
    return jax.shard_map(
        shards,
        mesh=mesh,
        in_specs=(
            P(("dp", "fsdp"), None),
            P(("dp", "fsdp"), None, None),
            P(),
            P(("dp", "fsdp"), None),
            P("dp", "fsdp"),
            P("dp", "fsdp"),
            P("dp", "fsdp"),
            P("dp", "fsdp"),
            P("dp", "fsdp"),
            P("dp", "fsdp"),
            P("dp", "fsdp"),
            P("dp", "fsdp"),
            P("fsdp"),
            P("fsdp"),
            P("fsdp"),
            P("fsdp"),
        ),
        out_specs=(
            P(("dp", "fsdp"), None),
            P(("dp", "fsdp"), None, None),
            P(("dp", "fsdp"), None),
            P("dp", "fsdp"),
            P("dp", "fsdp"),
            P("dp", "fsdp"),
            P("dp", "fsdp"),
            P("dp", "fsdp"),
            P("dp", "fsdp"),
            P("dp", "fsdp"),
            P("dp", "fsdp"),
            P("fsdp"),
            P("fsdp"),
            P("fsdp"),
            P("fsdp"),
        ),
        check_vma=False,
    )
```

```python
from functools import partial
import math

import jax
import jax.numpy as jnp
from jax import lax
from jax.experimental import pallas as pl
from jax.experimental.pallas import tpu as pltpu
from jax.sharding import PartitionSpec as P

HD = 128
WINDOW = 512
MIB = 1 << 20


norm_eps = 1e-06
masked_score = -1e30
EXP_SCALE = math.log2(math.e) / math.sqrt(HD)
RAW_SCALE = 1.0 / math.sqrt(HD)
NT = (((1,), (1,)), ((), ()))
TN = (((0,), (0,)), ((), ()))
NN = (((1,), (0,)), ((), ()))


def narrow(values):
    return values.astype(jnp.bfloat16)


def matmul_left_t(left, right):
    return lax.dot_general(left, right, TN, preferred_element_type=jnp.float32)


def launch(body, operands, *, grid, in_specs, out_specs, out_shape, name, flops, after=(), where=None, scratch=(), aliases=None, exps=0, limit=48):
    count = len(operands)
    late = len(after)
    lead = 0 if where is None else 1

    def run(*refs):
        body(*refs[: lead + count], *refs[lead + count + late :])

    specs = list(in_specs) + [pl.BlockSpec(memory_space=pl.ANY)] * late
    size = sum(math.prod(item.shape) * item.dtype.itemsize for item in (*operands, *out_shape))
    kwargs = dict(grid=grid, in_specs=specs, out_specs=list(out_specs))
    if where is None:
        kwargs["scratch_shapes"] = list(scratch)
    else:
        kwargs = dict(
            grid_spec=pltpu.PrefetchScalarGridSpec(
                num_scalar_prefetch=1, scratch_shapes=list(scratch), **kwargs
            )
        )
    return pl.pallas_call(
        run,
        out_shape=list(out_shape),
        input_output_aliases=aliases or {},
        compiler_params=pltpu.CompilerParams(vmem_limit_bytes=limit * MIB),
        cost_estimate=pl.CostEstimate(flops=int(flops), bytes_accessed=int(size), transcendentals=int(exps)),
        name=name,
        **kwargs,
    )(*(() if where is None else (where,)), *operands, *after)


def shaped(shape, dtype=jnp.bfloat16):
    return jax.ShapeDtypeStruct(shape, dtype)


def whole(shape):
    return pl.BlockSpec(shape, lambda *ids: (0,) * len(shape))


SMEM = pl.BlockSpec(memory_space=pltpu.SMEM)
F32 = jnp.float32


def norm_rows(values):
    centered = values - jnp.mean(values, axis=-1, keepdims=True)
    return centered, lax.rsqrt(jnp.mean(centered * centered, axis=-1, keepdims=True) + norm_eps)


def norm_back_rows(values, gain, grad):
    centered, inverse = norm_rows(values)
    normal = centered * inverse
    scaled = grad * gain
    mean = jnp.mean(scaled, axis=-1, keepdims=True)
    along = jnp.mean(scaled * normal, axis=-1, keepdims=True)
    return inverse * (scaled - mean - normal * along), jnp.sum(grad * normal, axis=0, keepdims=True)


ROWS = 128


def norm_project_kernel(x_ref, gain_ref, w_ref, normed_ref, out_ref):
    @pl.when(pl.program_id(0) == 0)
    def _():
        @pl.loop(0, x_ref.shape[0] // ROWS)
        def _(i):
            at = pl.ds(pl.multiple_of(i * ROWS, ROWS), ROWS)
            centered, inverse = norm_rows(x_ref[at, :].astype(F32))
            normed_ref[at, :] = narrow(centered * inverse * gain_ref[...])

    out_ref[...] = narrow(dot(normed_ref[...], w_ref[...], NN))


def norm_project(x, gain, weight, after=()):
    rows, width = x.shape
    cols = weight.shape[1]
    step = 512
    return launch(
        norm_project_kernel, [x, gain, weight], after=after, name="norm_project", grid=(cols // step,),
        in_specs=[whole((rows, width)), whole((1, width)), pl.BlockSpec((width, step), lambda i: (0, i))],
        out_specs=[whole((rows, width)), pl.BlockSpec((rows, step), lambda i: (0, i))],
        out_shape=[shaped((rows, width)), shaped((rows, cols))],
        flops=2 * rows * width * cols,
    )


def update_kernel(live_ref, self_ref, cross_ref, out_w_ref, gate_w_ref, bias_ref, state_ref, mixed_ref, gate_ref, new_ref):
    width = self_ref.shape[1]
    mixed = narrow(dot(self_ref[...], out_w_ref[:width, :], NN) + dot(cross_ref[...], out_w_ref[width:, :], NN))
    mixed_ref[...] = mixed
    gate = jax.nn.sigmoid(dot(mixed, gate_w_ref[...], NN) + bias_ref[...])
    gate_ref[...] = gate
    state = state_ref[...]
    updated = gate * state + (1.0 - gate) * jnp.tanh(mixed.astype(F32))
    new_ref[...] = state + live_ref[0] * (updated - state)


def update_state(live, inner_self, inner_cross, state_out, gate_weight, bias, state, after=()):
    rows, width = state.shape
    step = 256
    tile = pl.BlockSpec((step, width), lambda i: (i, 0))
    return launch(
        update_kernel, [live, inner_self, inner_cross, state_out, gate_weight, bias, state],
        after=after, name="update_state", grid=(rows // step,),
        in_specs=[SMEM, tile, tile, whole(state_out.shape), whole(gate_weight.shape), whole((1, width)), tile],
        out_specs=[tile, tile, tile],
        out_shape=[shaped((rows, width)), shaped((rows, width), F32), shaped((rows, width), F32)],
        flops=6 * rows * width * width, exps=2 * rows * width,
    )


def branch_kernel(self_ref, cross_ref, w_ref, x_ref, gain_ref, middle_ref, normed_ref):
    width = self_ref.shape[1]
    middle = x_ref[...].astype(F32) + (
        dot(self_ref[...], w_ref[:width, :], NN) + dot(cross_ref[...], w_ref[width:, :], NN)
    )
    middle_ref[...] = middle
    centered, inverse = norm_rows(middle)
    normed_ref[...] = narrow(centered * inverse * gain_ref[...])


def branch(self_out, cross_out, token_out, x, gain, after=()):
    rows, width = x.shape
    step = 256
    tile = pl.BlockSpec((step, width), lambda i: (i, 0))
    return launch(
        branch_kernel, [self_out, cross_out, token_out, x, gain], after=after, name="branch", grid=(rows // step,),
        in_specs=[tile, tile, whole(token_out.shape), tile, whole((1, width))],
        out_specs=[tile, tile],
        out_shape=[shaped((rows, width), F32), shaped((rows, width))],
        flops=4 * rows * width * width,
    )


GELU_A = math.sqrt(2.0 / math.pi)
GELU_B = 0.044715


def hidden_kernel(normed_ref, w_ref, active_ref, slope_ref):
    for start in range(0, normed_ref.shape[0], 256):
        at = slice(start, start + 256)
        v = dot(normed_ref[at, :], w_ref[...], NN)
        square = v * v
        t = jnp.tanh(v * (GELU_A + (GELU_A * GELU_B) * square))
        half = 0.5 + 0.5 * t
        active_ref[at, :] = narrow(v * half)
        slope = half + v * (1.0 - t * t) * (0.5 * GELU_A + (1.5 * GELU_A * GELU_B) * square)
        slope_ref[at, :] = narrow(slope)


def hidden(normed, weight, after=()):
    rows, width = normed.shape
    cols = weight.shape[1]
    step = 512
    tile = pl.BlockSpec((rows, step), lambda i: (0, i))
    return launch(
        hidden_kernel, [normed, weight], after=after, name="hidden", grid=(cols // step,),
        in_specs=[whole((rows, width)), pl.BlockSpec((width, step), lambda i: (0, i))],
        out_specs=[tile, tile], out_shape=[shaped((rows, cols))] * 2,
        flops=2 * rows * width * cols, exps=rows * cols,
    )


def result_kernel(active_ref, slope_ref, w_ref, middle_ref, grad_ref, result_ref, pre_ref, total_ref):
    first = pl.program_id(0) == 0
    for start in range(0, active_ref.shape[0], 256):
        at = slice(start, start + 256)
        pre_ref[at, :] = narrow(dot(grad_ref[at, :], w_ref[...], NT) * slope_ref[at, :].astype(F32))
        total_ref[at, :] = jnp.where(first, middle_ref[at, :], total_ref[at, :]) + dot(active_ref[at, :], w_ref[...], NN)

    @pl.when(pl.program_id(0) == pl.num_programs(0) - 1)
    def _():
        result_ref[...] = narrow(total_ref[...])


def result_and_pre(active, slope, weight, middle, grad, after=()):
    rows, hidden_units = active.shape
    width = middle.shape[1]
    step = 512
    tile = pl.BlockSpec((rows, step), lambda i: (0, i))
    return launch(
        result_kernel, [active, slope, weight, middle, grad], after=after, name="result_and_pre",
        grid=(hidden_units // step,),
        in_specs=[tile, tile, pl.BlockSpec((step, width), lambda i: (i, 0)), whole((rows, width)), whole((rows, width))],
        out_specs=[whole((rows, width)), tile],
        out_shape=[shaped((rows, width)), shaped((rows, hidden_units))],
        scratch=[pltpu.VMEM((rows, width), F32)],
        flops=4 * rows * width * hidden_units,
    )


def norm_back_kernel(parts, keep_wide, scale_ref, *refs):
    grads, (w_ref, x_ref, gain_ref, plus_ref) = refs[:parts], refs[parts : parts + 4]
    outs, total_ref = refs[parts + 4 : -1], refs[-1]
    i = pl.program_id(0)
    share = pl.num_programs(0) // parts

    @pl.when(i == 0)
    def _():
        total_ref[...] = jnp.zeros_like(total_ref)

    for part in range(parts):
        @pl.when(i // share == part)
        def _():
            total_ref[...] += dot(grads[part][...], w_ref[...], NT)

    @pl.when(i == pl.num_programs(0) - 1)
    def _():
        outs[0][...] = jnp.zeros_like(outs[0])

        @pl.loop(0, x_ref.shape[0] // ROWS)
        def _(j):
            at = pl.ds(pl.multiple_of(j * ROWS, ROWS), ROWS)
            grad, gain_grad = norm_back_rows(x_ref[at, :].astype(F32), gain_ref[...], total_ref[at, :])
            grad = grad + plus_ref[at, :].astype(F32)
            outs[0][...] += gain_grad
            outs[1][at, :] = narrow(jnp.where(scale_ref[0] > 0.0, grad, 0.0))
            if keep_wide:
                outs[2][at, :] = grad


def norm_back_project(grads, weight, x, gain, plus, name, keep_wide=False, offset=0, scale=None, after=()):
    rows, width = x.shape
    step = 512
    share = grads[0].shape[1] // step
    parts = len(grads)
    steps = parts * share
    def part_spec(part):
        return pl.BlockSpec((rows, step), lambda i: (0, jnp.clip(i - part * share, 0, share - 1)))
    out_shape = [shaped((1, width), F32), shaped((rows, width))]
    if keep_wide:
        out_shape.append(shaped((rows, width), F32))
    if scale is None:
        scale = jnp.ones((1,), F32)
    return launch(
        partial(norm_back_kernel, parts, keep_wide), [scale, *grads, weight, x, gain, plus], after=after, name=name,
        grid=(steps,),
        in_specs=[SMEM] + [part_spec(part) for part in range(parts)]
        + [pl.BlockSpec((width, step), lambda i: (0, i + offset // step)), whole((rows, width)), whole((1, width)), whole((rows, width))],
        out_specs=[whole(item.shape) for item in out_shape], out_shape=out_shape,
        scratch=[pltpu.VMEM((rows, width), F32)],
        flops=2 * rows * width * steps * step,
    )


def spread_kernel(grad_ref, w_ref, out_ref):
    out_ref[...] = narrow(dot(grad_ref[...], w_ref[...], NT))


def spread(grad, weight, after=()):
    rows, width = grad.shape
    cols = weight.shape[0]
    step = 512
    return launch(
        spread_kernel, [grad, weight], after=after, name="spread", grid=(cols // step,),
        in_specs=[whole((rows, width)), pl.BlockSpec((step, width), lambda i: (i, 0))],
        out_specs=[pl.BlockSpec((rows, step), lambda i: (0, i))],
        out_shape=[shaped((rows, cols))], flops=2 * rows * width * cols,
    )[0]


def gate_back_kernel(live_ref, grad_ref, gate_ref, state_ref, mixed_ref, gate_w_ref, out_w_ref,
                     pre_ref, grad_mixed_ref, inner_ref, direct_ref, bias_ref):
    grad, gate, live = grad_ref[...], gate_ref[...], live_ref[0]
    tanh_mixed = jnp.tanh(mixed_ref[...].astype(F32))
    updated = live * grad
    direct_ref[...] = (1.0 - live) * grad + updated * gate
    pre = gate * (1.0 - gate) * updated * (state_ref[...] - tanh_mixed)

    @pl.when(pl.program_id(0) == 0)
    def _():
        bias_ref[...] = jnp.zeros_like(bias_ref)

    bias_ref[...] += jnp.sum(pre, axis=0, keepdims=True)
    low = narrow(pre)
    pre_ref[...] = low
    grad_mixed = narrow(
        dot(low, gate_w_ref[...], NT) + updated * (1.0 - gate) * (1.0 - tanh_mixed * tanh_mixed)
    )
    grad_mixed_ref[...] = grad_mixed
    inner_ref[...] = narrow(dot(grad_mixed, out_w_ref[...], NT))


def gate_back(live, grad, gate, state, mixed, gate_weight, state_out, after=()):
    rows, width = grad.shape
    step = 256
    tile = pl.BlockSpec((step, width), lambda i: (i, 0))
    wide = pl.BlockSpec((step, 2 * width), lambda i: (i, 0))
    return launch(
        gate_back_kernel, [live, grad, gate, state, mixed, gate_weight, state_out], after=after, name="gate_back",
        grid=(rows // step,),
        in_specs=[SMEM, tile, tile, tile, tile, whole(gate_weight.shape), whole(state_out.shape)],
        out_specs=[tile, tile, wide, tile, whole((1, width))],
        out_shape=[shaped((rows, width)), shaped((rows, width)), shaped((rows, 2 * width)), shaped((rows, width), F32), shaped((1, width), F32)],
        flops=6 * rows * width * width, exps=rows * width,
    )


def weight_grad_kernel(rows, plan, split, counts, place_ref, *refs):
    lefts, rights = refs[: counts[0]], refs[counts[0] : counts[0] + counts[1]]
    keep_ref, send_ref = refs[-2], refs[-1]
    core = place_ref[1]

    def run(which):
        turned = [lefts[item][...].T for item in which]
        col = 0
        for terms in plan:
            cols = rights[terms[0][1]].shape[1]
            for start in range(0, cols, 512):
                total = sum(
                    dot(turned[left], rights[right][:, start : start + 512], NN) for left, right in terms
                )
                total = narrow(total)
                at = slice(col + start, col + start + 512)
                for x in range(2):
                    even = total[2 * x * rows : (2 * x + 1) * rows]
                    odd = total[(2 * x + 1) * rows : (2 * x + 2) * rows]
                    keep_ref[0, x, :, at] = jnp.where(core == 0, even, odd)
                    send_ref[0, x, :, at] = jnp.where(core == 0, odd, even)
            col += cols

    if split:
        @pl.when(pl.program_id(0) < 2)
        def _():
            run([0])

        @pl.when(pl.program_id(0) >= 2)
        def _():
            run([1])
    else:
        run(range(len(lefts)))


def weight_grad(lefts, rights, plan, where, name, split=False, after=()):
    tokens = lefts[0].shape[0]
    total_rows = lefts[0].shape[1] * (len(lefts) if split else 1)
    rows = total_rows // 16
    cols = sum(rights[terms[0][1]].shape[1] for terms in plan)
    if split:
        left_specs = [
            pl.BlockSpec((tokens, 4 * rows), lambda z, p: (0, jnp.minimum(z, 1))),
            pl.BlockSpec((tokens, 4 * rows), lambda z, p: (0, jnp.maximum(z, 2) - 2)),
        ]
    else:
        left_specs = [pl.BlockSpec((item.shape[0], 4 * rows), lambda z, p: (0, z)) for item in lefts]
    out = pl.BlockSpec((1, 2, rows, cols), lambda z, p: (z, 0, 0, 0))
    return launch(
        partial(weight_grad_kernel, rows, plan, split, (len(lefts), len(rights))), [*lefts, *rights],
        where=where, after=after, name=name, grid=(4,),
        in_specs=left_specs + [whole(item.shape) for item in rights],
        out_specs=[out, out], out_shape=[shaped((4, 2, rows, cols))] * 2,
        flops=2 * tokens * total_rows * cols, limit=56,
    )


def dot(a, b, dims):
    return lax.dot_general(a, b, dims, preferred_element_type=jnp.float32)


def attend_tile(q, k, v, mask):
    scores = dot(k, q, NT)
    if mask is not None:
        scores = jnp.where(mask, scores, masked_score)
    top = jnp.max(scores, axis=0, keepdims=True)
    weights = jnp.exp2((scores - top) * EXP_SCALE)
    total = jnp.sum(weights, axis=0, keepdims=True)
    mixed = dot(v, weights.astype(jnp.bfloat16), TN) / total
    return mixed.T.astype(jnp.bfloat16), top * EXP_SCALE + jnp.log2(total)


def attend_back_tile(q, k, v, mask, log_total, grad_out, delta):
    probs = jnp.exp2(dot(k, q, NT) * EXP_SCALE - log_total)
    if mask is not None:
        probs = jnp.where(mask, probs, 0.0)
    grad_probs = dot(v, grad_out, NT)
    grad_raw = (probs * (grad_probs - delta)).astype(jnp.bfloat16)
    grad_v = dot(probs.astype(jnp.bfloat16), grad_out, NN)
    grad_k = dot(grad_raw, q, NN)
    grad_q = dot(k, grad_raw, TN)
    return grad_q, grad_k, grad_v


def row_delta(out, grad_out):
    both = out.astype(jnp.float32) * grad_out.astype(jnp.float32)
    return jnp.sum(both.T, axis=0, keepdims=True)


def band_mask(rows, cols, key_start, query_start, window):
    key = lax.broadcasted_iota(jnp.int32, (rows, cols), 0) + key_start
    query = lax.broadcasted_iota(jnp.int32, (rows, cols), 1) + query_start
    return (key <= query) & (key > query - window)


TILE = 256


def self_kernel(window, q_ref, k_ref, v_ref, out_ref, log_ref):
    rows = q_ref.shape[0]
    for start in range(0, rows, TILE):
        low = max(0, start - window)
        size = start + TILE - low
        mask = band_mask(size, TILE, low, start, window)
        out, log = attend_tile(
            q_ref[start : start + TILE, :], k_ref[low : low + size, :], v_ref[low : low + size, :], mask
        )
        out_ref[start : start + TILE, :] = out
        log_ref[0, :, start : start + TILE] = log


def column(rows, offset):
    return pl.BlockSpec((rows, HD), lambda h: (0, h + offset))


def stat(rows):
    return pl.BlockSpec((1, 1, rows), lambda h: (h, 0, 0))


def self_attention(projected, window, after=()):
    rows, width = projected.shape
    heads = width // 4 // HD
    return launch(
        partial(self_kernel, window), [projected] * 3, after=after, name="self_attention", grid=(heads,),
        in_specs=[column(rows, 0), column(rows, 2 * heads), column(rows, 3 * heads)],
        out_specs=[column(rows, 0), stat(rows)],
        out_shape=[shaped((rows, width // 4)), shaped((heads, 1, rows), F32)],
        flops=heads * 4 * 2304 * 256 * HD, exps=heads * 2304 * 256,
    )


def block_column(rows, block, offset):
    return pl.BlockSpec((rows, HD), lambda h: (block, h + offset))


def cross_kernel(q_ref, k_ref, v_ref, *refs):
    out_ref, log_ref = refs[-2:]
    for start in range(0, q_ref.shape[0], TILE):
        at = slice(start, start + TILE)
        out_ref[at, :], log_ref[0, :, at] = attend_tile(q_ref[at, :], k_ref[...], v_ref[...], None)


def cross_attention(projected, state_side, block, before=None, after=()):
    rows, width = state_side.shape
    heads = width // 4 // HD
    operands = [projected, state_side, state_side]
    specs = [block_column(rows, block, heads), column(rows, 2 * heads), column(rows, 3 * heads)]
    if before is not None:
        operands.append(before)
        specs.append(pl.BlockSpec(memory_space=pl.ANY))
    return launch(
        cross_kernel, operands, after=after, name="cross_attention", grid=(heads,), in_specs=specs,
        out_specs=[block_column(rows, block, 0), stat(rows)],
        out_shape=[shaped((projected.shape[0], width // 4)), shaped((heads, 1, rows), F32)],
        aliases=None if before is None else {3: 0},
        flops=heads * 4 * rows * rows * HD, exps=heads * rows * rows,
    )


def inner_kernel(live_ref, sq_ref, scq_ref, sk_ref, sv_ref, tk_ref, tv_ref, self_ref, cross_ref, self_log, cross_log):
    rows = sq_ref.shape[0]
    for start in range(0, rows, TILE):
        at = slice(start, start + TILE)
        self_ref[at, :], self_log[0, :, at] = attend_tile(sq_ref[at, :], sk_ref[...], sv_ref[...], None)
        key = lax.broadcasted_iota(jnp.int32, (rows, TILE), 0)
        cross_ref[at, :], cross_log[0, :, at] = attend_tile(
            scq_ref[at, :], tk_ref[...], tv_ref[...], key < live_ref[0]
        )


def inner_attention(projected, state_side, live_keys, block, after=()):
    rows, width = state_side.shape
    heads = width // 4 // HD
    return launch(
        inner_kernel, [live_keys] + [state_side] * 4 + [projected] * 2, after=after, name="inner_attention", grid=(heads,),
        in_specs=[SMEM] + [column(rows, part * heads) for part in range(4)]
        + [block_column(rows, block, 2 * heads), block_column(rows, block, 3 * heads)],
        out_specs=[column(rows, 0)] * 2 + [stat(rows)] * 2,
        out_shape=[shaped((rows, width // 4))] * 2 + [shaped((heads, 1, rows), F32)] * 2,
        flops=heads * 8 * rows * rows * HD, exps=2 * heads * rows * rows,
    )


def self_back_kernel(window, q_ref, k_ref, v_ref, out_ref, log_ref, grad_ref, ek_ref, ev_ref, gq_ref, gk_ref, gv_ref, sk_ref, sv_ref):
    rows = q_ref.shape[0]
    extra = ek_ref.shape[0]
    sk_ref[...] = jnp.zeros_like(sk_ref)
    sv_ref[:extra, :] = ev_ref[...]
    sv_ref[extra:, :] = jnp.zeros((rows - extra, HD), jnp.float32)
    for start in range(0, rows, TILE):
        at = slice(start, start + TILE)
        low = max(0, start - window)
        size = start + TILE - low
        keys = slice(low, low + size)
        mask = band_mask(size, TILE, low, start, window)
        grad_out = grad_ref[at, :]
        grad_q, grad_k, grad_v = attend_back_tile(
            q_ref[at, :], k_ref[keys, :], v_ref[keys, :], mask, log_ref[0, :, at], grad_out,
            row_delta(out_ref[at, :], grad_out))
        gq_ref[at, :] = (grad_q * RAW_SCALE).T.astype(jnp.bfloat16)
        sk_ref[keys, :] += grad_k
        sv_ref[keys, :] += grad_v
    gk_ref[:extra, :] = (sk_ref[:extra, :] * RAW_SCALE + ek_ref[...]).astype(jnp.bfloat16)
    gk_ref[extra:, :] = (sk_ref[extra:, :] * RAW_SCALE).astype(jnp.bfloat16)
    gv_ref[...] = sv_ref[...].astype(jnp.bfloat16)


def cross_back_kernel(cq_ref, sk_ref, sv_ref, out_ref, log_ref, grad_ref, gq_ref, gk_ref, gv_ref):
    rows = cq_ref.shape[0]
    total_k = total_v = 0.0
    for start in range(0, rows, TILE):
        at = slice(start, start + TILE)
        grad_out = grad_ref[at, :]
        grad_q, grad_k, grad_v = attend_back_tile(
            cq_ref[at, :], sk_ref[...], sv_ref[...], None, log_ref[0, :, at], grad_out,
            row_delta(out_ref[at, :], grad_out))
        gq_ref[at, :] = (grad_q * RAW_SCALE).T.astype(jnp.bfloat16)
        total_k = total_k + grad_k
        total_v = total_v + grad_v
    gk_ref[...] = (total_k * RAW_SCALE).astype(jnp.bfloat16)
    gv_ref[...] = total_v.astype(jnp.bfloat16)


def state_back_kernel(live_ref, cq_ref, sq_ref, scq_ref, sk_ref, sv_ref, tk_ref, tv_ref,
                      co_ref, so_ref, io_ref, cl_ref, sl_ref, il_ref, cg_ref, sg_ref, ig_ref, before_ref,
                      gcq_ref, gsq_ref, gscq_ref, gsk_ref, gsv_ref, gtk_ref, gtv_ref):
    rows = cq_ref.shape[0]
    sums = [0.0] * 4
    for start in range(0, rows, TILE):
        at = slice(start, start + TILE)
        key = lax.broadcasted_iota(jnp.int32, (rows, TILE), 0)
        for q_ref, k_ref, v_ref, o_ref, l_ref, g_ref, gq_ref, mask, slot in (
            (cq_ref, sk_ref, sv_ref, co_ref, cl_ref, cg_ref, gcq_ref, None, 0),
            (sq_ref, sk_ref, sv_ref, so_ref, sl_ref, sg_ref, gsq_ref, None, 0),
            (scq_ref, tk_ref, tv_ref, io_ref, il_ref, ig_ref, gscq_ref, key < live_ref[0], 2),
        ):
            grad_out = g_ref[at, :]
            grad_q, grad_k, grad_v = attend_back_tile(
                q_ref[at, :], k_ref[...], v_ref[...], mask, l_ref[0, :, at], grad_out,
                row_delta(o_ref[at, :], grad_out))
            gq_ref[at, :] = (grad_q * RAW_SCALE).T.astype(jnp.bfloat16)
            sums[slot] = sums[slot] + grad_k
            sums[slot + 1] = sums[slot + 1] + grad_v
    gsk_ref[...] = (sums[0] * RAW_SCALE).astype(jnp.bfloat16)
    gsv_ref[...] = sums[1].astype(jnp.bfloat16)
    gtk_ref[...] = sums[2] * RAW_SCALE
    gtv_ref[...] = sums[3]


def self_attention_back(projected, out, log, grad_attended, extra_k, extra_v, window, after=()):
    rows, width = projected.shape
    heads = width // 4 // HD
    extra = extra_k.shape[0]
    return launch(
        partial(self_back_kernel, window), [projected] * 3 + [out, log, grad_attended, extra_k, extra_v],
        after=after, name="self_attention_back", grid=(heads,),
        in_specs=[column(rows, 0), column(rows, 2 * heads), column(rows, 3 * heads), column(rows, 0), stat(rows),
                  column(rows, 0), column(extra, 0), column(extra, 0)],
        out_specs=[column(rows, 0)] * 3, out_shape=[shaped((rows, width // 4))] * 3,
        scratch=[pltpu.VMEM((rows, HD), F32)] * 2,
        flops=heads * 10 * 2304 * 256 * HD, exps=heads * 2304 * 256,
    )


def cross_attention_back(projected, state_side, out, log, grad_attended, block, after=()):
    rows, width = state_side.shape
    heads = width // 4 // HD
    return launch(
        cross_back_kernel, [projected, state_side, state_side, out, log, grad_attended],
        after=after, name="cross_attention_back", grid=(heads,),
        in_specs=[block_column(rows, block, heads), column(rows, 2 * heads), column(rows, 3 * heads),
                  block_column(rows, block, 0), stat(rows), block_column(rows, block, heads)],
        out_specs=[block_column(rows, block, 0), column(rows, 0), column(rows, 0)],
        out_shape=[shaped((projected.shape[0], width // 4))] + [shaped((rows, width // 4))] * 2,
        flops=heads * 10 * rows * rows * HD, exps=heads * rows * rows,
    )


def state_attention_back(projected, state_side, live_keys, cross, inner_self, inner_cross, grad_attended, grad_inner, before, block, after=()):
    rows, width = state_side.shape
    heads = width // 4 // HD
    grad, wide = shaped((rows, width // 4)), shaped((rows, width // 4), F32)
    return launch(
        state_back_kernel,
        [live_keys, projected] + [state_side] * 4 + [projected] * 2
        + [cross[0], inner_self[0], inner_cross[0], cross[1], inner_self[1], inner_cross[1]]
        + [grad_attended, grad_inner, grad_inner, before],
        after=after, name="state_attention_back", grid=(heads,),
        in_specs=[SMEM, block_column(rows, block, heads)] + [column(rows, part * heads) for part in range(4)]
        + [block_column(rows, block, 2 * heads), block_column(rows, block, 3 * heads)]
        + [block_column(rows, block, 0), column(rows, 0), column(rows, 0)] + [stat(rows)] * 3
        + [block_column(rows, block, heads), column(rows, 0), column(rows, heads), pl.BlockSpec(memory_space=pl.ANY)],
        out_specs=[block_column(rows, block, 0)] + [column(rows, 0)] * 6,
        out_shape=[shaped((projected.shape[0], width // 4))] + [grad] * 4 + [wide] * 2,
        aliases={17: 0},
        flops=heads * 30 * rows * rows * HD, exps=3 * heads * rows * rows,
    )


def swap(values, axis):
    if axis == "y":
        return lax.ppermute(values, "fsdp", [(0, 1), (1, 0)])
    bit = {"core": 1, "x": 2, "z_low": 4, "z_high": 8}[axis]
    return lax.ppermute(values, "dp", [(d, d ^ bit) for d in range(16)])


LINES = [[line + 4 * z for z in range(4)] for line in range(4)]


def place():
    dp = lax.axis_index("dp")
    return jnp.stack([(dp // 2) % 2, dp % 2, lax.axis_index("fsdp")]).astype(jnp.int32)


def assemble_kernel(sizes, place_ref, *refs):
    x, core, y = place_ref[0], place_ref[1], place_ref[2]
    pieces, outs = refs[:10], refs[10:]
    cols = pieces[0].shape[-1]

    def put(piece, dx, dy, other):
        line = (x ^ dx) * 2 + (core ^ other)
        at = pl.ds(pl.multiple_of((y ^ dy) * cols, 128), cols)
        row = 0
        for size, out in zip(sizes, outs):
            out[0, line, :, at] = piece[0, row : row + size, :]
            row += size

    for other in range(2):
        put(pieces[5 * other], 0, 0, other)
        put(pieces[5 * other + 1], 1, 0, other)
        put(pieces[5 * other + 2], 0, 1, other)

        @pl.when(pl.program_id(0) < 2)
        def _():
            put(pieces[5 * other + 3], 1, 1, other)

        @pl.when(pl.program_id(0) >= 2)
        def _():
            put(pieces[5 * other + 4], 1, 1, other)


def assemble(pieces, sizes, where, after=()):
    _, rows, cols = pieces[0].shape
    full = pl.BlockSpec((1, rows, cols), lambda z, p: (z, 0, 0))
    low = pl.BlockSpec((1, rows, cols), lambda z, p: (jnp.minimum(z, 1), 0, 0))
    high = pl.BlockSpec((1, rows, cols), lambda z, p: (jnp.maximum(z, 2) - 2, 0, 0))
    outs = launch(
        partial(assemble_kernel, sizes), pieces, where=where, after=after, name="assemble", grid=(4,),
        in_specs=[full, full, full, low, high] * 2,
        out_specs=[pl.BlockSpec((1, 4, size, 2 * cols), lambda z, p: (z, 0, 0, 0)) for size in sizes],
        out_shape=[shaped((4, 4, size, 2 * cols)) for size in sizes],
        flops=0,
    )
    return [out.reshape(-1, 2 * cols) for out in outs]


def gather_pieces(blocks):
    packed = blocks[0] if len(blocks) == 1 else jnp.concatenate(blocks, axis=0)
    line = lax.all_gather(packed, "dp", axis=0, axis_index_groups=LINES)
    over_x, over_y = swap(line, "x"), swap(line, "y")
    near = [line, over_x, over_y, swap(over_x[:2], "y"), swap(over_y[2:], "x")]
    return near + [swap(piece, "core") for piece in near]


def add(*terms):
    return sum(term.astype(F32) for term in terms)


def fold_core_kernel(place_ref, keep_ref, come_ref, low_ref, high_ref, px_ref, py_ref, own_ref):
    x, y = place_ref[0], place_ref[2]
    cols = own_ref.shape[-1]

    def total(z, dx, dy):
        at = pl.ds(pl.multiple_of((y ^ dy) * cols, 128), cols)
        return narrow(add(keep_ref[z, x ^ dx, :, at], come_ref[z, x ^ dx, :, at]))

    for z in range(2):
        own_ref[z] = total(z, 0, 0)
        px_ref[z] = total(z, 1, 0)
        py_ref[z] = total(z, 0, 1)

    @pl.when(pl.program_id(0) == 0)
    def _():
        for z in range(2):
            low_ref[z] = total(z, 1, 1)

    @pl.when(pl.program_id(0) == 1)
    def _():
        for z in range(2):
            high_ref[z] = total(z, 1, 1)


def fold_core(keep, come, where, after=()):
    _, _, rows, cols = keep.shape
    pair = pl.BlockSpec((2, 2, rows, cols), lambda i, p: (i, 0, 0, 0))
    half = pl.BlockSpec((2, rows, cols // 2), lambda i, p: (0, 0, 0))
    full = pl.BlockSpec((2, rows, cols // 2), lambda i, p: (i, 0, 0))
    return launch(
        fold_core_kernel, [keep, come], where=where, after=after, name="fold_core", grid=(2,),
        in_specs=[pair, pair], out_specs=[half, half, full, full, full],
        out_shape=[shaped((2, rows, cols // 2))] * 2 + [shaped((4, rows, cols // 2))] * 3,
        flops=keep.size,
    )


def fold_mid_kernel(px_ref, py_ref, rx_ref, ry_ref, px_out, py_out):
    px_out[...] = narrow(add(px_ref[...], ry_ref[...]))
    py_out[...] = narrow(add(py_ref[...], rx_ref[...]))


def fold_mid(px, py, rx, ry, after=()):
    block = rx.shape
    low = pl.BlockSpec(block, lambda i: (0, 0, 0))
    high = pl.BlockSpec(block, lambda i: (1, 0, 0))
    return launch(
        fold_mid_kernel, [px, py, rx, ry], after=after, name="fold_mid", grid=(1,),
        in_specs=[high, low, low, low], out_specs=[high, low],
        out_shape=[shaped(px.shape), shaped(py.shape)], aliases={0: 0, 1: 1}, flops=px.size,
    )


def fold_last_kernel(own_ref, rx_ref, ry_ref, out_ref):
    out_ref[...] = narrow(add(own_ref[...], rx_ref[...], ry_ref[...]))


def fold_last(own, rx, ry, after=()):
    _, rows, cols = own.shape
    block = pl.BlockSpec((2, rows, cols), lambda i: (i, 0, 0))
    return launch(
        fold_last_kernel, [own, rx, ry], after=after, name="fold_last", grid=(2,),
        in_specs=[block] * 3, out_specs=[block], out_shape=[shaped(own.shape)], flops=2 * own.size,
    )[0]


class Scatter:
    def __init__(self, keep, send, where):
        self.where, self.keep = where, keep
        self.come = swap(send, "core")

    def core(self, after):
        low, high, self.px, self.py, self.own = fold_core(self.keep, self.come, self.where, after)
        self.rx, self.ry = swap(low, "x"), swap(high, "y")
        return self.own

    def mid(self, after):
        px, py = fold_mid(self.px, self.py, self.rx, self.ry, after)
        self.rx, self.ry = swap(px, "x"), swap(py, "y")
        return px

    def last(self, after):
        line = fold_last(self.own, self.rx, self.ry, after)
        rows, cols = line.shape[1:]
        self.out = lax.psum_scatter(
            line.reshape(4 * rows, cols), "dp", scatter_dimension=0, axis_index_groups=LINES, tiled=True
        )
        return line


def paired():
    return lax.axis_size("dp") == 16 and lax.axis_size("fsdp") == 2


def gather_plain(block):
    return lax.all_gather(lax.all_gather(block, "fsdp", axis=1, tiled=True), "dp", axis=0, tiled=True)


def scatter_plain(grad):
    rows = lax.psum_scatter(grad, "dp", scatter_dimension=0, tiled=True)
    return lax.psum_scatter(rows, "fsdp", scatter_dimension=1, tiled=True)


def gather_vectors(vectors):
    if not paired():
        return lax.all_gather(vectors, "fsdp", axis=1, tiled=True).astype(F32)
    other = swap(vectors, "y")
    first = lax.axis_index("fsdp") == 0
    return jnp.concatenate(
        [jnp.where(first, vectors, other), jnp.where(first, other, vectors)], axis=1
    ).astype(F32)


def scatter_vectors(vectors):
    part = vectors.shape[1] // lax.axis_size("fsdp")
    y = lax.axis_index("fsdp")
    if not paired():
        total = lax.psum(vectors, ("dp", "fsdp"))
        return lax.dynamic_slice_in_dim(total, y * part, part, axis=1)
    low, high = vectors[:, :part], vectors[:, part:]
    total = jnp.where(y == 0, low, high) + swap(jnp.where(y == 0, high, low), "y")
    for axis in ("core", "x", "z_low", "z_high"):
        total = total + swap(total, axis)
    return total


def shards(
    tokens,
    incoming,
    document_lengths,
    output_grad,
    token_proj,
    state_proj,
    token_out,
    state_out,
    gate_weight,
    init_state,
    hidden_in,
    hidden_out,
    token_gain,
    state_gain,
    hidden_gain,
    gate_bias,
):
    seg_len, width = tokens.shape
    window = WINDOW
    states = incoming.shape[1]
    where = place()
    segment_id = lax.axis_index(("dp", "fsdp"))
    counts = (document_lengths + seg_len - 1) // seg_len
    ends = jnp.cumsum(counts)
    starts = ends - counts
    inside = (segment_id >= starts) & (segment_id < ends)
    valid_len = jnp.sum(
        jnp.where(
            inside, jnp.minimum(seg_len, document_lengths - (segment_id - starts) * seg_len), 0
        )
    )
    first = jnp.any(segment_id == starts)
    lives = [jnp.where(b * window < valid_len, 1.0, 0.0).astype(F32).reshape(1) for b in range(2)]
    live_keys = [jnp.clip(valid_len - b * window, 0, window).astype(jnp.int32).reshape(1) for b in range(2)]

    gains = gather_vectors(jnp.stack([token_gain, state_gain, hidden_gain, gate_bias]))
    token_gain_f, state_gain_f, hidden_gain_f, gate_bias_f = [gains[i : i + 1] for i in range(4)]
    order = ()

    if paired():
        packed_init = jnp.pad(init_state.reshape(8, 2048), ((0, 8), (0, 0)))
        pieces = [
            gather_pieces(blocks)
            for blocks in (
                [state_proj, packed_init],
                [token_proj],
                [state_out, gate_weight, token_out],
                [hidden_in],
                [hidden_out],
            )
        ]
        full_state_proj, full_init = assemble(pieces[0], [64, 16], where)
        full_init = full_init.reshape(16, 16, 2, 4, 512)[:, :8].transpose(0, 1, 3, 2, 4).reshape(states, width)
    else:
        full_state_proj, full_token_proj, full_state_out, full_gate_weight, full_token_out, full_init = [
            gather_plain(w) for w in (state_proj, token_proj, state_out, gate_weight, token_out, init_state)
        ]
        full_hidden_in, full_hidden_out = gather_plain(hidden_in), gather_plain(hidden_out)
    state_0 = jnp.where(first, full_init, incoming[0]).astype(F32)
    normed_0, side_0 = norm_project(state_0, state_gain_f, full_state_proj, order)
    order = (side_0,)
    if paired():
        (full_token_proj,) = assemble(pieces[1], [64], where, order)
    normed, projected = norm_project(tokens, token_gain_f, full_token_proj, order)
    order = (projected,)
    inner_self_0, inner_cross_0, inner_self_log, inner_cross_log = inner_attention(
        projected, side_0, live_keys[0], 0, order
    )
    order = (inner_self_log,)
    cross_out, cross_log_0 = cross_attention(projected, side_0, 0, None, order)
    order = (cross_log_0,)
    self_out, self_log = self_attention(projected, window, order)
    order = (self_log,)
    if paired():
        full_state_out, full_gate_weight, full_token_out = assemble(pieces[2], [128, 64, 128], where, order)
        order = (full_gate_weight,)
    mixed_0, gate_0, state_1 = update_state(
        lives[0], inner_self_0, inner_cross_0, full_state_out, full_gate_weight, gate_bias_f, state_0, order
    )
    order = (mixed_0,)
    normed_1, side_1 = norm_project(state_1, state_gain_f, full_state_proj, order)
    order = (normed_1,)
    cross_out, cross_log_1 = cross_attention(projected, side_1, 1, cross_out, order)
    order = (cross_log_1,)
    middle, hidden_normed = branch(self_out, cross_out, full_token_out, tokens, hidden_gain_f, order)
    order = (hidden_normed,)
    if paired():
        (full_hidden_in,) = assemble(pieces[3], [64], where, order)
    active, slope = hidden(hidden_normed, full_hidden_in, order)
    order = (active,)

    scatters = {}

    def weight(name, lefts, rights, plan, split=False):
        nonlocal order
        if paired():
            keep, send = weight_grad(lefts, rights, plan, where, "grad_" + name, split, order)
            scatters[name] = Scatter(keep, send, where)
            order = (keep,)
            return
        if split:
            lefts = [jnp.concatenate(lefts, axis=1)]
        grad = jnp.concatenate(
            [sum(matmul_left_t(lefts[a], rights[b]) for a, b in terms) for terms in plan], axis=1
        )
        scatters[name] = scatter_plain(narrow(grad))

    def fold(name, step):
        nonlocal order
        if paired():
            order = (getattr(scatters[name], step)(order),)

    weight("hidden_out", [active], [output_grad], [[(0, 0)]])
    if paired():
        (full_hidden_out,) = assemble(pieces[4], [256], where, order)
        order = (full_hidden_out,)
    fold("hidden_out", "core")
    result, grad_pre = result_and_pre(active, slope, full_hidden_out, middle, output_grad, order)
    order = (result,)
    fold("hidden_out", "mid")
    weight("hidden_in", [hidden_normed], [grad_pre], [[(0, 0)]])
    grad_hidden_gain, grad_branch, grad_middle = norm_back_project(
        [grad_pre], full_hidden_in, middle, hidden_gain_f, output_grad, "hidden_back", True, after=order
    )
    order = (grad_hidden_gain,)
    fold("hidden_in", "core")
    fold("hidden_out", "last")
    grad_attended = spread(grad_branch, full_token_out, order)
    order = (grad_attended,)
    grad_cross, grad_keys_1, grad_values_1 = cross_attention_back(
        projected, side_1, cross_out, cross_log_1, grad_attended, 1, order
    )
    order = (grad_keys_1,)
    fold("hidden_in", "mid")
    no_term = jnp.zeros((states, width), jnp.bfloat16)
    grad_state_gain_1, _, grad_state_1 = norm_back_project(
        [grad_keys_1, grad_values_1], full_state_proj, state_1, state_gain_f, no_term, "side_back", True,
        offset=2 * width, after=order,
    )
    order = (grad_state_gain_1,)
    grad_gate_low, grad_mixed, grad_inner, grad_direct, grad_gate_bias = gate_back(
        lives[0], grad_state_1, gate_0, state_0, mixed_0, full_gate_weight, full_state_out, order
    )
    order = (grad_gate_bias,)
    weight_pairs = [[(0, 0)]]
    weight("token_out", [self_out, cross_out], [grad_branch], weight_pairs, True)
    fold("hidden_in", "last")
    parts = state_attention_back(
        projected, side_0, live_keys[0], (cross_out, cross_log_0), (inner_self_0, inner_self_log),
        (inner_cross_0, inner_cross_log), grad_attended, grad_inner, grad_cross, 0, order,
    )
    grad_cross, grads_side_0, extra_keys, extra_values = parts[0], parts[1:5], parts[5], parts[6]
    order = (extra_keys,)
    fold("token_out", "core")
    weight("state_out", [inner_self_0, inner_cross_0], [grad_mixed], weight_pairs, True)
    weight("gate_weight", [mixed_0], [grad_gate_low], weight_pairs)
    fold("token_out", "mid")
    weight(
        "state_proj", [normed_0, normed_1], [*grads_side_0, grad_keys_1, grad_values_1],
        [[(0, 0)], [(0, 1)], [(0, 2), (1, 4)], [(0, 3), (1, 5)]],
    )
    fold("state_out", "core")
    fold("gate_weight", "core")
    grad_state_gain_0, grad_init = norm_back_project(
        grads_side_0, full_state_proj, state_0, state_gain_f, grad_direct, "state_back",
        scale=jnp.where(first, 1.0, 0.0).astype(F32).reshape(1), after=order,
    )
    order = (grad_state_gain_0,)
    fold("token_out", "last")
    fold("state_proj", "core")
    grad_self, grad_keys, grad_values = self_attention_back(
        projected, self_out, self_log, grad_attended, extra_keys, extra_values, window, order
    )
    order = (grad_self,)
    fold("state_out", "mid")
    fold("gate_weight", "mid")
    fold("state_proj", "mid")
    grads_projected = [grad_self, grad_cross, grad_keys, grad_values]
    weight("token_proj", [normed], grads_projected, [[(0, i)] for i in range(4)])
    fold("state_out", "last")
    fold("gate_weight", "last")
    if paired():
        parts = grad_init.reshape(4, 2, 2, 32, width)
        keep = lax.dynamic_index_in_dim(parts, where[1], 2, keepdims=False)
        send = lax.dynamic_index_in_dim(parts, 1 - where[1], 2, keepdims=False)
        scatters["init"] = Scatter(keep, send, where)
    else:
        scatters["init"] = scatter_plain(grad_init)
    grad_token_gain, tokens_grad = norm_back_project(
        grads_projected, full_token_proj, tokens, token_gain_f, grad_middle, "tokens_back", after=order
    )
    order = (grad_token_gain,)
    fold("token_proj", "core")
    fold("init", "core")
    fold("state_proj", "last")
    inner_self_1, inner_cross_1, log, _ = inner_attention(projected, side_1, live_keys[1], 1, order)
    order = (log,)
    fold("token_proj", "mid")
    fold("init", "mid")
    _, _, state_2 = update_state(
        lives[1], inner_self_1, inner_cross_1, full_state_out, full_gate_weight, gate_bias_f, state_1, order
    )
    order = (state_2,)
    fold("init", "last")
    fold("token_proj", "last")
    vector_grads = scatter_vectors(
        jnp.concatenate(
            [grad_token_gain, grad_state_gain_0 + grad_state_gain_1, grad_hidden_gain, grad_gate_bias], axis=0
        )
    )
    matrix_grads = [
        (scatters[name].out if paired() else scatters[name]).astype(F32)
        for name in (
            "token_proj", "state_proj", "token_out", "state_out", "gate_weight", "init", "hidden_in", "hidden_out",
        )
    ]
    return (
        result,
        narrow(state_2)[None],
        tokens_grad,
        *matrix_grads,
        *[vector_grads[i] for i in range(4)],
    )


def solution(mesh):
    return jax.shard_map(
        shards,
        mesh=mesh,
        in_specs=(
            P(("dp", "fsdp"), None),
            P(("dp", "fsdp"), None, None),
            P(),
            P(("dp", "fsdp"), None),
            P("dp", "fsdp"),
            P("dp", "fsdp"),
            P("dp", "fsdp"),
            P("dp", "fsdp"),
            P("dp", "fsdp"),
            P("dp", "fsdp"),
            P("dp", "fsdp"),
            P("dp", "fsdp"),
            P("fsdp"),
            P("fsdp"),
            P("fsdp"),
            P("fsdp"),
        ),
        out_specs=(
            P(("dp", "fsdp"), None),
            P(("dp", "fsdp"), None, None),
            P(("dp", "fsdp"), None),
            P("dp", "fsdp"),
            P("dp", "fsdp"),
            P("dp", "fsdp"),
            P("dp", "fsdp"),
            P("dp", "fsdp"),
            P("dp", "fsdp"),
            P("dp", "fsdp"),
            P("dp", "fsdp"),
            P("fsdp"),
            P("fsdp"),
            P("fsdp"),
            P("fsdp"),
        ),
        check_vma=False,
    )
```

```python
from functools import partial
import math

import jax
import jax.numpy as jnp
from jax import lax
from jax.experimental import pallas as pl
from jax.experimental.pallas import tpu as pltpu
from jax.sharding import PartitionSpec as P

HD = 128
WINDOW = 512
MIB = 1 << 20


norm_eps = 1e-06
masked_score = -1e30
EXP_SCALE = math.log2(math.e) / math.sqrt(HD)
RAW_SCALE = 1.0 / math.sqrt(HD)
NT = (((1,), (1,)), ((), ()))
TN = (((0,), (0,)), ((), ()))
NN = (((1,), (0,)), ((), ()))


def narrow(values):
    return values.astype(jnp.bfloat16)


def matmul_left_t(left, right):
    return lax.dot_general(left, right, TN, preferred_element_type=jnp.float32)


def launch(body, operands, *, grid, in_specs, out_specs, out_shape, name, flops, after=(), where=None, scratch=(), aliases=None, exps=0, limit=48):
    count = len(operands)
    late = len(after)
    lead = 0 if where is None else 1

    def run(*refs):
        body(*refs[: lead + count], *refs[lead + count + late :])

    specs = list(in_specs) + [pl.BlockSpec(memory_space=pl.ANY)] * late
    size = sum(math.prod(item.shape) * item.dtype.itemsize for item in (*operands, *out_shape))
    kwargs = dict(grid=grid, in_specs=specs, out_specs=list(out_specs))
    if where is None:
        kwargs["scratch_shapes"] = list(scratch)
    else:
        kwargs = dict(
            grid_spec=pltpu.PrefetchScalarGridSpec(
                num_scalar_prefetch=1, scratch_shapes=list(scratch), **kwargs
            )
        )
    return pl.pallas_call(
        run,
        out_shape=list(out_shape),
        input_output_aliases=aliases or {},
        compiler_params=pltpu.CompilerParams(vmem_limit_bytes=limit * MIB),
        cost_estimate=pl.CostEstimate(flops=int(flops), bytes_accessed=int(size), transcendentals=int(exps)),
        name=name,
        **kwargs,
    )(*(() if where is None else (where,)), *operands, *after)


def shaped(shape, dtype=jnp.bfloat16):
    return jax.ShapeDtypeStruct(shape, dtype)


def whole(shape):
    return pl.BlockSpec(shape, lambda *ids: (0,) * len(shape))


SMEM = pl.BlockSpec(memory_space=pltpu.SMEM)
F32 = jnp.float32


def norm_rows(values):
    centered = values - jnp.mean(values, axis=-1, keepdims=True)
    return centered, lax.rsqrt(jnp.mean(centered * centered, axis=-1, keepdims=True) + norm_eps)


def norm_back_rows(values, gain, grad):
    centered, inverse = norm_rows(values)
    normal = centered * inverse
    scaled = grad * gain
    mean = jnp.mean(scaled, axis=-1, keepdims=True)
    along = jnp.mean(scaled * normal, axis=-1, keepdims=True)
    return inverse * (scaled - mean - normal * along), jnp.sum(grad * normal, axis=0, keepdims=True)


ROWS = 128
COLS = 512


def group_spec(weight, group):
    array, start, rows = weight
    groups = 4

    def place_of(*ids):
        which = group(ids[0])
        return 0, which // groups, start // rows + which % groups, 0

    return pl.BlockSpec((16, 1, rows, COLS), place_of)


def rows_spec(weight, count, step=lambda i: i):
    array, start, rows = weight
    return pl.BlockSpec((count, 2, rows, COLS), lambda *ids: (step(ids[0]), 0, start // rows, 0))


def side(w_ref, y, blocks=slice(None)):
    values = w_ref[blocks, y]
    return values.reshape(-1, COLS)


def times(left, w_ref, blocks=slice(None)):
    return jnp.concatenate([dot(left, side(w_ref, y, blocks), NN) for y in range(2)], axis=1)


def times_turned(left, w_ref):
    return sum(dot(left[:, y * COLS : (y + 1) * COLS], side(w_ref, y), NT) for y in range(2))


def norm_project_kernel(x_ref, gain_ref, w_ref, normed_ref, out_ref):
    @pl.when(pl.program_id(0) == 0)
    def _():
        @pl.loop(0, x_ref.shape[0] // ROWS)
        def _(i):
            at = pl.ds(pl.multiple_of(i * ROWS, ROWS), ROWS)
            centered, inverse = norm_rows(x_ref[at, :].astype(F32))
            normed_ref[at, :] = narrow(centered * inverse * gain_ref[...])

    out_ref[...] = narrow(dot(normed_ref[...], side(w_ref, 0), NN))


def norm_project(x, gain, weight, after=()):
    rows, width = x.shape
    cols = 4 * width
    step = COLS
    return launch(
        norm_project_kernel, [x, gain, weight[0]], after=after, name="norm_project", grid=(cols // step,),
        in_specs=[whole((rows, width)), whole((1, width)), group_spec(weight, lambda i: i)],
        out_specs=[whole((rows, width)), pl.BlockSpec((rows, step), lambda i: (0, i))],
        out_shape=[shaped((rows, width)), shaped((rows, cols))],
        flops=2 * rows * width * cols,
    )


def update_kernel(live_ref, self_ref, cross_ref, out_w_ref, gate_w_ref, bias_ref, state_ref, mixed_ref, gate_ref, new_ref):
    low, high = slice(0, 8), slice(8, 16)
    mixed = narrow(times(self_ref[...], out_w_ref, low) + times(cross_ref[...], out_w_ref, high))
    mixed_ref[...] = mixed
    gate = jax.nn.sigmoid(times(mixed, gate_w_ref) + bias_ref[...])
    gate_ref[...] = gate
    state = state_ref[...]
    updated = gate * state + (1.0 - gate) * jnp.tanh(mixed.astype(F32))
    new_ref[...] = state + live_ref[0] * (updated - state)


def update_state(live, inner_self, inner_cross, state_out, gate_weight, bias, state, after=()):
    rows, width = state.shape
    step = 256
    tile = pl.BlockSpec((step, width), lambda i: (i, 0))
    return launch(
        update_kernel, [live, inner_self, inner_cross, state_out[0], gate_weight[0], bias, state],
        after=after, name="update_state", grid=(rows // step,),
        in_specs=[SMEM, tile, tile, rows_spec(state_out, 16, lambda i: 0), rows_spec(gate_weight, 16, lambda i: 0), whole((1, width)), tile],
        out_specs=[tile, tile, tile],
        out_shape=[shaped((rows, width)), shaped((rows, width), F32), shaped((rows, width), F32)],
        flops=6 * rows * width * width, exps=2 * rows * width,
    )


def branch_kernel(self_ref, cross_ref, w_ref, x_ref, gain_ref, middle_ref, normed_ref):
    low, high = slice(0, 8), slice(8, 16)
    middle = x_ref[...].astype(F32) + (times(self_ref[...], w_ref, low) + times(cross_ref[...], w_ref, high))
    middle_ref[...] = middle
    centered, inverse = norm_rows(middle)
    normed_ref[...] = narrow(centered * inverse * gain_ref[...])


def branch(self_out, cross_out, token_out, x, gain, after=()):
    rows, width = x.shape
    step = 256
    tile = pl.BlockSpec((step, width), lambda i: (i, 0))
    return launch(
        branch_kernel, [self_out, cross_out, token_out[0], x, gain], after=after, name="branch", grid=(rows // step,),
        in_specs=[tile, tile, rows_spec(token_out, 16, lambda i: 0), tile, whole((1, width))],
        out_specs=[tile, tile],
        out_shape=[shaped((rows, width), F32), shaped((rows, width))],
        flops=4 * rows * width * width,
    )


GELU_A = math.sqrt(2.0 / math.pi)
GELU_B = 0.044715


def hidden_kernel(normed_ref, w_ref, active_ref, slope_ref):
    for start in range(0, normed_ref.shape[0], 256):
        at = slice(start, start + 256)
        v = dot(normed_ref[at, :], side(w_ref, 0), NN)
        square = v * v
        t = jnp.tanh(v * (GELU_A + (GELU_A * GELU_B) * square))
        half = 0.5 + 0.5 * t
        active_ref[at, :] = narrow(v * half)
        slope = half + v * (1.0 - t * t) * (0.5 * GELU_A + (1.5 * GELU_A * GELU_B) * square)
        slope_ref[at, :] = narrow(slope)


def hidden(normed, weight, after=()):
    rows, width = normed.shape
    cols = 4 * width
    step = COLS
    tile = pl.BlockSpec((rows, step), lambda i: (0, i))
    return launch(
        hidden_kernel, [normed, weight[0]], after=after, name="hidden", grid=(cols // step,),
        in_specs=[whole((rows, width)), group_spec(weight, lambda i: i)],
        out_specs=[tile, tile], out_shape=[shaped((rows, cols))] * 2,
        flops=2 * rows * width * cols, exps=rows * cols,
    )


def result_kernel(active_ref, slope_ref, w_ref, middle_ref, grad_ref, result_ref, pre_ref, total_ref):
    first = pl.program_id(0) == 0
    for start in range(0, active_ref.shape[0], 256):
        at = slice(start, start + 256)
        pre_ref[at, :] = narrow(times_turned(grad_ref[at, :], w_ref) * slope_ref[at, :].astype(F32))
        total_ref[at, :] = jnp.where(first, middle_ref[at, :], total_ref[at, :]) + times(active_ref[at, :], w_ref)

    @pl.when(pl.program_id(0) == pl.num_programs(0) - 1)
    def _():
        result_ref[...] = narrow(total_ref[...])


def result_and_pre(active, slope, weight, middle, grad, after=()):
    rows, hidden_units = active.shape
    width = middle.shape[1]
    step = 512
    tile = pl.BlockSpec((rows, step), lambda i: (0, i))
    return launch(
        result_kernel, [active, slope, weight[0], middle, grad], after=after, name="result_and_pre",
        grid=(hidden_units // step,),
        in_specs=[tile, tile, rows_spec(weight, step // weight[2]), whole((rows, width)), whole((rows, width))],
        out_specs=[whole((rows, width)), tile],
        out_shape=[shaped((rows, width)), shaped((rows, hidden_units))],
        scratch=[pltpu.VMEM((rows, width), F32)],
        flops=4 * rows * width * hidden_units,
    )


def norm_back_kernel(parts, keep_wide, scale_ref, *refs):
    grads, (w_ref, x_ref, gain_ref, plus_ref) = refs[:parts], refs[parts : parts + 4]
    outs, total_ref = refs[parts + 4 : -1], refs[-1]
    i = pl.program_id(0)
    share = pl.num_programs(0) // parts

    @pl.when(i == 0)
    def _():
        total_ref[...] = jnp.zeros_like(total_ref)

    for part in range(parts):
        @pl.when(i // share == part)
        def _():
            total_ref[...] += dot(grads[part][...], side(w_ref, 0), NT)

    @pl.when(i == pl.num_programs(0) - 1)
    def _():
        outs[0][...] = jnp.zeros_like(outs[0])

        @pl.loop(0, x_ref.shape[0] // ROWS)
        def _(j):
            at = pl.ds(pl.multiple_of(j * ROWS, ROWS), ROWS)
            grad, gain_grad = norm_back_rows(x_ref[at, :].astype(F32), gain_ref[...], total_ref[at, :])
            grad = grad + plus_ref[at, :].astype(F32)
            outs[0][...] += gain_grad
            outs[1][at, :] = narrow(jnp.where(scale_ref[0] > 0.0, grad, 0.0))
            if keep_wide:
                outs[2][at, :] = grad


def norm_back_project(grads, weight, x, gain, plus, name, keep_wide=False, offset=0, scale=None, after=()):
    rows, width = x.shape
    step = 512
    share = grads[0].shape[1] // step
    parts = len(grads)
    steps = parts * share
    def part_spec(part):
        return pl.BlockSpec((rows, step), lambda i: (0, jnp.clip(i - part * share, 0, share - 1)))
    out_shape = [shaped((1, width), F32), shaped((rows, width))]
    if keep_wide:
        out_shape.append(shaped((rows, width), F32))
    if scale is None:
        scale = jnp.ones((1,), F32)
    return launch(
        partial(norm_back_kernel, parts, keep_wide), [scale, *grads, weight[0], x, gain, plus], after=after, name=name,
        grid=(steps,),
        in_specs=[SMEM] + [part_spec(part) for part in range(parts)]
        + [group_spec(weight, lambda i: i + offset // step), whole((rows, width)), whole((1, width)), whole((rows, width))],
        out_specs=[whole(item.shape) for item in out_shape], out_shape=out_shape,
        scratch=[pltpu.VMEM((rows, width), F32)],
        flops=2 * rows * width * steps * step,
    )


def spread_kernel(grad_ref, w_ref, out_ref):
    out_ref[...] = narrow(times_turned(grad_ref[...], w_ref))


def spread(grad, weight, after=()):
    rows, width = grad.shape
    cols = 16 * weight[2]
    step = 512
    return launch(
        spread_kernel, [grad, weight[0]], after=after, name="spread", grid=(cols // step,),
        in_specs=[whole((rows, width)), rows_spec(weight, step // weight[2])],
        out_specs=[pl.BlockSpec((rows, step), lambda i: (0, i))],
        out_shape=[shaped((rows, cols))], flops=2 * rows * width * cols,
    )[0]


def gate_back_kernel(live_ref, grad_ref, gate_ref, state_ref, mixed_ref, gate_w_ref, out_w_ref,
                     pre_ref, grad_mixed_ref, inner_ref, direct_ref, bias_ref):
    grad, gate, live = grad_ref[...], gate_ref[...], live_ref[0]
    tanh_mixed = jnp.tanh(mixed_ref[...].astype(F32))
    updated = live * grad
    direct_ref[...] = (1.0 - live) * grad + updated * gate
    pre = gate * (1.0 - gate) * updated * (state_ref[...] - tanh_mixed)

    @pl.when(pl.program_id(0) == 0)
    def _():
        bias_ref[...] = jnp.zeros_like(bias_ref)

    bias_ref[...] += jnp.sum(pre, axis=0, keepdims=True)
    low = narrow(pre)
    pre_ref[...] = low
    grad_mixed = narrow(
        times_turned(low, gate_w_ref) + updated * (1.0 - gate) * (1.0 - tanh_mixed * tanh_mixed)
    )
    grad_mixed_ref[...] = grad_mixed
    inner_ref[...] = narrow(times_turned(grad_mixed, out_w_ref))


def gate_back(live, grad, gate, state, mixed, gate_weight, state_out, after=()):
    rows, width = grad.shape
    step = 256
    tile = pl.BlockSpec((step, width), lambda i: (i, 0))
    wide = pl.BlockSpec((step, 2 * width), lambda i: (i, 0))
    return launch(
        gate_back_kernel, [live, grad, gate, state, mixed, gate_weight[0], state_out[0]], after=after, name="gate_back",
        grid=(rows // step,),
        in_specs=[SMEM, tile, tile, tile, tile, rows_spec(gate_weight, 16, lambda i: 0), rows_spec(state_out, 16, lambda i: 0)],
        out_specs=[tile, tile, wide, tile, whole((1, width))],
        out_shape=[shaped((rows, width)), shaped((rows, width)), shaped((rows, 2 * width)), shaped((rows, width), F32), shaped((1, width), F32)],
        flops=6 * rows * width * width, exps=rows * width,
    )


def weight_grad_kernel(rows, plan, split, counts, place_ref, *refs):
    lefts, rights = refs[: counts[0]], refs[counts[0] : counts[0] + counts[1]]
    keep_ref, send_ref = refs[-2], refs[-1]
    core = place_ref[1]

    def run(which):
        turned = [lefts[item][...].T for item in which]
        col = 0
        for terms in plan:
            cols = rights[terms[0][1]].shape[1]
            for start in range(0, cols, 512):
                total = sum(
                    dot(turned[left], rights[right][:, start : start + 512], NN) for left, right in terms
                )
                total = narrow(total)
                at = slice(col + start, col + start + 512)
                for x in range(2):
                    even = total[2 * x * rows : (2 * x + 1) * rows]
                    odd = total[(2 * x + 1) * rows : (2 * x + 2) * rows]
                    keep_ref[0, x, :, at] = jnp.where(core == 0, even, odd)
                    send_ref[0, x, :, at] = jnp.where(core == 0, odd, even)
            col += cols

    if split:
        @pl.when(pl.program_id(0) < 2)
        def _():
            run([0])

        @pl.when(pl.program_id(0) >= 2)
        def _():
            run([1])
    else:
        run(range(len(lefts)))


def weight_grad(lefts, rights, plan, where, name, split=False, after=()):
    tokens = lefts[0].shape[0]
    total_rows = lefts[0].shape[1] * (len(lefts) if split else 1)
    rows = total_rows // 16
    cols = sum(rights[terms[0][1]].shape[1] for terms in plan)
    if split:
        left_specs = [
            pl.BlockSpec((tokens, 4 * rows), lambda z, p: (0, jnp.minimum(z, 1))),
            pl.BlockSpec((tokens, 4 * rows), lambda z, p: (0, jnp.maximum(z, 2) - 2)),
        ]
    else:
        left_specs = [pl.BlockSpec((item.shape[0], 4 * rows), lambda z, p: (0, z)) for item in lefts]
    out = pl.BlockSpec((1, 2, rows, cols), lambda z, p: (z, 0, 0, 0))
    return launch(
        partial(weight_grad_kernel, rows, plan, split, (len(lefts), len(rights))), [*lefts, *rights],
        where=where, after=after, name=name, grid=(4,),
        in_specs=left_specs + [whole(item.shape) for item in rights],
        out_specs=[out, out], out_shape=[shaped((4, 2, rows, cols))] * 2,
        flops=2 * tokens * total_rows * cols, limit=56,
    )


def dot(a, b, dims):
    return lax.dot_general(a, b, dims, preferred_element_type=jnp.float32)


def attend_tile(q, k, v, mask):
    scores = dot(k, q, NT)
    if mask is not None:
        scores = jnp.where(mask, scores, masked_score)
    top = jnp.max(scores, axis=0, keepdims=True)
    weights = jnp.exp2((scores - top) * EXP_SCALE)
    total = jnp.sum(weights, axis=0, keepdims=True)
    mixed = dot(v, weights.astype(jnp.bfloat16), TN) / total
    return mixed.T.astype(jnp.bfloat16), top * EXP_SCALE + jnp.log2(total)


def attend_back_tile(q, k, v, mask, log_total, grad_out, delta):
    probs = jnp.exp2(dot(k, q, NT) * EXP_SCALE - log_total)
    if mask is not None:
        probs = jnp.where(mask, probs, 0.0)
    grad_probs = dot(v, grad_out, NT)
    grad_raw = (probs * (grad_probs - delta)).astype(jnp.bfloat16)
    grad_v = dot(probs.astype(jnp.bfloat16), grad_out, NN)
    grad_k = dot(grad_raw, q, NN)
    grad_q = dot(k, grad_raw, TN)
    return grad_q, grad_k, grad_v


def row_delta(out, grad_out):
    both = out.astype(jnp.float32) * grad_out.astype(jnp.float32)
    return jnp.sum(both.T, axis=0, keepdims=True)


def band_mask(rows, cols, key_start, query_start, window):
    key = lax.broadcasted_iota(jnp.int32, (rows, cols), 0) + key_start
    query = lax.broadcasted_iota(jnp.int32, (rows, cols), 1) + query_start
    return (key <= query) & (key > query - window)


TILE = 256


def self_kernel(window, q_ref, k_ref, v_ref, out_ref, log_ref):
    rows = q_ref.shape[0]
    for start in range(0, rows, TILE):
        low = max(0, start - window)
        size = start + TILE - low
        mask = band_mask(size, TILE, low, start, window)
        out, log = attend_tile(
            q_ref[start : start + TILE, :], k_ref[low : low + size, :], v_ref[low : low + size, :], mask
        )
        out_ref[start : start + TILE, :] = out
        log_ref[0, :, start : start + TILE] = log


def column(rows, offset):
    return pl.BlockSpec((rows, HD), lambda h: (0, h + offset))


def stat(rows):
    return pl.BlockSpec((1, 1, rows), lambda h: (h, 0, 0))


def self_attention(projected, window, after=()):
    rows, width = projected.shape
    heads = width // 4 // HD
    return launch(
        partial(self_kernel, window), [projected] * 3, after=after, name="self_attention", grid=(heads,),
        in_specs=[column(rows, 0), column(rows, 2 * heads), column(rows, 3 * heads)],
        out_specs=[column(rows, 0), stat(rows)],
        out_shape=[shaped((rows, width // 4)), shaped((heads, 1, rows), F32)],
        flops=heads * 4 * 2304 * 256 * HD, exps=heads * 2304 * 256,
    )


def block_column(rows, block, offset):
    return pl.BlockSpec((rows, HD), lambda h: (block, h + offset))


def cross_kernel(q_ref, k_ref, v_ref, *refs):
    out_ref, log_ref = refs[-2:]
    for start in range(0, q_ref.shape[0], TILE):
        at = slice(start, start + TILE)
        out_ref[at, :], log_ref[0, :, at] = attend_tile(q_ref[at, :], k_ref[...], v_ref[...], None)


def cross_attention(projected, state_side, block, before=None, after=()):
    rows, width = state_side.shape
    heads = width // 4 // HD
    operands = [projected, state_side, state_side]
    specs = [block_column(rows, block, heads), column(rows, 2 * heads), column(rows, 3 * heads)]
    if before is not None:
        operands.append(before)
        specs.append(pl.BlockSpec(memory_space=pl.ANY))
    return launch(
        cross_kernel, operands, after=after, name="cross_attention", grid=(heads,), in_specs=specs,
        out_specs=[block_column(rows, block, 0), stat(rows)],
        out_shape=[shaped((projected.shape[0], width // 4)), shaped((heads, 1, rows), F32)],
        aliases=None if before is None else {3: 0},
        flops=heads * 4 * rows * rows * HD, exps=heads * rows * rows,
    )


def inner_kernel(live_ref, sq_ref, scq_ref, sk_ref, sv_ref, tk_ref, tv_ref, self_ref, cross_ref, self_log, cross_log):
    rows = sq_ref.shape[0]
    for start in range(0, rows, TILE):
        at = slice(start, start + TILE)
        self_ref[at, :], self_log[0, :, at] = attend_tile(sq_ref[at, :], sk_ref[...], sv_ref[...], None)
        key = lax.broadcasted_iota(jnp.int32, (rows, TILE), 0)
        cross_ref[at, :], cross_log[0, :, at] = attend_tile(
            scq_ref[at, :], tk_ref[...], tv_ref[...], key < live_ref[0]
        )


def inner_attention(projected, state_side, live_keys, block, after=()):
    rows, width = state_side.shape
    heads = width // 4 // HD
    return launch(
        inner_kernel, [live_keys] + [state_side] * 4 + [projected] * 2, after=after, name="inner_attention", grid=(heads,),
        in_specs=[SMEM] + [column(rows, part * heads) for part in range(4)]
        + [block_column(rows, block, 2 * heads), block_column(rows, block, 3 * heads)],
        out_specs=[column(rows, 0)] * 2 + [stat(rows)] * 2,
        out_shape=[shaped((rows, width // 4))] * 2 + [shaped((heads, 1, rows), F32)] * 2,
        flops=heads * 8 * rows * rows * HD, exps=2 * heads * rows * rows,
    )


def self_back_kernel(window, q_ref, k_ref, v_ref, out_ref, log_ref, grad_ref, ek_ref, ev_ref, gq_ref, gk_ref, gv_ref, sk_ref, sv_ref):
    rows = q_ref.shape[0]
    extra = ek_ref.shape[0]
    sk_ref[...] = jnp.zeros_like(sk_ref)
    sv_ref[:extra, :] = ev_ref[...]
    sv_ref[extra:, :] = jnp.zeros((rows - extra, HD), jnp.float32)
    for start in range(0, rows, TILE):
        at = slice(start, start + TILE)
        low = max(0, start - window)
        size = start + TILE - low
        keys = slice(low, low + size)
        mask = band_mask(size, TILE, low, start, window)
        grad_out = grad_ref[at, :]
        grad_q, grad_k, grad_v = attend_back_tile(
            q_ref[at, :], k_ref[keys, :], v_ref[keys, :], mask, log_ref[0, :, at], grad_out,
            row_delta(out_ref[at, :], grad_out))
        gq_ref[at, :] = (grad_q * RAW_SCALE).T.astype(jnp.bfloat16)
        sk_ref[keys, :] += grad_k
        sv_ref[keys, :] += grad_v
    gk_ref[:extra, :] = (sk_ref[:extra, :] * RAW_SCALE + ek_ref[...]).astype(jnp.bfloat16)
    gk_ref[extra:, :] = (sk_ref[extra:, :] * RAW_SCALE).astype(jnp.bfloat16)
    gv_ref[...] = sv_ref[...].astype(jnp.bfloat16)


def cross_back_kernel(cq_ref, sk_ref, sv_ref, out_ref, log_ref, grad_ref, gq_ref, gk_ref, gv_ref):
    rows = cq_ref.shape[0]
    total_k = total_v = 0.0
    for start in range(0, rows, TILE):
        at = slice(start, start + TILE)
        grad_out = grad_ref[at, :]
        grad_q, grad_k, grad_v = attend_back_tile(
            cq_ref[at, :], sk_ref[...], sv_ref[...], None, log_ref[0, :, at], grad_out,
            row_delta(out_ref[at, :], grad_out))
        gq_ref[at, :] = (grad_q * RAW_SCALE).T.astype(jnp.bfloat16)
        total_k = total_k + grad_k
        total_v = total_v + grad_v
    gk_ref[...] = (total_k * RAW_SCALE).astype(jnp.bfloat16)
    gv_ref[...] = total_v.astype(jnp.bfloat16)


def state_back_kernel(live_ref, cq_ref, sq_ref, scq_ref, sk_ref, sv_ref, tk_ref, tv_ref,
                      co_ref, so_ref, io_ref, cl_ref, sl_ref, il_ref, cg_ref, sg_ref, ig_ref, before_ref,
                      gcq_ref, gsq_ref, gscq_ref, gsk_ref, gsv_ref, gtk_ref, gtv_ref):
    rows = cq_ref.shape[0]
    sums = [0.0] * 4
    for start in range(0, rows, TILE):
        at = slice(start, start + TILE)
        key = lax.broadcasted_iota(jnp.int32, (rows, TILE), 0)
        for q_ref, k_ref, v_ref, o_ref, l_ref, g_ref, gq_ref, mask, slot in (
            (cq_ref, sk_ref, sv_ref, co_ref, cl_ref, cg_ref, gcq_ref, None, 0),
            (sq_ref, sk_ref, sv_ref, so_ref, sl_ref, sg_ref, gsq_ref, None, 0),
            (scq_ref, tk_ref, tv_ref, io_ref, il_ref, ig_ref, gscq_ref, key < live_ref[0], 2),
        ):
            grad_out = g_ref[at, :]
            grad_q, grad_k, grad_v = attend_back_tile(
                q_ref[at, :], k_ref[...], v_ref[...], mask, l_ref[0, :, at], grad_out,
                row_delta(o_ref[at, :], grad_out))
            gq_ref[at, :] = (grad_q * RAW_SCALE).T.astype(jnp.bfloat16)
            sums[slot] = sums[slot] + grad_k
            sums[slot + 1] = sums[slot + 1] + grad_v
    gsk_ref[...] = (sums[0] * RAW_SCALE).astype(jnp.bfloat16)
    gsv_ref[...] = sums[1].astype(jnp.bfloat16)
    gtk_ref[...] = sums[2] * RAW_SCALE
    gtv_ref[...] = sums[3]


def self_attention_back(projected, out, log, grad_attended, extra_k, extra_v, window, after=()):
    rows, width = projected.shape
    heads = width // 4 // HD
    extra = extra_k.shape[0]
    return launch(
        partial(self_back_kernel, window), [projected] * 3 + [out, log, grad_attended, extra_k, extra_v],
        after=after, name="self_attention_back", grid=(heads,),
        in_specs=[column(rows, 0), column(rows, 2 * heads), column(rows, 3 * heads), column(rows, 0), stat(rows),
                  column(rows, 0), column(extra, 0), column(extra, 0)],
        out_specs=[column(rows, 0)] * 3, out_shape=[shaped((rows, width // 4))] * 3,
        scratch=[pltpu.VMEM((rows, HD), F32)] * 2,
        flops=heads * 10 * 2304 * 256 * HD, exps=heads * 2304 * 256,
    )


def cross_attention_back(projected, state_side, out, log, grad_attended, block, after=()):
    rows, width = state_side.shape
    heads = width // 4 // HD
    return launch(
        cross_back_kernel, [projected, state_side, state_side, out, log, grad_attended],
        after=after, name="cross_attention_back", grid=(heads,),
        in_specs=[block_column(rows, block, heads), column(rows, 2 * heads), column(rows, 3 * heads),
                  block_column(rows, block, 0), stat(rows), block_column(rows, block, heads)],
        out_specs=[block_column(rows, block, 0), column(rows, 0), column(rows, 0)],
        out_shape=[shaped((projected.shape[0], width // 4))] + [shaped((rows, width // 4))] * 2,
        flops=heads * 10 * rows * rows * HD, exps=heads * rows * rows,
    )


def state_attention_back(projected, state_side, live_keys, cross, inner_self, inner_cross, grad_attended, grad_inner, before, block, after=()):
    rows, width = state_side.shape
    heads = width // 4 // HD
    grad, wide = shaped((rows, width // 4)), shaped((rows, width // 4), F32)
    return launch(
        state_back_kernel,
        [live_keys, projected] + [state_side] * 4 + [projected] * 2
        + [cross[0], inner_self[0], inner_cross[0], cross[1], inner_self[1], inner_cross[1]]
        + [grad_attended, grad_inner, grad_inner, before],
        after=after, name="state_attention_back", grid=(heads,),
        in_specs=[SMEM, block_column(rows, block, heads)] + [column(rows, part * heads) for part in range(4)]
        + [block_column(rows, block, 2 * heads), block_column(rows, block, 3 * heads)]
        + [block_column(rows, block, 0), column(rows, 0), column(rows, 0)] + [stat(rows)] * 3
        + [block_column(rows, block, heads), column(rows, 0), column(rows, heads), pl.BlockSpec(memory_space=pl.ANY)],
        out_specs=[block_column(rows, block, 0)] + [column(rows, 0)] * 6,
        out_shape=[shaped((projected.shape[0], width // 4))] + [grad] * 4 + [wide] * 2,
        aliases={17: 0},
        flops=heads * 30 * rows * rows * HD, exps=3 * heads * rows * rows,
    )


def swap(values, axis):
    if axis == "y":
        return lax.ppermute(values, "fsdp", [(0, 1), (1, 0)])
    bit = {"core": 1, "x": 2, "z_low": 4, "z_high": 8}[axis]
    return lax.ppermute(values, "dp", [(d, d ^ bit) for d in range(16)])


LINES = [[line + 4 * z for z in range(4)] for line in range(4)]


def place():
    if not paired():
        return jnp.zeros((3,), jnp.int32)
    dp = lax.axis_index("dp")
    return jnp.stack([(dp // 2) % 2, dp % 2, lax.axis_index("fsdp")]).astype(jnp.int32)


def fence_kernel(*refs):
    pass


def fence(arrays, after):
    return launch(
        fence_kernel, arrays, after=after, name="fence", grid=(1,),
        in_specs=[pl.BlockSpec(memory_space=pl.ANY)] * len(arrays),
        out_specs=[pl.BlockSpec(memory_space=pl.ANY)] * len(arrays),
        out_shape=[shaped(item.shape, item.dtype) for item in arrays],
        aliases={i: i for i in range(len(arrays))}, flops=0,
    )


def stacked(block):
    return [block[:, i : i + COLS] for i in range(0, block.shape[1], COLS)]


def gather_blocks(blocks):
    packed = jnp.concatenate([part for block in blocks for part in stacked(block)], axis=0)
    every = lax.all_gather(packed, ("dp", "fsdp"), axis=0).reshape(16, 2, *packed.shape)
    weights, row = [], 0
    for block in blocks:
        weights.append((every, row, block.shape[0]))
        row += block.shape[0] * block.shape[1] // COLS
    return weights


def add(*terms):
    return sum(term.astype(F32) for term in terms)


def fold_core_kernel(place_ref, keep_ref, come_ref, far_ref, px_ref, py_ref, own_ref):
    x, y = place_ref[0], place_ref[2]
    cols = own_ref.shape[-1]
    for out, dx, dy in ((own_ref, 0, 0), (px_ref, 1, 0), (py_ref, 0, 1), (far_ref, 1, 1)):
        at = pl.ds(pl.multiple_of((y ^ dy) * cols, 128), cols)
        for z in range(out.shape[0]):
            out[z] = narrow(add(keep_ref[z, x ^ dx, :, at], come_ref[z, x ^ dx, :, at]))


def fold_core(keep, come, where, after=()):
    _, _, rows, cols = keep.shape
    pair = pl.BlockSpec((2, 2, rows, cols), lambda i, p: (i, 0, 0, 0))
    full = pl.BlockSpec((2, rows, cols // 2), lambda i, p: (i, 0, 0))
    return launch(
        fold_core_kernel, [keep, come], where=where, after=after, name="fold_core", grid=(2,),
        in_specs=[pair, pair], out_specs=[full] * 4, out_shape=[shaped((4, rows, cols // 2))] * 4,
        flops=keep.size,
    )


def fold_mid_kernel(near_ref, come_ref, out_ref):
    out_ref[...] = narrow(add(near_ref[...], come_ref[...]))


def fold_mid(near, come, after=()):
    _, rows, cols = near.shape
    block = pl.BlockSpec((2, rows, cols), lambda i: (i, 0, 0))
    return launch(
        fold_mid_kernel, [near, come], after=after, name="fold_mid", grid=(2,),
        in_specs=[block] * 2, out_specs=[block], out_shape=[shaped(near.shape)], flops=near.size,
    )[0]


def fold_last_kernel(own_ref, rx_ref, ry_ref, out_ref):
    out_ref[...] = narrow(add(own_ref[...], rx_ref[...], ry_ref[...]))


def fold_last(own, rx, ry, after=()):
    _, rows, cols = own.shape
    block = pl.BlockSpec((2, rows, cols), lambda i: (i, 0, 0))
    return launch(
        fold_last_kernel, [own, rx, ry], after=after, name="fold_last", grid=(2,),
        in_specs=[block] * 3, out_specs=[block], out_shape=[shaped(own.shape)], flops=2 * own.size,
    )[0]


class Scatter:
    def __init__(self, keep, send, way, where):
        self.where, self.keep, self.way = where, keep, way
        self.come = swap(send, "core")

    def core(self, after):
        far, px, py, self.own = fold_core(self.keep, self.come, self.where, after)
        self.far = swap(far, self.way)
        if self.way == "x":
            self.near, self.one = py, swap(px, "x")
        else:
            self.near, self.one = px, swap(py, "y")
        return (self.own,)

    def mid(self, after):
        near = fold_mid(self.near, self.far, after)
        self.two = swap(near, "y" if self.way == "x" else "x")
        return (near,)

    def last(self, after):
        line = fold_last(self.own, self.one, self.two, after)
        rows, cols = line.shape[1:]
        self.out = lax.psum_scatter(
            line.reshape(4 * rows, cols), "dp", scatter_dimension=0, axis_index_groups=LINES, tiled=True
        )
        return (line,)


def paired():
    return lax.axis_size("dp") == 16 and lax.axis_size("fsdp") == 2


def gather_plain(block):
    full = lax.all_gather(lax.all_gather(block, "fsdp", axis=1, tiled=True), "dp", axis=0, tiled=True)
    rows, cols = full.shape[0] // 16, full.shape[1]
    cut = full.reshape(16, rows, 2, cols // 2 // COLS, COLS).transpose(0, 2, 3, 1, 4)
    return cut.reshape(16, 2, -1, COLS), 0, rows


def scatter_plain(grad):
    rows = lax.psum_scatter(grad, "dp", scatter_dimension=0, tiled=True)
    return lax.psum_scatter(rows, "fsdp", scatter_dimension=1, tiled=True)


def gather_vectors(vectors):
    if not paired():
        return lax.all_gather(vectors, "fsdp", axis=1, tiled=True).astype(F32)
    other = swap(vectors, "y")
    first = lax.axis_index("fsdp") == 0
    return jnp.concatenate(
        [jnp.where(first, vectors, other), jnp.where(first, other, vectors)], axis=1
    ).astype(F32)


def scatter_vectors(vectors):
    part = vectors.shape[1] // lax.axis_size("fsdp")
    y = lax.axis_index("fsdp")
    if not paired():
        total = lax.psum(vectors, ("dp", "fsdp"))
        return lax.dynamic_slice_in_dim(total, y * part, part, axis=1)
    low, high = vectors[:, :part], vectors[:, part:]
    total = jnp.where(y == 0, low, high) + swap(jnp.where(y == 0, high, low), "y")
    for axis in ("core", "x", "z_low", "z_high"):
        total = total + swap(total, axis)
    return total


def shards(
    tokens,
    incoming,
    document_lengths,
    output_grad,
    token_proj,
    state_proj,
    token_out,
    state_out,
    gate_weight,
    init_state,
    hidden_in,
    hidden_out,
    token_gain,
    state_gain,
    hidden_gain,
    gate_bias,
):
    seg_len, width = tokens.shape
    window = WINDOW
    states = incoming.shape[1]
    where = place()
    segment_id = lax.axis_index(("dp", "fsdp"))
    counts = (document_lengths + seg_len - 1) // seg_len
    ends = jnp.cumsum(counts)
    starts = ends - counts
    inside = (segment_id >= starts) & (segment_id < ends)
    valid_len = jnp.sum(
        jnp.where(
            inside, jnp.minimum(seg_len, document_lengths - (segment_id - starts) * seg_len), 0
        )
    )
    first = jnp.any(segment_id == starts)
    lives = [jnp.where(b * window < valid_len, 1.0, 0.0).astype(F32).reshape(1) for b in range(2)]
    live_keys = [jnp.clip(valid_len - b * window, 0, window).astype(jnp.int32).reshape(1) for b in range(2)]

    gains = gather_vectors(jnp.stack([token_gain, state_gain, hidden_gain, gate_bias]))
    token_gain_f, state_gain_f, hidden_gain_f, gate_bias_f = [gains[i : i + 1] for i in range(4)]
    order = ()

    early = [token_proj, state_proj, state_out, token_out, gate_weight, init_state]
    late = [hidden_in, hidden_out]
    gather = gather_blocks if paired() else lambda blocks: [gather_plain(block) for block in blocks]
    full_token_proj, full_state_proj, full_state_out, full_token_out, full_gate_weight, full_init = gather(early)
    full_hidden_in, full_hidden_out = gather(late)
    array, row, rows = full_init
    full_init = array[:, :, row : row + rows].transpose(0, 2, 1, 3).reshape(states, width)
    state_0 = jnp.where(first, full_init, incoming[0]).astype(F32)
    normed, projected = norm_project(tokens, token_gain_f, full_token_proj, order)
    order = (projected,)
    normed_0, side_0 = norm_project(state_0, state_gain_f, full_state_proj, order)
    order = (side_0,)
    inner_self_0, inner_cross_0, inner_self_log, inner_cross_log = inner_attention(
        projected, side_0, live_keys[0], 0, order
    )
    order = (inner_self_log,)
    mixed_0, gate_0, state_1 = update_state(
        lives[0], inner_self_0, inner_cross_0, full_state_out, full_gate_weight, gate_bias_f, state_0, order
    )
    order = (mixed_0,)
    normed_1, side_1 = norm_project(state_1, state_gain_f, full_state_proj, order)
    order = (normed_1,)
    cross_out, cross_log_0 = cross_attention(projected, side_0, 0, None, order)
    order = (cross_log_0,)
    cross_out, cross_log_1 = cross_attention(projected, side_1, 1, cross_out, order)
    order = (cross_log_1,)
    self_out, self_log = self_attention(projected, window, order)
    order = (self_log,)
    middle, hidden_normed = branch(self_out, cross_out, full_token_out, tokens, hidden_gain_f, order)
    order = (hidden_normed,)
    active, slope = hidden(hidden_normed, full_hidden_in, order)
    order = (active,)

    scatters = {}

    def weight(name, way, lefts, rights, plan, split=False):
        nonlocal order
        if paired():
            keep, send = weight_grad(lefts, rights, plan, where, "grad_" + name, split, order)
            scatters[name] = Scatter(keep, send, way, where)
            order = (keep,)
            return
        if split:
            lefts = [jnp.concatenate(lefts, axis=1)]
        grad = jnp.concatenate(
            [sum(matmul_left_t(lefts[a], rights[b]) for a, b in terms) for terms in plan], axis=1
        )
        scatters[name] = scatter_plain(narrow(grad))

    def fold(name, step):
        nonlocal order
        if paired():
            order = getattr(scatters[name], step)(order)

    one = [[(0, 0)]]
    weight("hidden_out", "x", [active], [output_grad], one)
    fold("hidden_out", "core")
    result, grad_pre = result_and_pre(active, slope, full_hidden_out, middle, output_grad, order)
    order = (result,)
    fold("hidden_out", "mid")
    weight("hidden_in", "y", [hidden_normed], [grad_pre], one)
    grad_hidden_gain, grad_branch, grad_middle = norm_back_project(
        [grad_pre], full_hidden_in, middle, hidden_gain_f, output_grad, "hidden_back", True, after=order
    )
    order = (grad_hidden_gain,)
    fold("hidden_in", "core")
    fold("hidden_out", "last")
    grad_attended = spread(grad_branch, full_token_out, order)
    order = (grad_attended,)
    weight("token_out", "x", [self_out, cross_out], [grad_branch], one, True)
    grad_cross, grad_keys_1, grad_values_1 = cross_attention_back(
        projected, side_1, cross_out, cross_log_1, grad_attended, 1, order
    )
    order = (grad_keys_1,)
    fold("hidden_in", "mid")
    fold("token_out", "core")
    no_term = jnp.zeros((states, width), jnp.bfloat16)
    grad_state_gain_1, _, grad_state_1 = norm_back_project(
        [grad_keys_1, grad_values_1], full_state_proj, state_1, state_gain_f, no_term, "side_back", True,
        offset=2 * width, after=order,
    )
    order = (grad_state_gain_1,)
    grad_gate_low, grad_mixed, grad_inner, grad_direct, grad_gate_bias = gate_back(
        lives[0], grad_state_1, gate_0, state_0, mixed_0, full_gate_weight, full_state_out, order
    )
    order = (grad_gate_bias,)
    fold("token_out", "mid")
    parts = state_attention_back(
        projected, side_0, live_keys[0], (cross_out, cross_log_0), (inner_self_0, inner_self_log),
        (inner_cross_0, inner_cross_log), grad_attended, grad_inner, grad_cross, 0, order,
    )
    grad_cross, grads_side_0, extra_keys, extra_values = parts[0], parts[1:5], parts[5], parts[6]
    order = (extra_keys,)
    fold("hidden_in", "last")
    weight("state_out", "y", [inner_self_0, inner_cross_0], [grad_mixed], one, True)
    weight("gate_weight", "y", [mixed_0], [grad_gate_low], one)
    fold("token_out", "last")
    fold("state_out", "core")
    fold("gate_weight", "core")
    grad_self, grad_keys, grad_values = self_attention_back(
        projected, self_out, self_log, grad_attended, extra_keys, extra_values, window, order
    )
    order = (grad_self,)
    grads_projected = [grad_self, grad_cross, grad_keys, grad_values]
    weight("token_proj", "x", [normed], grads_projected, [[(0, i)] for i in range(4)])
    fold("state_out", "mid")
    fold("gate_weight", "mid")
    weight(
        "state_proj", "y", [normed_0, normed_1], [*grads_side_0, grad_keys_1, grad_values_1],
        [[(0, 0)], [(0, 1)], [(0, 2), (1, 4)], [(0, 3), (1, 5)]],
    )
    fold("token_proj", "core")
    grad_state_gain_0, grad_init = norm_back_project(
        grads_side_0, full_state_proj, state_0, state_gain_f, grad_direct, "state_back",
        scale=jnp.where(first, 1.0, 0.0).astype(F32).reshape(1), after=order,
    )
    order = (grad_state_gain_0,)
    fold("state_proj", "core")
    fold("state_out", "last")
    fold("gate_weight", "last")
    if paired():
        parts = grad_init.reshape(4, 2, 2, 32, width)
        keep = lax.dynamic_index_in_dim(parts, where[1], 2, keepdims=False)
        send = lax.dynamic_index_in_dim(parts, 1 - where[1], 2, keepdims=False)
        scatters["init"] = Scatter(keep, send, "x", where)
    else:
        scatters["init"] = scatter_plain(grad_init)
    grad_token_gain, tokens_grad = norm_back_project(
        grads_projected, full_token_proj, tokens, token_gain_f, grad_middle, "tokens_back", after=order
    )
    order = (grad_token_gain,)
    fold("init", "core")
    fold("token_proj", "mid")
    inner_self_1, inner_cross_1, log, _ = inner_attention(projected, side_1, live_keys[1], 1, order)
    order = (log,)
    fold("init", "mid")
    fold("token_proj", "last")
    fold("state_proj", "mid")
    _, _, state_2 = update_state(
        lives[1], inner_self_1, inner_cross_1, full_state_out, full_gate_weight, gate_bias_f, state_1, order
    )
    order = (state_2,)
    fold("init", "last")
    fold("state_proj", "last")
    vector_grads = scatter_vectors(
        jnp.concatenate(
            [grad_token_gain, grad_state_gain_0 + grad_state_gain_1, grad_hidden_gain, grad_gate_bias], axis=0
        )
    )
    matrix_grads = [
        (scatters[name].out if paired() else scatters[name]).astype(F32)
        for name in (
            "token_proj", "state_proj", "token_out", "state_out", "gate_weight", "init", "hidden_in", "hidden_out",
        )
    ]
    return (
        result,
        narrow(state_2)[None],
        tokens_grad,
        *matrix_grads,
        *[vector_grads[i] for i in range(4)],
    )


def solution(mesh):
    return jax.shard_map(
        shards,
        mesh=mesh,
        in_specs=(
            P(("dp", "fsdp"), None),
            P(("dp", "fsdp"), None, None),
            P(),
            P(("dp", "fsdp"), None),
            P("dp", "fsdp"),
            P("dp", "fsdp"),
            P("dp", "fsdp"),
            P("dp", "fsdp"),
            P("dp", "fsdp"),
            P("dp", "fsdp"),
            P("dp", "fsdp"),
            P("dp", "fsdp"),
            P("fsdp"),
            P("fsdp"),
            P("fsdp"),
            P("fsdp"),
        ),
        out_specs=(
            P(("dp", "fsdp"), None),
            P(("dp", "fsdp"), None, None),
            P(("dp", "fsdp"), None),
            P("dp", "fsdp"),
            P("dp", "fsdp"),
            P("dp", "fsdp"),
            P("dp", "fsdp"),
            P("dp", "fsdp"),
            P("dp", "fsdp"),
            P("dp", "fsdp"),
            P("dp", "fsdp"),
            P("fsdp"),
            P("fsdp"),
            P("fsdp"),
            P("fsdp"),
        ),
        check_vma=False,
    )
```

```python
from functools import partial
import math

import jax
import jax.numpy as jnp
from jax import lax
from jax.experimental import pallas as pl
from jax.experimental.pallas import tpu as pltpu
from jax.sharding import PartitionSpec as P

HD = 128
WINDOW = 512
MIB = 1 << 20


norm_eps = 1e-06
masked_score = -1e30
EXP_SCALE = math.log2(math.e) / math.sqrt(HD)
RAW_SCALE = 1.0 / math.sqrt(HD)
NT = (((1,), (1,)), ((), ()))
TN = (((0,), (0,)), ((), ()))
NN = (((1,), (0,)), ((), ()))


def narrow(values):
    return values.astype(jnp.bfloat16)


def matmul_left_t(left, right):
    return lax.dot_general(left, right, TN, preferred_element_type=jnp.float32)


MICROSECOND = 1.15e9
TIMES = {
    "norm_project": 13, "self_attention": 17, "inner_attention": 17, "cross_attention": 10, "update_state": 9, "branch": 10,
    "hidden": 20, "grad_hidden_out": 14, "result_and_pre": 24, "grad_hidden_in": 15, "hidden_back": 20, "spread": 8,
    "cross_attention_back": 10, "side_back": 9, "gate_back": 9, "grad_out": 16, "state_attention_back": 22, "state_back": 13,
    "grad_state_proj": 13, "self_attention_back": 18, "grad_token_proj": 15, "tokens_back": 21, "spell": 7, "fence": 1,
    "fold_core": 5, "fold_mid": 2, "fold_last": 2, "widen": 1,
}


def launch(body, operands, *, grid, in_specs, out_specs, out_shape, name, flops, after=(), where=None, scratch=(), aliases=None, exps=0, limit=48):
    count = len(operands)
    late = len(after)
    lead = 0 if where is None else 1

    def run(*refs):
        body(*refs[: lead + count], *refs[lead + count + late :])

    specs = list(in_specs) + [pl.BlockSpec(memory_space=pl.ANY)] * late
    size = sum(math.prod(item.shape) * item.dtype.itemsize for item in (*operands, *out_shape))
    kwargs = dict(grid=grid, in_specs=specs, out_specs=list(out_specs))
    if where is None:
        kwargs["scratch_shapes"] = list(scratch)
    else:
        kwargs = dict(
            grid_spec=pltpu.PrefetchScalarGridSpec(
                num_scalar_prefetch=1, scratch_shapes=list(scratch), **kwargs
            )
        )
    return pl.pallas_call(
        run,
        out_shape=list(out_shape),
        input_output_aliases=aliases or {},
        compiler_params=pltpu.CompilerParams(vmem_limit_bytes=limit * MIB),
        cost_estimate=pl.CostEstimate(flops=int(MICROSECOND * TIMES[name]), bytes_accessed=1024, transcendentals=0),
        name=name,
        **kwargs,
    )(*(() if where is None else (where,)), *operands, *after)


def shaped(shape, dtype=jnp.bfloat16):
    return jax.ShapeDtypeStruct(shape, dtype)


def whole(shape):
    return pl.BlockSpec(shape, lambda *ids: (0,) * len(shape))


SMEM = pl.BlockSpec(memory_space=pltpu.SMEM)
F32 = jnp.float32


def norm_rows(values):
    centered = values - jnp.mean(values, axis=-1, keepdims=True)
    return centered, lax.rsqrt(jnp.mean(centered * centered, axis=-1, keepdims=True) + norm_eps)


def norm_back_rows(values, gain, grad):
    centered, inverse = norm_rows(values)
    normal = centered * inverse
    scaled = grad * gain
    mean = jnp.mean(scaled, axis=-1, keepdims=True)
    along = jnp.mean(scaled * normal, axis=-1, keepdims=True)
    return inverse * (scaled - mean - normal * along), jnp.sum(grad * normal, axis=0, keepdims=True)


ROWS = 128
COLS = 512


STEP = 2 * COLS


def group_spec(weight, group):
    array, start, rows = weight

    def place_of(*ids):
        which = group(ids[0])
        return 0, which // 2, start // (2 * rows) + which % 2, 0

    return pl.BlockSpec((16, 1, 2 * rows, COLS), place_of)


def group(w_ref, which):
    rows = w_ref.shape[2] // 2
    return w_ref[:, 0, which * rows : (which + 1) * rows, :].reshape(-1, COLS)


def cols(which):
    return slice(which * COLS, (which + 1) * COLS)


def rows_spec(weight, count, step=lambda i: i):
    array, start, rows = weight
    return pl.BlockSpec((count, 2, rows, COLS), lambda *ids: (step(ids[0]), 0, start // rows, 0))


def side(w_ref, y, blocks=slice(None)):
    values = w_ref[blocks, y]
    return values.reshape(-1, COLS)


def times(left, w_ref, blocks=slice(None)):
    return jnp.concatenate([dot(left, side(w_ref, y, blocks), NN) for y in range(2)], axis=1)


def times_turned(left, w_ref):
    return sum(dot(left[:, y * COLS : (y + 1) * COLS], side(w_ref, y), NT) for y in range(2))


def norm_project_kernel(x_ref, gain_ref, w_ref, normed_ref, out_ref):
    @pl.when(pl.program_id(0) == 0)
    def _():
        @pl.loop(0, x_ref.shape[0] // ROWS)
        def _(i):
            at = pl.ds(pl.multiple_of(i * ROWS, ROWS), ROWS)
            centered, inverse = norm_rows(x_ref[at, :].astype(F32))
            normed_ref[at, :] = narrow(centered * inverse * gain_ref[...])

    for which in range(2):
        out_ref[:, cols(which)] = narrow(dot(normed_ref[...], group(w_ref, which), NN))


def norm_project(x, gain, weight, after=()):
    rows, width = x.shape
    total_cols = 4 * width
    step = STEP
    return launch(
        norm_project_kernel, [x, gain, weight[0]], after=after, name="norm_project", grid=(total_cols // step,),
        in_specs=[whole((rows, width)), whole((1, width)), group_spec(weight, lambda i: i)],
        out_specs=[whole((rows, width)), pl.BlockSpec((rows, step), lambda i: (0, i))],
        out_shape=[shaped((rows, width)), shaped((rows, total_cols))],
        flops=2 * rows * width * total_cols,
    )


def update_kernel(live_ref, self_ref, cross_ref, out_w_ref, gate_w_ref, bias_ref, state_ref, mixed_ref, gate_ref, new_ref):
    low, high = slice(0, 8), slice(8, 16)
    mixed = narrow(times(self_ref[...], out_w_ref, low) + times(cross_ref[...], out_w_ref, high))
    mixed_ref[...] = mixed
    gate = jax.nn.sigmoid(times(mixed, gate_w_ref) + bias_ref[...])
    gate_ref[...] = gate
    state = state_ref[...]
    updated = gate * state + (1.0 - gate) * jnp.tanh(mixed.astype(F32))
    new_ref[...] = state + live_ref[0] * (updated - state)


def update_state(live, inner_self, inner_cross, state_out, gate_weight, bias, state, after=()):
    rows, width = state.shape
    step = 256
    tile = pl.BlockSpec((step, width), lambda i: (i, 0))
    return launch(
        update_kernel, [live, inner_self, inner_cross, state_out[0], gate_weight[0], bias, state],
        after=after, name="update_state", grid=(rows // step,),
        in_specs=[SMEM, tile, tile, rows_spec(state_out, 16, lambda i: 0), rows_spec(gate_weight, 16, lambda i: 0), whole((1, width)), tile],
        out_specs=[tile, tile, tile],
        out_shape=[shaped((rows, width)), shaped((rows, width), F32), shaped((rows, width), F32)],
        flops=6 * rows * width * width, exps=2 * rows * width,
    )


def branch_kernel(self_ref, cross_ref, w_ref, x_ref, gain_ref, middle_ref, normed_ref):
    low, high = slice(0, 8), slice(8, 16)
    middle = x_ref[...].astype(F32) + (times(self_ref[...], w_ref, low) + times(cross_ref[...], w_ref, high))
    middle_ref[...] = middle
    centered, inverse = norm_rows(middle)
    normed_ref[...] = narrow(centered * inverse * gain_ref[...])


def branch(self_out, cross_out, token_out, x, gain, after=()):
    rows, width = x.shape
    step = 256
    tile = pl.BlockSpec((step, width), lambda i: (i, 0))
    return launch(
        branch_kernel, [self_out, cross_out, token_out[0], x, gain], after=after, name="branch", grid=(rows // step,),
        in_specs=[tile, tile, rows_spec(token_out, 16, lambda i: 0), tile, whole((1, width))],
        out_specs=[tile, tile],
        out_shape=[shaped((rows, width), F32), shaped((rows, width))],
        flops=4 * rows * width * width,
    )


GELU_A = math.sqrt(2.0 / math.pi)
GELU_B = 0.044715


def hidden_kernel(normed_ref, w_ref, active_ref, slope_ref):
    for start in range(0, normed_ref.shape[0], 256):
        for which in range(2):
            at = slice(start, start + 256), cols(which)
            v = dot(normed_ref[start : start + 256, :], group(w_ref, which), NN)
            square = v * v
            t = jnp.tanh(v * (GELU_A + (GELU_A * GELU_B) * square))
            half = 0.5 + 0.5 * t
            active_ref[at] = narrow(v * half)
            slope = half + v * (1.0 - t * t) * (0.5 * GELU_A + (1.5 * GELU_A * GELU_B) * square)
            slope_ref[at] = narrow(slope)


def hidden(normed, weight, after=()):
    rows, width = normed.shape
    total_cols = 4 * width
    step = STEP
    tile = pl.BlockSpec((rows, step), lambda i: (0, i))
    return launch(
        hidden_kernel, [normed, weight[0]], after=after, name="hidden", grid=(total_cols // step,),
        in_specs=[whole((rows, width)), group_spec(weight, lambda i: i)],
        out_specs=[tile, tile], out_shape=[shaped((rows, total_cols))] * 2,
        flops=2 * rows * width * total_cols, exps=rows * total_cols,
    )


def result_kernel(active_ref, slope_ref, w_ref, middle_ref, grad_ref, result_ref, pre_ref, total_ref):
    first = pl.program_id(0) == 0
    for start in range(0, active_ref.shape[0], 256):
        at = slice(start, start + 256)
        pre_ref[at, :] = narrow(times_turned(grad_ref[at, :], w_ref) * slope_ref[at, :].astype(F32))
        total_ref[at, :] = jnp.where(first, middle_ref[at, :], total_ref[at, :]) + times(active_ref[at, :], w_ref)

    @pl.when(pl.program_id(0) == pl.num_programs(0) - 1)
    def _():
        result_ref[...] = narrow(total_ref[...])


def result_and_pre(active, slope, weight, middle, grad, after=()):
    rows, hidden_units = active.shape
    width = middle.shape[1]
    step = STEP
    tile = pl.BlockSpec((rows, step), lambda i: (0, i))
    return launch(
        result_kernel, [active, slope, weight[0], middle, grad], after=after, name="result_and_pre",
        grid=(hidden_units // step,),
        in_specs=[tile, tile, rows_spec(weight, step // weight[2]), whole((rows, width)), whole((rows, width))],
        out_specs=[whole((rows, width)), tile],
        out_shape=[shaped((rows, width)), shaped((rows, hidden_units))],
        scratch=[pltpu.VMEM((rows, width), F32)],
        flops=4 * rows * width * hidden_units,
    )


def norm_back_kernel(parts, keep_wide, scale_ref, *refs):
    grads, (w_ref, x_ref, gain_ref, plus_ref) = refs[:parts], refs[parts : parts + 4]
    outs, total_ref = refs[parts + 4 : -1], refs[-1]
    i = pl.program_id(0)
    share = pl.num_programs(0) // parts

    @pl.when(i == 0)
    def _():
        total_ref[...] = jnp.zeros_like(total_ref)

    for part in range(parts):
        @pl.when(i // share == part)
        def _():
            total_ref[...] += sum(dot(grads[part][:, cols(which)], group(w_ref, which), NT) for which in range(2))

    @pl.when(i == pl.num_programs(0) - 1)
    def _():
        outs[0][...] = jnp.zeros_like(outs[0])

        @pl.loop(0, x_ref.shape[0] // ROWS)
        def _(j):
            at = pl.ds(pl.multiple_of(j * ROWS, ROWS), ROWS)
            grad, gain_grad = norm_back_rows(x_ref[at, :].astype(F32), gain_ref[...], total_ref[at, :])
            grad = grad + plus_ref[at, :].astype(F32)
            outs[0][...] += gain_grad
            outs[1][at, :] = narrow(jnp.where(scale_ref[0] > 0.0, grad, 0.0))
            if keep_wide:
                outs[2][at, :] = grad


def norm_back_project(grads, weight, x, gain, plus, name, keep_wide=False, offset=0, scale=None, after=()):
    rows, width = x.shape
    step = STEP
    share = grads[0].shape[1] // step
    parts = len(grads)
    steps = parts * share
    def part_spec(part):
        return pl.BlockSpec((rows, step), lambda i: (0, jnp.clip(i - part * share, 0, share - 1)))
    out_shape = [shaped((1, width), F32), shaped((rows, width))]
    if keep_wide:
        out_shape.append(shaped((rows, width), F32))
    if scale is None:
        scale = jnp.ones((1,), F32)
    return launch(
        partial(norm_back_kernel, parts, keep_wide), [scale, *grads, weight[0], x, gain, plus], after=after, name=name,
        grid=(steps,),
        in_specs=[SMEM] + [part_spec(part) for part in range(parts)]
        + [group_spec(weight, lambda i: i + offset // step), whole((rows, width)), whole((1, width)), whole((rows, width))],
        out_specs=[whole(item.shape) for item in out_shape], out_shape=out_shape,
        scratch=[pltpu.VMEM((rows, width), F32)],
        flops=2 * rows * width * steps * step,
    )


def spread_kernel(grad_ref, w_ref, out_ref):
    out_ref[...] = narrow(times_turned(grad_ref[...], w_ref))


def spread(grad, weight, after=()):
    rows, width = grad.shape
    total_cols = 16 * weight[2]
    step = STEP
    return launch(
        spread_kernel, [grad, weight[0]], after=after, name="spread", grid=(total_cols // step,),
        in_specs=[whole((rows, width)), rows_spec(weight, step // weight[2])],
        out_specs=[pl.BlockSpec((rows, step), lambda i: (0, i))],
        out_shape=[shaped((rows, total_cols))], flops=2 * rows * width * total_cols,
    )[0]


def gate_back_kernel(live_ref, grad_ref, gate_ref, state_ref, mixed_ref, gate_w_ref, out_w_ref,
                     pre_ref, grad_mixed_ref, inner_ref, direct_ref, bias_ref):
    grad, gate, live = grad_ref[...], gate_ref[...], live_ref[0]
    tanh_mixed = jnp.tanh(mixed_ref[...].astype(F32))
    updated = live * grad
    direct_ref[...] = (1.0 - live) * grad + updated * gate
    pre = gate * (1.0 - gate) * updated * (state_ref[...] - tanh_mixed)

    @pl.when(pl.program_id(0) == 0)
    def _():
        bias_ref[...] = jnp.zeros_like(bias_ref)

    bias_ref[...] += jnp.sum(pre, axis=0, keepdims=True)
    low = narrow(pre)
    pre_ref[...] = low
    grad_mixed = narrow(
        times_turned(low, gate_w_ref) + updated * (1.0 - gate) * (1.0 - tanh_mixed * tanh_mixed)
    )
    grad_mixed_ref[...] = grad_mixed
    inner_ref[...] = narrow(times_turned(grad_mixed, out_w_ref))


def gate_back(live, grad, gate, state, mixed, gate_weight, state_out, after=()):
    rows, width = grad.shape
    step = 256
    tile = pl.BlockSpec((step, width), lambda i: (i, 0))
    wide = pl.BlockSpec((step, 2 * width), lambda i: (i, 0))
    return launch(
        gate_back_kernel, [live, grad, gate, state, mixed, gate_weight[0], state_out[0]], after=after, name="gate_back",
        grid=(rows // step,),
        in_specs=[SMEM, tile, tile, tile, tile, rows_spec(gate_weight, 16, lambda i: 0), rows_spec(state_out, 16, lambda i: 0)],
        out_specs=[tile, tile, wide, tile, whole((1, width))],
        out_shape=[shaped((rows, width)), shaped((rows, width)), shaped((rows, 2 * width)), shaped((rows, width), F32), shaped((1, width), F32)],
        flops=6 * rows * width * width, exps=rows * width,
    )


def weight_grad_kernel(jobs, counts, extra, place_ref, *refs):
    lefts, rights = refs[: counts[0]], refs[counts[0] : counts[0] + counts[1]]
    keep_ref, send_ref = refs[-2], refs[-1]
    core = place_ref[1]
    z = pl.program_id(0)

    def run(plan, row, rows, pick):
        turned = {left: lefts[pick(left)][...].T for left in sorted({left for terms in plan for left, _ in terms})}
        col = 0
        for terms in plan:
            cols = rights[terms[0][1]].shape[1]
            for start in range(0, cols, 512):
                total = sum(
                    dot(turned[left], rights[right][:, start : start + 512], NN) for left, right in terms
                )
                total = narrow(total)
                at = slice(col + start, col + start + 512)
                for x in range(2):
                    even = total[2 * x * rows : (2 * x + 1) * rows]
                    odd = total[(2 * x + 1) * rows : (2 * x + 2) * rows]
                    keep_ref[0, x, row : row + rows, at] = jnp.where(core == 0, even, odd)
                    send_ref[0, x, row : row + rows, at] = jnp.where(core == 0, odd, even)
            col += cols

    for plan, split, row, rows in jobs:
        if split:
            pl.when(z < 2)(partial(run, plan, row, rows, lambda left: left))
            pl.when(z >= 2)(partial(run, plan, row, rows, lambda left: left + 1))
        else:
            run(plan, row, rows, lambda left: left)
    if extra is not None:
        source, row = refs[counts[0] + counts[1]], extra
        for x in range(2):
            for part in range(2):
                for y in range(2):
                    at = slice(y * 2048 + part * 512, y * 2048 + (part + 1) * 512)
                    even = source[0, x, 0, part * 16 : (part + 1) * 16, y * 512 : (y + 1) * 512]
                    odd = source[0, x, 1, part * 16 : (part + 1) * 16, y * 512 : (y + 1) * 512]
                    keep_ref[0, x, row : row + 16, at] = jnp.where(core == 0, even, odd)
                    send_ref[0, x, row : row + 16, at] = jnp.where(core == 0, odd, even)
            for y in range(2):
                at = slice(y * 2048 + 1024, (y + 1) * 2048)
                keep_ref[0, x, row : row + 16, at] = jnp.zeros((16, 1024), jnp.bfloat16)
                send_ref[0, x, row : row + 16, at] = jnp.zeros((16, 1024), jnp.bfloat16)


def weight_grad(jobs, where, name, extra=None, after=()):
    lefts, rights, specs, table, row = [], [], [], [], 0
    for these, those, plan, split in jobs:
        rows = these[0].shape[1] * (2 if split else 1) // 16
        shift = [[(left + len(lefts), right + len(rights)) for left, right in terms] for terms in plan]
        table.append((shift, split, row, rows))
        for index, item in enumerate(these):
            if split:
                block = (lambda z, p: (0, jnp.minimum(z, 1))) if index == 0 else (lambda z, p: (0, jnp.maximum(z, 2) - 2))
            else:
                block = lambda z, p: (0, z)
            specs.append(pl.BlockSpec((item.shape[0], 4 * rows), block))
        lefts += these
        rights += those
        row += rows
    cols = sum(rights[terms[0][1]].shape[1] for terms in table[0][0])
    operands = [*lefts, *rights]
    specs += [whole(item.shape) for item in rights]
    at = None
    if extra is not None:
        operands.append(extra.reshape(4, 2, 2, 32, extra.shape[1]))
        specs.append(pl.BlockSpec((1, 2, 2, 32, extra.shape[1]), lambda z, p: (z, 0, 0, 0, 0)))
        at, row = row, row + 16
    out = pl.BlockSpec((1, 2, row, cols), lambda z, p: (z, 0, 0, 0))
    return launch(
        partial(weight_grad_kernel, table, (len(lefts), len(rights)), at), operands,
        where=where, after=after, name=name, grid=(4,), in_specs=specs,
        out_specs=[out, out], out_shape=[shaped((4, 2, row, cols))] * 2,
        flops=2 * rights[0].shape[0] * 16 * row * cols, limit=56,
    )


def dot(a, b, dims):
    return lax.dot_general(a, b, dims, preferred_element_type=jnp.float32)


HEADS = 2
TILE = 256


def attend_all(items):
    scores = [dot(k, q, NT) for q, k, v, mask, put in items]
    scores = [
        part if item[3] is None else jnp.where(item[3], part, masked_score) for part, item in zip(scores, items)
    ]
    tops = [jnp.max(part, axis=0, keepdims=True) for part in scores]
    weights = [jnp.exp2((part - top) * EXP_SCALE) for part, top in zip(scores, tops)]
    totals = [jnp.sum(part, axis=0, keepdims=True) for part in weights]
    for (q, k, v, mask, put), top, part, total in zip(items, tops, weights, totals):
        mixed = dot(v, narrow(part), TN) / total
        put(narrow(mixed.T), top * EXP_SCALE + jnp.log2(total))


def attend_all_back(items):
    probs = [jnp.exp2(dot(k, q, NT) * EXP_SCALE - log) for q, k, v, mask, log, out, grad, put in items]
    probs = [part if item[3] is None else jnp.where(item[3], part, 0.0) for part, item in zip(probs, items)]
    deltas = [row_delta(out, grad) for q, k, v, mask, log, out, grad, put in items]
    grad_probs = [dot(v, grad, NT) for q, k, v, mask, log, out, grad, put in items]
    grad_raws = [narrow(part * (other - delta)) for part, other, delta in zip(probs, grad_probs, deltas)]
    for (q, k, v, mask, log, out, grad, put), part, grad_raw in zip(items, probs, grad_raws):
        grad_q = (dot(k, grad_raw, TN) * RAW_SCALE).T
        put(narrow(grad_q), dot(grad_raw, q, NN), dot(narrow(part), grad, NN))


def row_delta(out, grad_out):
    both = out.astype(jnp.float32) * grad_out.astype(jnp.float32)
    return jnp.sum(both.T, axis=0, keepdims=True)


def band_mask(rows, cols, key_start, query_start, window):
    key = lax.broadcasted_iota(jnp.int32, (rows, cols), 0) + key_start
    query = lax.broadcasted_iota(jnp.int32, (rows, cols), 1) + query_start
    return (key <= query) & (key > query - window)


def head_cols(head):
    return slice(head * HD, (head + 1) * HD)


def storing(out_ref, log_ref, head, at):
    def put(out, log):
        out_ref[at, head_cols(head)] = out
        log_ref[head, :, at] = log

    return put


def column(rows, offset):
    return pl.BlockSpec((rows, HD * HEADS), lambda h: (0, h + offset // HEADS))


def block_column(rows, block, offset):
    return pl.BlockSpec((rows, HD * HEADS), lambda h: (block, h + offset // HEADS))


def stat(rows):
    return pl.BlockSpec((HEADS, 1, rows), lambda h: (h, 0, 0))


def bands(rows, window):
    for start in range(0, rows, TILE):
        low = max(0, start - window)
        yield slice(start, start + TILE), slice(low, start + TILE), band_mask(start + TILE - low, TILE, low, start, window)


def self_kernel(window, q_ref, k_ref, v_ref, out_ref, log_ref):
    attend_all(
        [
            (q_ref[at, head_cols(h)], k_ref[keys, head_cols(h)], v_ref[keys, head_cols(h)], mask, storing(out_ref, log_ref, h, at))
            for h in range(HEADS)
            for at, keys, mask in bands(q_ref.shape[0], window)
        ]
    )


def self_attention(projected, window, after=()):
    rows, width = projected.shape
    heads = width // 4 // HD
    return launch(
        partial(self_kernel, window), [projected] * 3, after=after, name="self_attention", grid=(heads // HEADS,),
        in_specs=[column(rows, 0), column(rows, 2 * heads), column(rows, 3 * heads)],
        out_specs=[column(rows, 0), stat(rows)],
        out_shape=[shaped((rows, width // 4)), shaped((heads, 1, rows), F32)],
        flops=heads * 4 * 2304 * 256 * HD, exps=heads * 2304 * 256,
    )


def cross_kernel(q_ref, k_ref, v_ref, *refs):
    out_ref, log_ref = refs[-2:]
    attend_all(
        [
            (q_ref[at, head_cols(h)], k_ref[:, head_cols(h)], v_ref[:, head_cols(h)], None, storing(out_ref, log_ref, h, at))
            for h in range(HEADS)
            for at in (slice(start, start + TILE) for start in range(0, q_ref.shape[0], TILE))
        ]
    )


def cross_attention(projected, state_side, block, before=None, after=()):
    rows, width = state_side.shape
    heads = width // 4 // HD
    operands = [projected, state_side, state_side]
    specs = [block_column(rows, block, heads), column(rows, 2 * heads), column(rows, 3 * heads)]
    if before is not None:
        operands.append(before)
        specs.append(pl.BlockSpec(memory_space=pl.ANY))
    return launch(
        cross_kernel, operands, after=after, name="cross_attention", grid=(heads // HEADS,), in_specs=specs,
        out_specs=[block_column(rows, block, 0), stat(rows)],
        out_shape=[shaped((projected.shape[0], width // 4)), shaped((heads, 1, rows), F32)],
        aliases=None if before is None else {3: 0},
        flops=heads * 4 * rows * rows * HD, exps=heads * rows * rows,
    )


def inner_kernel(live_ref, sq_ref, scq_ref, sk_ref, sv_ref, tk_ref, tv_ref, self_ref, cross_ref, self_log, cross_log):
    rows = sq_ref.shape[0]
    mask = lax.broadcasted_iota(jnp.int32, (rows, rows), 0) < live_ref[0]
    at = slice(0, rows)
    items = []
    for h in range(HEADS):
        cols_h = head_cols(h)
        items.append((sq_ref[:, cols_h], sk_ref[:, cols_h], sv_ref[:, cols_h], None, storing(self_ref, self_log, h, at)))
        items.append((scq_ref[:, cols_h], tk_ref[:, cols_h], tv_ref[:, cols_h], mask, storing(cross_ref, cross_log, h, at)))
    attend_all(items)


def inner_attention(projected, state_side, live_keys, block, after=()):
    rows, width = state_side.shape
    heads = width // 4 // HD
    return launch(
        inner_kernel, [live_keys] + [state_side] * 4 + [projected] * 2, after=after, name="inner_attention", grid=(heads // HEADS,),
        in_specs=[SMEM] + [column(rows, part * heads) for part in range(4)]
        + [block_column(rows, block, 2 * heads), block_column(rows, block, 3 * heads)],
        out_specs=[column(rows, 0)] * 2 + [stat(rows)] * 2,
        out_shape=[shaped((rows, width // 4))] * 2 + [shaped((heads, 1, rows), F32)] * 2,
        flops=heads * 8 * rows * rows * HD, exps=2 * heads * rows * rows,
    )


def self_back_kernel(window, q_ref, k_ref, v_ref, out_ref, log_ref, grad_ref, ek_ref, ev_ref, gq_ref, gk_ref, gv_ref, sk_ref, sv_ref):
    rows = q_ref.shape[0]
    extra = ek_ref.shape[0]
    sk_ref[...] = jnp.zeros_like(sk_ref)
    sv_ref[:extra, :] = ev_ref[...]
    sv_ref[extra:, :] = jnp.zeros((rows - extra, HD * HEADS), F32)

    def adding(cols_h, at, keys):
        def put(grad_q, grad_k, grad_v):
            gq_ref[at, cols_h] = grad_q
            sk_ref[keys, cols_h] += grad_k
            sv_ref[keys, cols_h] += grad_v

        return put

    for h in range(HEADS):
        cols_h = head_cols(h)
        attend_all_back(
            [
                (q_ref[at, cols_h], k_ref[keys, cols_h], v_ref[keys, cols_h], mask, log_ref[h, :, at], out_ref[at, cols_h],
                 grad_ref[at, cols_h], adding(cols_h, at, keys))
                for at, keys, mask in bands(rows, window)
            ]
        )
    gk_ref[:extra, :] = narrow(sk_ref[:extra, :] * RAW_SCALE + ek_ref[...])
    gk_ref[extra:, :] = narrow(sk_ref[extra:, :] * RAW_SCALE)
    gv_ref[...] = narrow(sv_ref[...])


def cross_back_kernel(q_ref, k_ref, v_ref, out_ref, log_ref, grad_ref, gq_ref, gk_ref, gv_ref):
    def storing_back(cols_h):
        def put(grad_q, grad_k, grad_v):
            gq_ref[:, cols_h] = grad_q
            gk_ref[:, cols_h] = narrow(grad_k * RAW_SCALE)
            gv_ref[:, cols_h] = narrow(grad_v)

        return put

    attend_all_back(
        [
            (q_ref[:, head_cols(h)], k_ref[:, head_cols(h)], v_ref[:, head_cols(h)], None, log_ref[h], out_ref[:, head_cols(h)],
             grad_ref[:, head_cols(h)], storing_back(head_cols(h)))
            for h in range(HEADS)
        ]
    )


def state_back_kernel(live_ref, cq_ref, sq_ref, scq_ref, sk_ref, sv_ref, tk_ref, tv_ref,
                      co_ref, so_ref, io_ref, cl_ref, sl_ref, il_ref, cg_ref, sg_ref, ig_ref, before_ref,
                      gcq_ref, gsq_ref, gscq_ref, gsk_ref, gsv_ref, gtk_ref, gtv_ref):
    rows = cq_ref.shape[0]
    mask = lax.broadcasted_iota(jnp.int32, (rows, rows), 0) < live_ref[0]
    for h in range(HEADS):
        cols_h = head_cols(h)
        terms = []

        def put_into(gq_ref):
            def put(grad_q, grad_k, grad_v):
                gq_ref[:, cols_h] = grad_q
                terms.append((grad_k, grad_v))

            return put

        attend_all_back(
            [
                (q_ref[:, cols_h], k_ref[:, cols_h], v_ref[:, cols_h], which, l_ref[h], o_ref[:, cols_h], g_ref[:, cols_h], put_into(gq_ref))
                for q_ref, k_ref, v_ref, o_ref, l_ref, g_ref, gq_ref, which in (
                    (cq_ref, sk_ref, sv_ref, co_ref, cl_ref, cg_ref, gcq_ref, None),
                    (sq_ref, sk_ref, sv_ref, so_ref, sl_ref, sg_ref, gsq_ref, None),
                    (scq_ref, tk_ref, tv_ref, io_ref, il_ref, ig_ref, gscq_ref, mask),
                )
            ]
        )
        gsk_ref[:, cols_h] = narrow((terms[0][0] + terms[1][0]) * RAW_SCALE)
        gsv_ref[:, cols_h] = narrow(terms[0][1] + terms[1][1])
        gtk_ref[:, cols_h] = terms[2][0] * RAW_SCALE
        gtv_ref[:, cols_h] = terms[2][1]


def self_attention_back(projected, out, log, grad_attended, extra_k, extra_v, window, after=()):
    rows, width = projected.shape
    heads = width // 4 // HD
    extra = extra_k.shape[0]
    return launch(
        partial(self_back_kernel, window), [projected] * 3 + [out, log, grad_attended, extra_k, extra_v],
        after=after, name="self_attention_back", grid=(heads // HEADS,),
        in_specs=[column(rows, 0), column(rows, 2 * heads), column(rows, 3 * heads), column(rows, 0), stat(rows),
                  column(rows, 0), column(extra, 0), column(extra, 0)],
        out_specs=[column(rows, 0)] * 3, out_shape=[shaped((rows, width // 4))] * 3,
        scratch=[pltpu.VMEM((rows, HD * HEADS), F32)] * 2,
        flops=heads * 10 * 2304 * 256 * HD, exps=heads * 2304 * 256,
    )


def cross_attention_back(projected, state_side, out, log, grad_attended, block, after=()):
    rows, width = state_side.shape
    heads = width // 4 // HD
    return launch(
        cross_back_kernel, [projected, state_side, state_side, out, log, grad_attended],
        after=after, name="cross_attention_back", grid=(heads // HEADS,),
        in_specs=[block_column(rows, block, heads), column(rows, 2 * heads), column(rows, 3 * heads),
                  block_column(rows, block, 0), stat(rows), block_column(rows, block, heads)],
        out_specs=[block_column(rows, block, 0), column(rows, 0), column(rows, 0)],
        out_shape=[shaped((projected.shape[0], width // 4))] + [shaped((rows, width // 4))] * 2,
        flops=heads * 10 * rows * rows * HD, exps=heads * rows * rows,
    )


def state_attention_back(projected, state_side, live_keys, cross, inner_self, inner_cross, grad_attended, grad_inner, before, block, after=()):
    rows, width = state_side.shape
    heads = width // 4 // HD
    grad, wide = shaped((rows, width // 4)), shaped((rows, width // 4), F32)
    return launch(
        state_back_kernel,
        [live_keys, projected] + [state_side] * 4 + [projected] * 2
        + [cross[0], inner_self[0], inner_cross[0], cross[1], inner_self[1], inner_cross[1]]
        + [grad_attended, grad_inner, grad_inner, before],
        after=after, name="state_attention_back", grid=(heads // HEADS,),
        in_specs=[SMEM, block_column(rows, block, heads)] + [column(rows, part * heads) for part in range(4)]
        + [block_column(rows, block, 2 * heads), block_column(rows, block, 3 * heads)]
        + [block_column(rows, block, 0), column(rows, 0), column(rows, 0)] + [stat(rows)] * 3
        + [block_column(rows, block, heads), column(rows, 0), column(rows, heads), pl.BlockSpec(memory_space=pl.ANY)],
        out_specs=[block_column(rows, block, 0)] + [column(rows, 0)] * 6,
        out_shape=[shaped((projected.shape[0], width // 4))] + [grad] * 4 + [wide] * 2,
        aliases={17: 0},
        flops=heads * 30 * rows * rows * HD, exps=3 * heads * rows * rows,
    )


def swap(values, axis):
    if axis == "y":
        return lax.ppermute(values, "fsdp", [(0, 1), (1, 0)])
    bit = {"core": 1, "x": 2, "z_low": 4, "z_high": 8, "z_far": 12}[axis]
    return lax.ppermute(values, "dp", [(d, d ^ bit) for d in range(16)])


LINES = [[line + 4 * z for z in range(4)] for line in range(4)]


def place():
    if not paired():
        return jnp.zeros((4,), jnp.int32)
    dp = lax.axis_index("dp")
    return jnp.stack([(dp // 2) % 2, dp % 2, lax.axis_index("fsdp"), dp // 4]).astype(jnp.int32)


def fence_kernel(*refs):
    pass


def fence(arrays, after):
    return launch(
        fence_kernel, arrays, after=after, name="fence", grid=(1,),
        in_specs=[pl.BlockSpec(memory_space=pl.ANY)] * len(arrays),
        out_specs=[pl.BlockSpec(memory_space=pl.ANY)] * len(arrays),
        out_shape=[shaped(item.shape, item.dtype) for item in arrays],
        aliases={i: i for i in range(len(arrays))}, flops=0,
    )


def stacked(block):
    return [block[:, i : i + COLS] for i in range(0, block.shape[1], COLS)]


def gather_blocks(blocks):
    packed = jnp.concatenate([part for block in blocks for part in stacked(block)], axis=0)
    return cut(lax.all_gather(packed, ("dp", "fsdp"), axis=0).reshape(16, 2, *packed.shape), blocks)


def cut(every, blocks):
    weights, row = [], 0
    for block in blocks:
        weights.append((every, row, block.shape[0]))
        row += block.shape[0] * block.shape[1] // COLS
    return weights


def spell_kernel(place_ref, *refs):
    x, core, y = place_ref[0], place_ref[1], place_ref[2]
    pieces, out = refs[:-1], refs[-1]
    for other in range(2):
        line, over_x, over_y, low, high = pieces[5 * other : 5 * other + 5]
        at = core ^ other
        out[0, x, at, y] = line[0]
        out[0, 1 - x, at, y] = over_x[0]
        out[0, x, at, 1 - y] = over_y[0]
        far = jnp.where(pl.program_id(0) < 2, low[0], high[0])
        out[0, 1 - x, at, 1 - y] = far


def fence_kernel(*refs):
    pass


def fence(arrays, after):
    return launch(
        fence_kernel, arrays, after=after, name="fence", grid=(1,),
        in_specs=[pl.BlockSpec(memory_space=pl.ANY)] * len(arrays),
        out_specs=[pl.BlockSpec(memory_space=pl.ANY)] * len(arrays),
        out_shape=[shaped(item.shape, item.dtype) for item in arrays],
        aliases={i: i for i in range(len(arrays))}, flops=0,
    )


class Gather:
    def __init__(self, blocks, where):
        self.where, self.blocks = where, blocks
        self.packed = jnp.concatenate([part for block in blocks for part in stacked(block)], axis=0)

    def start(self, after):
        packed = fence([self.packed], after)[0] if after else self.packed
        self.line = jnp.stack([packed] + [swap(packed, axis) for axis in ("z_low", "z_high", "z_far")])
        return (packed,)

    def near(self, after):
        (line,) = fence([self.line], after)
        self.over = swap(line, "x"), swap(line, "y")
        self.pieces = [line]
        return (line,)

    def far(self, after):
        over_x, over_y = fence(self.over, after)
        self.last = swap(over_x[:2], "y"), swap(over_y[2:], "x")
        self.pieces += [over_x, over_y]
        return (over_x,)

    def cross(self, after):
        low, high = fence(self.last, after)
        self.pieces += [low, high]
        self.pieces += [swap(piece, "core") for piece in self.pieces]
        return (low,)

    def whole(self, after):
        rows = self.packed.shape[0]

        def spec(low, high):
            return pl.BlockSpec((1, rows, COLS), lambda i, p: (jnp.clip(i, low, high - 1) - low, 0, 0))

        (every,) = launch(
            spell_kernel, self.pieces, where=self.where, after=after, name="spell", grid=(4,),
            in_specs=[spec(0, 4), spec(0, 4), spec(0, 4), spec(0, 2), spec(2, 4)] * 2,
            out_specs=[pl.BlockSpec((1, 2, 2, 2, rows, COLS), lambda i, p: (i ^ p[3], 0, 0, 0, 0, 0))],
            out_shape=[shaped((4, 2, 2, 2, rows, COLS))], flops=0,
        )
        return cut(every.reshape(16, 2, rows, COLS), self.blocks)


def add(*terms):
    return sum(term.astype(F32) for term in terms)


def fold_core_kernel(place_ref, keep_ref, come_ref, low_ref, high_ref, px_ref, py_ref, own_ref):
    x, y = place_ref[0], place_ref[2]
    cols = own_ref.shape[-1]

    def fold(out, dx, dy):
        at = pl.ds(pl.multiple_of((y ^ dy) * cols, 128), cols)
        for z in range(out.shape[0]):
            out[z] = narrow(add(keep_ref[z, x ^ dx, :, at], come_ref[z, x ^ dx, :, at]))

    fold(own_ref, 0, 0)
    fold(px_ref, 1, 0)
    fold(py_ref, 0, 1)
    pl.when(pl.program_id(0) == 0)(lambda: fold(low_ref, 1, 1))
    pl.when(pl.program_id(0) == 1)(lambda: fold(high_ref, 1, 1))


def fold_core(keep, come, where, after=()):
    _, _, rows, cols = keep.shape
    pair = pl.BlockSpec((2, 2, rows, cols), lambda i, p: (i, 0, 0, 0))
    full = pl.BlockSpec((2, rows, cols // 2), lambda i, p: (i, 0, 0))
    half = pl.BlockSpec((2, rows, cols // 2), lambda i, p: (0, 0, 0))
    return launch(
        fold_core_kernel, [keep, come], where=where, after=after, name="fold_core", grid=(2,),
        in_specs=[pair, pair], out_specs=[half, half, full, full, full],
        out_shape=[shaped((2, rows, cols // 2))] * 2 + [shaped((4, rows, cols // 2))] * 3,
        flops=keep.size,
    )


def fold_mid_kernel(px_ref, py_ref, rx_ref, ry_ref, px_out, py_out):
    px_out[...] = narrow(add(px_ref[...], ry_ref[...]))
    py_out[...] = narrow(add(py_ref[...], rx_ref[...]))


def fold_mid(px, py, rx, ry, after=()):
    block = rx.shape
    low = pl.BlockSpec(block, lambda i: (0, 0, 0))
    high = pl.BlockSpec(block, lambda i: (1, 0, 0))
    return launch(
        fold_mid_kernel, [px, py, rx, ry], after=after, name="fold_mid", grid=(1,),
        in_specs=[high, low, low, low], out_specs=[high, low],
        out_shape=[shaped(px.shape), shaped(py.shape)], aliases={0: 0, 1: 1}, flops=px.size,
    )


def fold_last_kernel(own_ref, rx_ref, ry_ref, out_ref):
    out_ref[...] = narrow(add(own_ref[...], rx_ref[...], ry_ref[...]))


def fold_last(own, rx, ry, after=()):
    _, rows, cols = own.shape
    block = pl.BlockSpec((2, rows, cols), lambda i: (i, 0, 0))
    return launch(
        fold_last_kernel, [own, rx, ry], after=after, name="fold_last", grid=(2,),
        in_specs=[block] * 3, out_specs=[block], out_shape=[shaped(own.shape)], flops=2 * own.size,
    )[0]


def widen_kernel(cuts, sum_ref, *outs):
    for out, (row, rows, parts, cols) in zip(outs, cuts):
        for part in range(parts):
            out[part * rows : (part + 1) * rows, :] = sum_ref[
                row : row + rows, part * cols : (part + 1) * cols
            ].astype(F32)


class Scatter:
    def __init__(self, keep, send, where):
        self.where, self.keep = where, keep
        self.come = swap(send, "core")

    def core(self, after):
        low, high, self.px, self.py, self.own = fold_core(self.keep, self.come, self.where, after)
        self.rx, self.ry = swap(low, "x"), swap(high, "y")
        return (self.own,)

    def mid(self, after):
        px, py = fold_mid(self.px, self.py, self.rx, self.ry, after)
        self.one, self.two = swap(px, "x"), swap(py, "y")
        return (px,)

    def last(self, after):
        line = fold_last(self.own, self.one, self.two, after)
        rows, cols = line.shape[1:]
        self.out = lax.psum_scatter(
            line.reshape(4 * rows, cols), "dp", scatter_dimension=0, axis_index_groups=LINES, tiled=True
        )
        return (line,)

    def widen(self, cuts, after):
        outs = launch(
            partial(widen_kernel, cuts), [self.out], after=after, name="widen", grid=(1,),
            in_specs=[whole(self.out.shape)], out_specs=[whole((rows * parts, cols)) for _, rows, parts, cols in cuts],
            out_shape=[shaped((rows * parts, cols), F32) for _, rows, parts, cols in cuts], flops=0,
        )
        return outs


def paired():
    return lax.axis_size("dp") == 16 and lax.axis_size("fsdp") == 2


def gather_plain(block):
    full = lax.all_gather(lax.all_gather(block, "fsdp", axis=1, tiled=True), "dp", axis=0, tiled=True)
    rows, cols = full.shape[0] // 16, full.shape[1]
    cut = full.reshape(16, rows, 2, cols // 2 // COLS, COLS).transpose(0, 2, 3, 1, 4)
    return cut.reshape(16, 2, -1, COLS), 0, rows


def scatter_plain(grad):
    rows = lax.psum_scatter(grad, "dp", scatter_dimension=0, tiled=True)
    return lax.psum_scatter(rows, "fsdp", scatter_dimension=1, tiled=True)


def gather_vectors(vectors):
    if not paired():
        return lax.all_gather(vectors, "fsdp", axis=1, tiled=True).astype(F32)
    other = swap(vectors, "y")
    first = lax.axis_index("fsdp") == 0
    return jnp.concatenate(
        [jnp.where(first, vectors, other), jnp.where(first, other, vectors)], axis=1
    ).astype(F32)


def scatter_vectors(vectors):
    part = vectors.shape[1] // lax.axis_size("fsdp")
    y = lax.axis_index("fsdp")
    if not paired():
        total = lax.psum(vectors, ("dp", "fsdp"))
        return lax.dynamic_slice_in_dim(total, y * part, part, axis=1)
    low, high = vectors[:, :part], vectors[:, part:]
    total = jnp.where(y == 0, low, high) + swap(jnp.where(y == 0, high, low), "y")
    for axis in ("core", "x", "z_low", "z_high"):
        total = total + swap(total, axis)
    return total


def shards(
    tokens,
    incoming,
    document_lengths,
    output_grad,
    token_proj,
    state_proj,
    token_out,
    state_out,
    gate_weight,
    init_state,
    hidden_in,
    hidden_out,
    token_gain,
    state_gain,
    hidden_gain,
    gate_bias,
):
    seg_len, width = tokens.shape
    window = WINDOW
    states = incoming.shape[1]
    where = place()
    segment_id = lax.axis_index(("dp", "fsdp"))
    counts = (document_lengths + seg_len - 1) // seg_len
    ends = jnp.cumsum(counts)
    starts = ends - counts
    inside = (segment_id >= starts) & (segment_id < ends)
    valid_len = jnp.sum(
        jnp.where(
            inside, jnp.minimum(seg_len, document_lengths - (segment_id - starts) * seg_len), 0
        )
    )
    first = jnp.any(segment_id == starts)
    lives = [jnp.where(b * window < valid_len, 1.0, 0.0).astype(F32).reshape(1) for b in range(2)]
    live_keys = [jnp.clip(valid_len - b * window, 0, window).astype(jnp.int32).reshape(1) for b in range(2)]

    gains = gather_vectors(jnp.stack([token_gain, state_gain, hidden_gain, gate_bias]))
    token_gain_f, state_gain_f, hidden_gain_f, gate_bias_f = [gains[i : i + 1] for i in range(4)]
    order = ()

    if paired():
        first_gather, second_gather = Gather([token_proj], where), Gather([state_proj, init_state], where)
        order = first_gather.start(order)
        order = first_gather.near(order)
        order = second_gather.start(order)
        order = first_gather.far(order)
        order = second_gather.near(order)
        order = first_gather.cross(order)
        (full_token_proj,) = first_gather.whole(order)
        full_hidden_in, full_state_out, full_token_out, full_gate_weight = gather_blocks(
            [hidden_in, state_out, token_out, gate_weight]
        )
        (full_hidden_out,) = gather_blocks([hidden_out])
    else:
        (
            full_token_proj, full_state_proj, full_state_out, full_gate_weight, full_init, full_token_out, full_hidden_in,
            full_hidden_out,
        ) = [
            gather_plain(block)
            for block in (
                token_proj, state_proj, state_out, gate_weight, init_state, token_out, hidden_in, hidden_out,
            )
        ]
    normed, projected = norm_project(tokens, token_gain_f, full_token_proj, order)
    order = (projected,)
    if paired():
        order = second_gather.far(order)
    self_out, self_log = self_attention(projected, window, order)
    order = (self_log,)
    if paired():
        order = second_gather.cross(order)
        full_state_proj, full_init = second_gather.whole(order)
    array, row, rows = full_init
    full_init = array[:, :, row : row + rows].transpose(0, 2, 1, 3).reshape(states, width)
    state_0 = jnp.where(first, full_init, incoming[0]).astype(F32)
    normed_0, side_0 = norm_project(state_0, state_gain_f, full_state_proj, order)
    order = (side_0,)
    inner_self_0, inner_cross_0, inner_self_log, inner_cross_log = inner_attention(
        projected, side_0, live_keys[0], 0, order
    )
    order = (inner_self_log,)
    mixed_0, gate_0, state_1 = update_state(
        lives[0], inner_self_0, inner_cross_0, full_state_out, full_gate_weight, gate_bias_f, state_0, order
    )
    order = (mixed_0,)
    normed_1, side_1 = norm_project(state_1, state_gain_f, full_state_proj, order)
    order = (normed_1,)
    cross_out, cross_log_0 = cross_attention(projected, side_0, 0, None, order)
    order = (cross_log_0,)
    cross_out, cross_log_1 = cross_attention(projected, side_1, 1, cross_out, order)
    order = (cross_log_1,)
    middle, hidden_normed = branch(self_out, cross_out, full_token_out, tokens, hidden_gain_f, order)
    order = (hidden_normed,)
    active, slope = hidden(hidden_normed, full_hidden_in, order)
    order = (active,)

    scatters = {}

    def weight(name, *jobs, extra=None):
        nonlocal order
        if paired():
            keep, send = weight_grad(jobs, where, "grad_" + name, extra, order)
            scatters[name] = Scatter(keep, send, where)
            order = (keep,)
            return
        scatters[name] = []
        for lefts, rights, plan, split in jobs:
            if split:
                lefts = [jnp.concatenate(lefts, axis=1)]
            grad = jnp.concatenate(
                [sum(matmul_left_t(lefts[a], rights[b]) for a, b in terms) for terms in plan], axis=1
            )
            scatters[name].append(scatter_plain(narrow(grad)).astype(F32))
        if extra is not None:
            scatters[name].append(scatter_plain(extra).astype(F32))

    def sums(name, *cuts):
        nonlocal order
        if not paired():
            return scatters[name]
        outs = scatters[name].widen(cuts, order)
        order = (outs[0],)
        return outs

    def fold(name, step):
        nonlocal order
        if paired():
            order = getattr(scatters[name], step)(order)

    one = [[(0, 0)]]
    weight("hidden_out", ([active], [output_grad], one, False))
    result, grad_pre = result_and_pre(active, slope, full_hidden_out, middle, output_grad, order)
    order = (result,)
    fold("hidden_out", "core")
    weight("hidden_in", ([hidden_normed], [grad_pre], one, False))
    fold("hidden_out", "mid")
    grad_hidden_gain, grad_branch, grad_middle = norm_back_project(
        [grad_pre], full_hidden_in, middle, hidden_gain_f, output_grad, "hidden_back", True, after=order
    )
    order = (grad_hidden_gain,)
    fold("hidden_in", "core")
    fold("hidden_out", "last")
    grad_attended = spread(grad_branch, full_token_out, order)
    order = (grad_attended,)
    grad_cross, grad_keys_1, grad_values_1 = cross_attention_back(
        projected, side_1, cross_out, cross_log_1, grad_attended, 1, order
    )
    order = (grad_keys_1,)
    fold("hidden_in", "mid")
    no_term = jnp.zeros((states, width), jnp.bfloat16)
    grad_state_gain_1, _, grad_state_1 = norm_back_project(
        [grad_keys_1, grad_values_1], full_state_proj, state_1, state_gain_f, no_term, "side_back", True,
        offset=2 * width, after=order,
    )
    order = (grad_state_gain_1,)
    grad_gate_low, grad_mixed, grad_inner, grad_direct, grad_gate_bias = gate_back(
        lives[0], grad_state_1, gate_0, state_0, mixed_0, full_gate_weight, full_state_out, order
    )
    order = (grad_gate_bias,)
    weight(
        "out",
        ([self_out, cross_out], [grad_branch], one, True),
        ([inner_self_0, inner_cross_0], [grad_mixed], one, True),
        ([mixed_0], [grad_gate_low], one, False),
    )
    parts = state_attention_back(
        projected, side_0, live_keys[0], (cross_out, cross_log_0), (inner_self_0, inner_self_log),
        (inner_cross_0, inner_cross_log), grad_attended, grad_inner, grad_cross, 0, order,
    )
    grad_cross, grads_side_0, extra_keys, extra_values = parts[0], parts[1:5], parts[5], parts[6]
    order = (extra_keys,)
    fold("hidden_in", "last")
    fold("out", "core")
    (hidden_out_sum,) = sums("hidden_out", (0, 256, 1, 512))
    grad_state_gain_0, grad_init = norm_back_project(
        grads_side_0, full_state_proj, state_0, state_gain_f, grad_direct, "state_back",
        scale=jnp.where(first, 1.0, 0.0).astype(F32).reshape(1), after=order,
    )
    order = (grad_state_gain_0,)
    fold("out", "mid")
    weight(
        "state_proj",
        (
            [normed_0, normed_1],
            [*grads_side_0, grad_keys_1, grad_values_1],
            [[(0, 0)], [(0, 1)], [(0, 2), (1, 4)], [(0, 3), (1, 5)]],
            False,
        ),
        extra=grad_init,
    )
    grad_self, grad_keys, grad_values = self_attention_back(
        projected, self_out, self_log, grad_attended, extra_keys, extra_values, window, order
    )
    order = (grad_self,)
    fold("state_proj", "core")
    fold("out", "last")
    (hidden_in_sum,) = sums("hidden_in", (0, 64, 1, 2048))
    grads_projected = [grad_self, grad_cross, grad_keys, grad_values]
    weight("token_proj", ([normed], grads_projected, [[(0, i)] for i in range(4)], False))
    fold("state_proj", "mid")
    fold("token_proj", "core")
    grad_token_gain, tokens_grad = norm_back_project(
        grads_projected, full_token_proj, tokens, token_gain_f, grad_middle, "tokens_back", after=order
    )
    order = (grad_token_gain,)
    fold("token_proj", "mid")
    fold("state_proj", "last")
    token_out_sum, state_out_sum, gate_sum = sums("out", (0, 128, 1, 512), (128, 128, 1, 512), (256, 64, 1, 512))
    inner_self_1, inner_cross_1, log, _ = inner_attention(projected, side_1, live_keys[1], 1, order)
    order = (log,)
    fold("token_proj", "last")
    _, _, state_2 = update_state(
        lives[1], inner_self_1, inner_cross_1, full_state_out, full_gate_weight, gate_bias_f, state_1, order
    )
    order = (state_2,)
    state_proj_sum, init_sum = sums("state_proj", (0, 64, 1, 2048), (64, 16, 2, 512))
    (token_proj_sum,) = sums("token_proj", (0, 64, 1, 2048))
    vector_grads = scatter_vectors(
        jnp.concatenate(
            [grad_token_gain, grad_state_gain_0 + grad_state_gain_1, grad_hidden_gain, grad_gate_bias], axis=0
        )
    )
    matrix_grads = [
        token_proj_sum, state_proj_sum, token_out_sum, state_out_sum, gate_sum, init_sum, hidden_in_sum, hidden_out_sum,
    ]
    return (
        result,
        narrow(state_2)[None],
        tokens_grad,
        *matrix_grads,
        *[vector_grads[i] for i in range(4)],
    )


def solution(mesh):
    return jax.shard_map(
        shards,
        mesh=mesh,
        in_specs=(
            P(("dp", "fsdp"), None),
            P(("dp", "fsdp"), None, None),
            P(),
            P(("dp", "fsdp"), None),
            P("dp", "fsdp"),
            P("dp", "fsdp"),
            P("dp", "fsdp"),
            P("dp", "fsdp"),
            P("dp", "fsdp"),
            P("dp", "fsdp"),
            P("dp", "fsdp"),
            P("dp", "fsdp"),
            P("fsdp"),
            P("fsdp"),
            P("fsdp"),
            P("fsdp"),
        ),
        out_specs=(
            P(("dp", "fsdp"), None),
            P(("dp", "fsdp"), None, None),
            P(("dp", "fsdp"), None),
            P("dp", "fsdp"),
            P("dp", "fsdp"),
            P("dp", "fsdp"),
            P("dp", "fsdp"),
            P("dp", "fsdp"),
            P("dp", "fsdp"),
            P("dp", "fsdp"),
            P("dp", "fsdp"),
            P("fsdp"),
            P("fsdp"),
            P("fsdp"),
            P("fsdp"),
        ),
        check_vma=False,
    )
```

```python
from functools import partial
import math

import jax
import jax.numpy as jnp
from jax import lax
from jax.experimental import pallas as pl
from jax.experimental.pallas import tpu as pltpu
from jax.sharding import PartitionSpec as P

HD = 128
WINDOW = 512
MIB = 1 << 20


norm_eps = 1e-06
masked_score = -1e30
EXP_SCALE = math.log2(math.e) / math.sqrt(HD)
RAW_SCALE = 1.0 / math.sqrt(HD)
NT = (((1,), (1,)), ((), ()))
TN = (((0,), (0,)), ((), ()))
NN = (((1,), (0,)), ((), ()))


def narrow(values):
    return values.astype(jnp.bfloat16)


def matmul_left_t(left, right):
    return lax.dot_general(left, right, TN, preferred_element_type=jnp.float32)


MICROSECOND = 1.15e9
def launch(body, operands, *, grid, in_specs, out_specs, out_shape, us, flops, after=(), where=None, scratch=(), aliases=None, exps=0, limit=48):
    count = len(operands)
    late = len(after)
    lead = 0 if where is None else 1

    def run(*refs):
        body(*refs[: lead + count], *refs[lead + count + late :])

    specs = list(in_specs) + [pl.BlockSpec(memory_space=pl.ANY)] * late
    size = sum(math.prod(item.shape) * item.dtype.itemsize for item in (*operands, *out_shape))
    kwargs = dict(grid=grid, in_specs=specs, out_specs=list(out_specs))
    if where is None:
        kwargs["scratch_shapes"] = list(scratch)
    else:
        kwargs = dict(
            grid_spec=pltpu.PrefetchScalarGridSpec(
                num_scalar_prefetch=1, scratch_shapes=list(scratch), **kwargs
            )
        )
    return pl.pallas_call(
        run,
        out_shape=list(out_shape),
        input_output_aliases=aliases or {},
        compiler_params=pltpu.CompilerParams(vmem_limit_bytes=limit * MIB),
        cost_estimate=pl.CostEstimate(flops=int(MICROSECOND * us), bytes_accessed=1024, transcendentals=0),
        name=getattr(body, "func", body).__name__,
        **kwargs,
    )(*(() if where is None else (where,)), *operands, *after)


def shaped(shape, dtype=jnp.bfloat16):
    return jax.ShapeDtypeStruct(shape, dtype)


def whole(shape):
    return pl.BlockSpec(shape, lambda *ids: (0,) * len(shape))


SMEM = pl.BlockSpec(memory_space=pltpu.SMEM)
F32 = jnp.float32


def norm_rows(values):
    centered = values - jnp.mean(values, axis=-1, keepdims=True)
    return centered, lax.rsqrt(jnp.mean(centered * centered, axis=-1, keepdims=True) + norm_eps)


def norm_back_rows(values, gain, grad):
    centered, inverse = norm_rows(values)
    normal = centered * inverse
    scaled = grad * gain
    mean = jnp.mean(scaled, axis=-1, keepdims=True)
    along = jnp.mean(scaled * normal, axis=-1, keepdims=True)
    return inverse * (scaled - mean - normal * along), jnp.sum(grad * normal, axis=0, keepdims=True)


ROWS = 128
COLS = 512


STEP = 2 * COLS


def group_spec(weight, group):
    array, start, rows = weight

    def place_of(*ids):
        which = group(ids[0])
        return 0, which // 2, start // (2 * rows) + which % 2, 0

    return pl.BlockSpec((16, 1, 2 * rows, COLS), place_of)


def group(w_ref, which):
    rows = w_ref.shape[2] // 2
    return w_ref[:, 0, which * rows : (which + 1) * rows, :].reshape(-1, COLS)


def cols(which):
    return slice(which * COLS, (which + 1) * COLS)


def rows_spec(weight, count, step=lambda i: i):
    array, start, rows = weight
    return pl.BlockSpec((count, 2, rows, COLS), lambda *ids: (step(ids[0]), 0, start // rows, 0))


def side(w_ref, y, blocks=slice(None)):
    values = w_ref[blocks, y]
    return values.reshape(-1, COLS)


def times(left, w_ref, blocks=slice(None)):
    return jnp.concatenate([dot(left, side(w_ref, y, blocks), NN) for y in range(2)], axis=1)


def times_turned(left, w_ref):
    return sum(dot(left[:, y * COLS : (y + 1) * COLS], side(w_ref, y), NT) for y in range(2))


def norm_project_kernel(x_ref, gain_ref, w_ref, normed_ref, out_ref):
    @pl.when(pl.program_id(0) == 0)
    def _():
        @pl.loop(0, x_ref.shape[0] // ROWS)
        def _(i):
            at = pl.ds(pl.multiple_of(i * ROWS, ROWS), ROWS)
            centered, inverse = norm_rows(x_ref[at, :].astype(F32))
            normed_ref[at, :] = narrow(centered * inverse * gain_ref[...])

    for which in range(2):
        out_ref[:, cols(which)] = narrow(dot(normed_ref[...], group(w_ref, which), NN))


def norm_project(x, gain, weight, after=()):
    rows, width = x.shape
    total_cols = 4 * width
    step = STEP
    return launch(
        norm_project_kernel, [x, gain, weight[0]], after=after, us=13, grid=(total_cols // step,),
        in_specs=[whole((rows, width)), whole((1, width)), group_spec(weight, lambda i: i)],
        out_specs=[whole((rows, width)), pl.BlockSpec((rows, step), lambda i: (0, i))],
        out_shape=[shaped((rows, width)), shaped((rows, total_cols))],
        flops=2 * rows * width * total_cols,
    )


def update_kernel(live_ref, self_ref, cross_ref, out_w_ref, gate_w_ref, bias_ref, state_ref, mixed_ref, gate_ref, new_ref):
    low, high = slice(0, 8), slice(8, 16)
    mixed = narrow(times(self_ref[...], out_w_ref, low) + times(cross_ref[...], out_w_ref, high))
    mixed_ref[...] = mixed
    gate = jax.nn.sigmoid(times(mixed, gate_w_ref) + bias_ref[...])
    gate_ref[...] = gate
    state = state_ref[...]
    updated = gate * state + (1.0 - gate) * jnp.tanh(mixed.astype(F32))
    new_ref[...] = state + live_ref[0] * (updated - state)


def update_state(live, inner_self, inner_cross, state_out, gate_weight, bias, state, after=()):
    rows, width = state.shape
    step = 256
    tile = pl.BlockSpec((step, width), lambda i: (i, 0))
    return launch(
        update_kernel, [live, inner_self, inner_cross, state_out[0], gate_weight[0], bias, state],
        after=after, us=9, grid=(rows // step,),
        in_specs=[SMEM, tile, tile, rows_spec(state_out, 16, lambda i: 0), rows_spec(gate_weight, 16, lambda i: 0), whole((1, width)), tile],
        out_specs=[tile, tile, tile],
        out_shape=[shaped((rows, width)), shaped((rows, width), F32), shaped((rows, width), F32)],
        flops=6 * rows * width * width, exps=2 * rows * width,
    )


def branch_kernel(self_ref, cross_ref, w_ref, x_ref, gain_ref, middle_ref, normed_ref):
    low, high = slice(0, 8), slice(8, 16)
    middle = x_ref[...].astype(F32) + (times(self_ref[...], w_ref, low) + times(cross_ref[...], w_ref, high))
    middle_ref[...] = middle
    centered, inverse = norm_rows(middle)
    normed_ref[...] = narrow(centered * inverse * gain_ref[...])


def branch(self_out, cross_out, token_out, x, gain, after=()):
    rows, width = x.shape
    step = 256
    tile = pl.BlockSpec((step, width), lambda i: (i, 0))
    return launch(
        branch_kernel, [self_out, cross_out, token_out[0], x, gain], after=after, us=10, grid=(rows // step,),
        in_specs=[tile, tile, rows_spec(token_out, 16, lambda i: 0), tile, whole((1, width))],
        out_specs=[tile, tile],
        out_shape=[shaped((rows, width), F32), shaped((rows, width))],
        flops=4 * rows * width * width,
    )


GELU_A = math.sqrt(2.0 / math.pi)
GELU_B = 0.044715


def hidden_kernel(normed_ref, w_ref, active_ref, slope_ref):
    for start in range(0, normed_ref.shape[0], 256):
        for which in range(2):
            at = slice(start, start + 256), cols(which)
            v = dot(normed_ref[start : start + 256, :], group(w_ref, which), NN)
            square = v * v
            t = jnp.tanh(v * (GELU_A + (GELU_A * GELU_B) * square))
            half = 0.5 + 0.5 * t
            active_ref[at] = narrow(v * half)
            slope = half + v * (1.0 - t * t) * (0.5 * GELU_A + (1.5 * GELU_A * GELU_B) * square)
            slope_ref[at] = narrow(slope)


def hidden(normed, weight, after=()):
    rows, width = normed.shape
    total_cols = 4 * width
    step = STEP
    tile = pl.BlockSpec((rows, step), lambda i: (0, i))
    return launch(
        hidden_kernel, [normed, weight[0]], after=after, us=20, grid=(total_cols // step,),
        in_specs=[whole((rows, width)), group_spec(weight, lambda i: i)],
        out_specs=[tile, tile], out_shape=[shaped((rows, total_cols))] * 2,
        flops=2 * rows * width * total_cols, exps=rows * total_cols,
    )


def result_kernel(active_ref, slope_ref, w_ref, middle_ref, grad_ref, result_ref, pre_ref, total_ref):
    first = pl.program_id(0) == 0
    for start in range(0, active_ref.shape[0], 256):
        at = slice(start, start + 256)
        pre_ref[at, :] = narrow(times_turned(grad_ref[at, :], w_ref) * slope_ref[at, :].astype(F32))
        total_ref[at, :] = jnp.where(first, middle_ref[at, :], total_ref[at, :]) + times(active_ref[at, :], w_ref)

    @pl.when(pl.program_id(0) == pl.num_programs(0) - 1)
    def _():
        result_ref[...] = narrow(total_ref[...])


def result_and_pre(active, slope, weight, middle, grad, after=()):
    rows, hidden_units = active.shape
    width = middle.shape[1]
    step = STEP
    tile = pl.BlockSpec((rows, step), lambda i: (0, i))
    return launch(
        result_kernel, [active, slope, weight[0], middle, grad], after=after, us=40,
        grid=(hidden_units // step,),
        in_specs=[tile, tile, rows_spec(weight, step // weight[2]), whole((rows, width)), whole((rows, width))],
        out_specs=[whole((rows, width)), tile],
        out_shape=[shaped((rows, width)), shaped((rows, hidden_units))],
        scratch=[pltpu.VMEM((rows, width), F32)],
        flops=4 * rows * width * hidden_units,
    )


def norm_back_kernel(parts, keep_wide, scale_ref, *refs):
    grads, (w_ref, x_ref, gain_ref, plus_ref) = refs[:parts], refs[parts : parts + 4]
    outs, total_ref = refs[parts + 4 : -1], refs[-1]
    i = pl.program_id(0)
    share = pl.num_programs(0) // parts

    @pl.when(i == 0)
    def _():
        total_ref[...] = jnp.zeros_like(total_ref)

    for part in range(parts):
        @pl.when(i // share == part)
        def _():
            total_ref[...] += sum(dot(grads[part][:, cols(which)], group(w_ref, which), NT) for which in range(2))

    @pl.when(i == pl.num_programs(0) - 1)
    def _():
        outs[0][...] = jnp.zeros_like(outs[0])

        @pl.loop(0, x_ref.shape[0] // ROWS)
        def _(j):
            at = pl.ds(pl.multiple_of(j * ROWS, ROWS), ROWS)
            grad, gain_grad = norm_back_rows(x_ref[at, :].astype(F32), gain_ref[...], total_ref[at, :])
            grad = grad + plus_ref[at, :].astype(F32)
            outs[0][...] += gain_grad
            outs[1][at, :] = narrow(jnp.where(scale_ref[0] > 0.0, grad, 0.0))
            if keep_wide:
                outs[2][at, :] = grad


def norm_back_project(grads, weight, x, gain, plus, us, keep_wide=False, offset=0, scale=None, after=()):
    rows, width = x.shape
    step = STEP
    share = grads[0].shape[1] // step
    parts = len(grads)
    steps = parts * share
    def part_spec(part):
        return pl.BlockSpec((rows, step), lambda i: (0, jnp.clip(i - part * share, 0, share - 1)))
    out_shape = [shaped((1, width), F32), shaped((rows, width))]
    if keep_wide:
        out_shape.append(shaped((rows, width), F32))
    if scale is None:
        scale = jnp.ones((1,), F32)
    return launch(
        partial(norm_back_kernel, parts, keep_wide), [scale, *grads, weight[0], x, gain, plus], after=after, us=us,
        grid=(steps,),
        in_specs=[SMEM] + [part_spec(part) for part in range(parts)]
        + [group_spec(weight, lambda i: i + offset // step), whole((rows, width)), whole((1, width)), whole((rows, width))],
        out_specs=[whole(item.shape) for item in out_shape], out_shape=out_shape,
        scratch=[pltpu.VMEM((rows, width), F32)],
        flops=2 * rows * width * steps * step,
    )


def spread_kernel(grad_ref, w_ref, out_ref):
    out_ref[...] = narrow(times_turned(grad_ref[...], w_ref))


def spread(grad, weight, after=()):
    rows, width = grad.shape
    total_cols = 16 * weight[2]
    step = STEP
    return launch(
        spread_kernel, [grad, weight[0]], after=after, us=8, grid=(total_cols // step,),
        in_specs=[whole((rows, width)), rows_spec(weight, step // weight[2])],
        out_specs=[pl.BlockSpec((rows, step), lambda i: (0, i))],
        out_shape=[shaped((rows, total_cols))], flops=2 * rows * width * total_cols,
    )[0]


def gate_back_kernel(live_ref, grad_ref, gate_ref, state_ref, mixed_ref, gate_w_ref, out_w_ref,
                     pre_ref, grad_mixed_ref, inner_ref, direct_ref, bias_ref):
    grad, gate, live = grad_ref[...], gate_ref[...], live_ref[0]
    tanh_mixed = jnp.tanh(mixed_ref[...].astype(F32))
    updated = live * grad
    direct_ref[...] = (1.0 - live) * grad + updated * gate
    pre = gate * (1.0 - gate) * updated * (state_ref[...] - tanh_mixed)

    @pl.when(pl.program_id(0) == 0)
    def _():
        bias_ref[...] = jnp.zeros_like(bias_ref)

    bias_ref[...] += jnp.sum(pre, axis=0, keepdims=True)
    low = narrow(pre)
    pre_ref[...] = low
    grad_mixed = narrow(
        times_turned(low, gate_w_ref) + updated * (1.0 - gate) * (1.0 - tanh_mixed * tanh_mixed)
    )
    grad_mixed_ref[...] = grad_mixed
    inner_ref[...] = narrow(times_turned(grad_mixed, out_w_ref))


def gate_back(live, grad, gate, state, mixed, gate_weight, state_out, after=()):
    rows, width = grad.shape
    step = 256
    tile = pl.BlockSpec((step, width), lambda i: (i, 0))
    wide = pl.BlockSpec((step, 2 * width), lambda i: (i, 0))
    return launch(
        gate_back_kernel, [live, grad, gate, state, mixed, gate_weight[0], state_out[0]], after=after, us=9,
        grid=(rows // step,),
        in_specs=[SMEM, tile, tile, tile, tile, rows_spec(gate_weight, 16, lambda i: 0), rows_spec(state_out, 16, lambda i: 0)],
        out_specs=[tile, tile, wide, tile, whole((1, width))],
        out_shape=[shaped((rows, width)), shaped((rows, width)), shaped((rows, 2 * width)), shaped((rows, width), F32), shaped((1, width), F32)],
        flops=6 * rows * width * width, exps=rows * width,
    )


def weight_grad_kernel(jobs, counts, extra, place_ref, *refs):
    lefts, rights = refs[: counts[0]], refs[counts[0] : counts[0] + counts[1]]
    keep_ref, send_ref = refs[-2], refs[-1]
    core = place_ref[1]
    z = pl.program_id(0)

    def run(plan, row, rows, pick):
        turned = {left: lefts[pick(left)][...].T for left in sorted({left for terms in plan for left, _ in terms})}
        col = 0
        for terms in plan:
            cols = rights[terms[0][1]].shape[1]
            for start in range(0, cols, 512):
                total = sum(
                    dot(turned[left], rights[right][:, start : start + 512], NN) for left, right in terms
                )
                total = narrow(total)
                at = slice(col + start, col + start + 512)
                for x in range(2):
                    even = total[2 * x * rows : (2 * x + 1) * rows]
                    odd = total[(2 * x + 1) * rows : (2 * x + 2) * rows]
                    keep_ref[0, x, row : row + rows, at] = jnp.where(core == 0, even, odd)
                    send_ref[0, x, row : row + rows, at] = jnp.where(core == 0, odd, even)
            col += cols

    for plan, split, row, rows in jobs:
        if split:
            pl.when(z < 2)(partial(run, plan, row, rows, lambda left: left))
            pl.when(z >= 2)(partial(run, plan, row, rows, lambda left: left + 1))
        else:
            run(plan, row, rows, lambda left: left)
    if extra is not None:
        source, row = refs[counts[0] + counts[1]], extra
        for x in range(2):
            for part in range(2):
                for y in range(2):
                    at = slice(y * 2048 + part * 512, y * 2048 + (part + 1) * 512)
                    even = source[0, x, 0, part * 16 : (part + 1) * 16, y * 512 : (y + 1) * 512]
                    odd = source[0, x, 1, part * 16 : (part + 1) * 16, y * 512 : (y + 1) * 512]
                    keep_ref[0, x, row : row + 16, at] = jnp.where(core == 0, even, odd)
                    send_ref[0, x, row : row + 16, at] = jnp.where(core == 0, odd, even)
            for y in range(2):
                at = slice(y * 2048 + 1024, (y + 1) * 2048)
                keep_ref[0, x, row : row + 16, at] = jnp.zeros((16, 1024), jnp.bfloat16)
                send_ref[0, x, row : row + 16, at] = jnp.zeros((16, 1024), jnp.bfloat16)


def weight_grad(jobs, where, us, extra=None, after=()):
    lefts, rights, specs, table, row = [], [], [], [], 0
    for these, those, plan, split in jobs:
        rows = these[0].shape[1] * (2 if split else 1) // 16
        shift = [[(left + len(lefts), right + len(rights)) for left, right in terms] for terms in plan]
        table.append((shift, split, row, rows))
        for index, item in enumerate(these):
            if split:
                block = (lambda z, p: (0, jnp.minimum(z, 1))) if index == 0 else (lambda z, p: (0, jnp.maximum(z, 2) - 2))
            else:
                block = lambda z, p: (0, z)
            specs.append(pl.BlockSpec((item.shape[0], 4 * rows), block))
        lefts += these
        rights += those
        row += rows
    cols = sum(rights[terms[0][1]].shape[1] for terms in table[0][0])
    operands = [*lefts, *rights]
    specs += [whole(item.shape) for item in rights]
    at = None
    if extra is not None:
        operands.append(extra.reshape(4, 2, 2, 32, extra.shape[1]))
        specs.append(pl.BlockSpec((1, 2, 2, 32, extra.shape[1]), lambda z, p: (z, 0, 0, 0, 0)))
        at, row = row, row + 16
    out = pl.BlockSpec((1, 2, row, cols), lambda z, p: (z, 0, 0, 0))
    return launch(
        partial(weight_grad_kernel, table, (len(lefts), len(rights)), at), operands,
        where=where, after=after, us=us, grid=(4,), in_specs=specs,
        out_specs=[out, out], out_shape=[shaped((4, 2, row, cols))] * 2,
        flops=2 * rights[0].shape[0] * 16 * row * cols, limit=56,
    )


def dot(a, b, dims):
    return lax.dot_general(a, b, dims, preferred_element_type=jnp.float32)


HEADS = 2
TILE = 256


def attend_all(items):
    scores = [dot(k, q, NT) for q, k, v, mask, put in items]
    scores = [
        part if item[3] is None else jnp.where(item[3], part, masked_score) for part, item in zip(scores, items)
    ]
    tops = [jnp.max(part, axis=0, keepdims=True) for part in scores]
    weights = [jnp.exp2((part - top) * EXP_SCALE) for part, top in zip(scores, tops)]
    totals = [jnp.sum(part, axis=0, keepdims=True) for part in weights]
    for (q, k, v, mask, put), top, part, total in zip(items, tops, weights, totals):
        mixed = dot(v, narrow(part), TN) / total
        put(narrow(mixed.T), top * EXP_SCALE + jnp.log2(total))


def attend_all_back(items):
    probs = [jnp.exp2(dot(k, q, NT) * EXP_SCALE - log) for q, k, v, mask, log, out, grad, put in items]
    probs = [part if item[3] is None else jnp.where(item[3], part, 0.0) for part, item in zip(probs, items)]
    deltas = [row_delta(out, grad) for q, k, v, mask, log, out, grad, put in items]
    grad_probs = [dot(v, grad, NT) for q, k, v, mask, log, out, grad, put in items]
    grad_raws = [narrow(part * (other - delta)) for part, other, delta in zip(probs, grad_probs, deltas)]
    for (q, k, v, mask, log, out, grad, put), part, grad_raw in zip(items, probs, grad_raws):
        grad_q = (dot(k, grad_raw, TN) * RAW_SCALE).T
        put(narrow(grad_q), dot(grad_raw, q, NN), dot(narrow(part), grad, NN))


def row_delta(out, grad_out):
    both = out.astype(jnp.float32) * grad_out.astype(jnp.float32)
    return jnp.sum(both.T, axis=0, keepdims=True)


def band_mask(rows, cols, key_start, query_start, window):
    key = lax.broadcasted_iota(jnp.int32, (rows, cols), 0) + key_start
    query = lax.broadcasted_iota(jnp.int32, (rows, cols), 1) + query_start
    return (key <= query) & (key > query - window)


def head_cols(head):
    return slice(head * HD, (head + 1) * HD)


def storing(out_ref, log_ref, head, at):
    def put(out, log):
        out_ref[at, head_cols(head)] = out
        log_ref[head, :, at] = log

    return put


def column(rows, offset):
    return pl.BlockSpec((rows, HD * HEADS), lambda h: (0, h + offset // HEADS))


def block_column(rows, block, offset):
    return pl.BlockSpec((rows, HD * HEADS), lambda h: (block, h + offset // HEADS))


def stat(rows):
    return pl.BlockSpec((HEADS, 1, rows), lambda h: (h, 0, 0))


def bands(rows, window):
    for start in range(0, rows, TILE):
        low = max(0, start - window)
        yield slice(start, start + TILE), slice(low, start + TILE), band_mask(start + TILE - low, TILE, low, start, window)


def self_kernel(window, q_ref, k_ref, v_ref, out_ref, log_ref):
    attend_all(
        [
            (q_ref[at, head_cols(h)], k_ref[keys, head_cols(h)], v_ref[keys, head_cols(h)], mask, storing(out_ref, log_ref, h, at))
            for h in range(HEADS)
            for at, keys, mask in bands(q_ref.shape[0], window)
        ]
    )


def self_attention(projected, window, after=()):
    rows, width = projected.shape
    heads = width // 4 // HD
    return launch(
        partial(self_kernel, window), [projected] * 3, after=after, us=17, grid=(heads // HEADS,),
        in_specs=[column(rows, 0), column(rows, 2 * heads), column(rows, 3 * heads)],
        out_specs=[column(rows, 0), stat(rows)],
        out_shape=[shaped((rows, width // 4)), shaped((heads, 1, rows), F32)],
        flops=heads * 4 * 2304 * 256 * HD, exps=heads * 2304 * 256,
    )


def cross_kernel(q_ref, k_ref, v_ref, *refs):
    out_ref, log_ref = refs[-2:]
    attend_all(
        [
            (q_ref[at, head_cols(h)], k_ref[:, head_cols(h)], v_ref[:, head_cols(h)], None, storing(out_ref, log_ref, h, at))
            for h in range(HEADS)
            for at in (slice(start, start + TILE) for start in range(0, q_ref.shape[0], TILE))
        ]
    )


def cross_attention(projected, state_side, block, before=None, after=()):
    rows, width = state_side.shape
    heads = width // 4 // HD
    operands = [projected, state_side, state_side]
    specs = [block_column(rows, block, heads), column(rows, 2 * heads), column(rows, 3 * heads)]
    if before is not None:
        operands.append(before)
        specs.append(pl.BlockSpec(memory_space=pl.ANY))
    return launch(
        cross_kernel, operands, after=after, us=10, grid=(heads // HEADS,), in_specs=specs,
        out_specs=[block_column(rows, block, 0), stat(rows)],
        out_shape=[shaped((projected.shape[0], width // 4)), shaped((heads, 1, rows), F32)],
        aliases=None if before is None else {3: 0},
        flops=heads * 4 * rows * rows * HD, exps=heads * rows * rows,
    )


def inner_kernel(live_ref, sq_ref, scq_ref, sk_ref, sv_ref, tk_ref, tv_ref, self_ref, cross_ref, self_log, cross_log):
    rows = sq_ref.shape[0]
    mask = lax.broadcasted_iota(jnp.int32, (rows, rows), 0) < live_ref[0]
    at = slice(0, rows)
    items = []
    for h in range(HEADS):
        cols_h = head_cols(h)
        items.append((sq_ref[:, cols_h], sk_ref[:, cols_h], sv_ref[:, cols_h], None, storing(self_ref, self_log, h, at)))
        items.append((scq_ref[:, cols_h], tk_ref[:, cols_h], tv_ref[:, cols_h], mask, storing(cross_ref, cross_log, h, at)))
    attend_all(items)


def inner_attention(projected, state_side, live_keys, block, after=()):
    rows, width = state_side.shape
    heads = width // 4 // HD
    return launch(
        inner_kernel, [live_keys] + [state_side] * 4 + [projected] * 2, after=after, us=17, grid=(heads // HEADS,),
        in_specs=[SMEM] + [column(rows, part * heads) for part in range(4)]
        + [block_column(rows, block, 2 * heads), block_column(rows, block, 3 * heads)],
        out_specs=[column(rows, 0)] * 2 + [stat(rows)] * 2,
        out_shape=[shaped((rows, width // 4))] * 2 + [shaped((heads, 1, rows), F32)] * 2,
        flops=heads * 8 * rows * rows * HD, exps=2 * heads * rows * rows,
    )


def self_back_kernel(window, q_ref, k_ref, v_ref, out_ref, log_ref, grad_ref, ek_ref, ev_ref, gq_ref, gk_ref, gv_ref, sk_ref, sv_ref):
    rows = q_ref.shape[0]
    extra = ek_ref.shape[0]
    sk_ref[...] = jnp.zeros_like(sk_ref)
    sv_ref[:extra, :] = ev_ref[...]
    sv_ref[extra:, :] = jnp.zeros((rows - extra, HD * HEADS), F32)

    def adding(cols_h, at, keys):
        def put(grad_q, grad_k, grad_v):
            gq_ref[at, cols_h] = grad_q
            sk_ref[keys, cols_h] += grad_k
            sv_ref[keys, cols_h] += grad_v

        return put

    for h in range(HEADS):
        cols_h = head_cols(h)
        attend_all_back(
            [
                (q_ref[at, cols_h], k_ref[keys, cols_h], v_ref[keys, cols_h], mask, log_ref[h, :, at], out_ref[at, cols_h],
                 grad_ref[at, cols_h], adding(cols_h, at, keys))
                for at, keys, mask in bands(rows, window)
            ]
        )
    gk_ref[:extra, :] = narrow(sk_ref[:extra, :] * RAW_SCALE + ek_ref[...])
    gk_ref[extra:, :] = narrow(sk_ref[extra:, :] * RAW_SCALE)
    gv_ref[...] = narrow(sv_ref[...])


def cross_back_kernel(q_ref, k_ref, v_ref, out_ref, log_ref, grad_ref, gq_ref, gk_ref, gv_ref):
    def storing_back(cols_h):
        def put(grad_q, grad_k, grad_v):
            gq_ref[:, cols_h] = grad_q
            gk_ref[:, cols_h] = narrow(grad_k * RAW_SCALE)
            gv_ref[:, cols_h] = narrow(grad_v)

        return put

    attend_all_back(
        [
            (q_ref[:, head_cols(h)], k_ref[:, head_cols(h)], v_ref[:, head_cols(h)], None, log_ref[h], out_ref[:, head_cols(h)],
             grad_ref[:, head_cols(h)], storing_back(head_cols(h)))
            for h in range(HEADS)
        ]
    )


def state_back_kernel(live_ref, cq_ref, sq_ref, scq_ref, sk_ref, sv_ref, tk_ref, tv_ref,
                      co_ref, so_ref, io_ref, cl_ref, sl_ref, il_ref, cg_ref, sg_ref, ig_ref, before_ref,
                      gcq_ref, gsq_ref, gscq_ref, gsk_ref, gsv_ref, gtk_ref, gtv_ref):
    rows = cq_ref.shape[0]
    mask = lax.broadcasted_iota(jnp.int32, (rows, rows), 0) < live_ref[0]
    for h in range(HEADS):
        cols_h = head_cols(h)
        terms = []

        def put_into(gq_ref):
            def put(grad_q, grad_k, grad_v):
                gq_ref[:, cols_h] = grad_q
                terms.append((grad_k, grad_v))

            return put

        attend_all_back(
            [
                (q_ref[:, cols_h], k_ref[:, cols_h], v_ref[:, cols_h], which, l_ref[h], o_ref[:, cols_h], g_ref[:, cols_h], put_into(gq_ref))
                for q_ref, k_ref, v_ref, o_ref, l_ref, g_ref, gq_ref, which in (
                    (cq_ref, sk_ref, sv_ref, co_ref, cl_ref, cg_ref, gcq_ref, None),
                    (sq_ref, sk_ref, sv_ref, so_ref, sl_ref, sg_ref, gsq_ref, None),
                    (scq_ref, tk_ref, tv_ref, io_ref, il_ref, ig_ref, gscq_ref, mask),
                )
            ]
        )
        gsk_ref[:, cols_h] = narrow((terms[0][0] + terms[1][0]) * RAW_SCALE)
        gsv_ref[:, cols_h] = narrow(terms[0][1] + terms[1][1])
        gtk_ref[:, cols_h] = terms[2][0] * RAW_SCALE
        gtv_ref[:, cols_h] = terms[2][1]


def self_attention_back(projected, out, log, grad_attended, extra_k, extra_v, window, after=()):
    rows, width = projected.shape
    heads = width // 4 // HD
    extra = extra_k.shape[0]
    return launch(
        partial(self_back_kernel, window), [projected] * 3 + [out, log, grad_attended, extra_k, extra_v],
        after=after, us=18, grid=(heads // HEADS,),
        in_specs=[column(rows, 0), column(rows, 2 * heads), column(rows, 3 * heads), column(rows, 0), stat(rows),
                  column(rows, 0), column(extra, 0), column(extra, 0)],
        out_specs=[column(rows, 0)] * 3, out_shape=[shaped((rows, width // 4))] * 3,
        scratch=[pltpu.VMEM((rows, HD * HEADS), F32)] * 2,
        flops=heads * 10 * 2304 * 256 * HD, exps=heads * 2304 * 256,
    )


def cross_attention_back(projected, state_side, out, log, grad_attended, block, after=()):
    rows, width = state_side.shape
    heads = width // 4 // HD
    return launch(
        cross_back_kernel, [projected, state_side, state_side, out, log, grad_attended],
        after=after, us=10, grid=(heads // HEADS,),
        in_specs=[block_column(rows, block, heads), column(rows, 2 * heads), column(rows, 3 * heads),
                  block_column(rows, block, 0), stat(rows), block_column(rows, block, heads)],
        out_specs=[block_column(rows, block, 0), column(rows, 0), column(rows, 0)],
        out_shape=[shaped((projected.shape[0], width // 4))] + [shaped((rows, width // 4))] * 2,
        flops=heads * 10 * rows * rows * HD, exps=heads * rows * rows,
    )


def state_attention_back(projected, state_side, live_keys, cross, inner_self, inner_cross, grad_attended, grad_inner, before, block, after=()):
    rows, width = state_side.shape
    heads = width // 4 // HD
    grad, wide = shaped((rows, width // 4)), shaped((rows, width // 4), F32)
    return launch(
        state_back_kernel,
        [live_keys, projected] + [state_side] * 4 + [projected] * 2
        + [cross[0], inner_self[0], inner_cross[0], cross[1], inner_self[1], inner_cross[1]]
        + [grad_attended, grad_inner, grad_inner, before],
        after=after, us=40, grid=(heads // HEADS,),
        in_specs=[SMEM, block_column(rows, block, heads)] + [column(rows, part * heads) for part in range(4)]
        + [block_column(rows, block, 2 * heads), block_column(rows, block, 3 * heads)]
        + [block_column(rows, block, 0), column(rows, 0), column(rows, 0)] + [stat(rows)] * 3
        + [block_column(rows, block, heads), column(rows, 0), column(rows, heads), pl.BlockSpec(memory_space=pl.ANY)],
        out_specs=[block_column(rows, block, 0)] + [column(rows, 0)] * 6,
        out_shape=[shaped((projected.shape[0], width // 4))] + [grad] * 4 + [wide] * 2,
        aliases={17: 0},
        flops=heads * 30 * rows * rows * HD, exps=3 * heads * rows * rows,
    )


def swap(values, axis):
    if axis == "y":
        return lax.ppermute(values, "fsdp", [(0, 1), (1, 0)])
    bit = {"core": 1, "x": 2, "z_low": 4, "z_high": 8, "z_far": 12}[axis]
    return lax.ppermute(values, "dp", [(d, d ^ bit) for d in range(16)])


LINES = [[line + 4 * z for z in range(4)] for line in range(4)]


def place():
    if not paired():
        return jnp.zeros((4,), jnp.int32)
    dp = lax.axis_index("dp")
    return jnp.stack([(dp // 2) % 2, dp % 2, lax.axis_index("fsdp"), dp // 4]).astype(jnp.int32)


def fence_kernel(*refs):
    pass


def fence(arrays, after):
    return launch(
        fence_kernel, arrays, after=after, us=1, grid=(1,),
        in_specs=[pl.BlockSpec(memory_space=pl.ANY)] * len(arrays),
        out_specs=[pl.BlockSpec(memory_space=pl.ANY)] * len(arrays),
        out_shape=[shaped(item.shape, item.dtype) for item in arrays],
        aliases={i: i for i in range(len(arrays))}, flops=0,
    )


def stacked(block):
    return [block[:, i : i + COLS] for i in range(0, block.shape[1], COLS)]


def gather_blocks(blocks):
    packed = jnp.concatenate([part for block in blocks for part in stacked(block)], axis=0)
    return cut(lax.all_gather(packed, ("dp", "fsdp"), axis=0).reshape(16, 2, *packed.shape), blocks)


def cut(every, blocks):
    weights, row = [], 0
    for block in blocks:
        weights.append((every, row, block.shape[0]))
        row += block.shape[0] * block.shape[1] // COLS
    return weights


def spell_kernel(place_ref, *refs):
    x, core, y = place_ref[0], place_ref[1], place_ref[2]
    pieces, out = refs[:-1], refs[-1]
    for other in range(2):
        line, over_x, over_y, low, high = pieces[5 * other : 5 * other + 5]
        at = core ^ other
        out[0, x, at, y] = line[0]
        out[0, 1 - x, at, y] = over_x[0]
        out[0, x, at, 1 - y] = over_y[0]
        far = jnp.where(pl.program_id(0) < 2, low[0], high[0])
        out[0, 1 - x, at, 1 - y] = far


def fence_kernel(*refs):
    pass


def fence(arrays, after):
    return launch(
        fence_kernel, arrays, after=after, us=1, grid=(1,),
        in_specs=[pl.BlockSpec(memory_space=pl.ANY)] * len(arrays),
        out_specs=[pl.BlockSpec(memory_space=pl.ANY)] * len(arrays),
        out_shape=[shaped(item.shape, item.dtype) for item in arrays],
        aliases={i: i for i in range(len(arrays))}, flops=0,
    )


class Gather:
    def __init__(self, blocks, where):
        self.where, self.blocks = where, blocks
        self.packed = jnp.concatenate([part for block in blocks for part in stacked(block)], axis=0)

    def start(self, after):
        packed = fence([self.packed], after)[0] if after else self.packed
        self.line = jnp.stack([packed] + [swap(packed, axis) for axis in ("z_low", "z_high", "z_far")])
        return (packed,)

    def near(self, after):
        (line,) = fence([self.line], after)
        self.over = swap(line, "x"), swap(line, "y")
        self.pieces = [line]
        return (line,)

    def far(self, after):
        over_x, over_y = fence(self.over, after)
        self.last = swap(over_x[:2], "y"), swap(over_y[2:], "x")
        self.pieces += [over_x, over_y]
        return (over_x,)

    def cross(self, after):
        low, high = fence(self.last, after)
        self.pieces += [low, high]
        self.pieces += [swap(piece, "core") for piece in self.pieces]
        return (low,)

    def whole(self, after):
        rows = self.packed.shape[0]

        def spec(low, high):
            return pl.BlockSpec((1, rows, COLS), lambda i, p: (jnp.clip(i, low, high - 1) - low, 0, 0))

        (every,) = launch(
            spell_kernel, self.pieces, where=self.where, after=after, us=7, grid=(4,),
            in_specs=[spec(0, 4), spec(0, 4), spec(0, 4), spec(0, 2), spec(2, 4)] * 2,
            out_specs=[pl.BlockSpec((1, 2, 2, 2, rows, COLS), lambda i, p: (i ^ p[3], 0, 0, 0, 0, 0))],
            out_shape=[shaped((4, 2, 2, 2, rows, COLS))], flops=0,
        )
        return cut(every.reshape(16, 2, rows, COLS), self.blocks)


def add(*terms):
    return sum(term.astype(F32) for term in terms)


def fold_core_kernel(place_ref, keep_ref, come_ref, low_ref, high_ref, px_ref, py_ref, own_ref):
    x, y = place_ref[0], place_ref[2]
    cols = own_ref.shape[-1]

    def fold(out, dx, dy):
        at = pl.ds(pl.multiple_of((y ^ dy) * cols, 128), cols)
        for z in range(out.shape[0]):
            out[z] = narrow(add(keep_ref[z, x ^ dx, :, at], come_ref[z, x ^ dx, :, at]))

    fold(own_ref, 0, 0)
    fold(px_ref, 1, 0)
    fold(py_ref, 0, 1)
    pl.when(pl.program_id(0) == 0)(lambda: fold(low_ref, 1, 1))
    pl.when(pl.program_id(0) == 1)(lambda: fold(high_ref, 1, 1))


def fold_core(keep, come, where, after=()):
    _, _, rows, cols = keep.shape
    pair = pl.BlockSpec((2, 2, rows, cols), lambda i, p: (i, 0, 0, 0))
    full = pl.BlockSpec((2, rows, cols // 2), lambda i, p: (i, 0, 0))
    half = pl.BlockSpec((2, rows, cols // 2), lambda i, p: (0, 0, 0))
    return launch(
        fold_core_kernel, [keep, come], where=where, after=after, us=5, grid=(2,),
        in_specs=[pair, pair], out_specs=[half, half, full, full, full],
        out_shape=[shaped((2, rows, cols // 2))] * 2 + [shaped((4, rows, cols // 2))] * 3,
        flops=keep.size,
    )


def fold_mid_kernel(px_ref, py_ref, rx_ref, ry_ref, px_out, py_out):
    px_out[...] = narrow(add(px_ref[...], ry_ref[...]))
    py_out[...] = narrow(add(py_ref[...], rx_ref[...]))


def fold_mid(px, py, rx, ry, after=()):
    block = rx.shape
    low = pl.BlockSpec(block, lambda i: (0, 0, 0))
    high = pl.BlockSpec(block, lambda i: (1, 0, 0))
    return launch(
        fold_mid_kernel, [px, py, rx, ry], after=after, us=2, grid=(1,),
        in_specs=[high, low, low, low], out_specs=[high, low],
        out_shape=[shaped(px.shape), shaped(py.shape)], aliases={0: 0, 1: 1}, flops=px.size,
    )


def fold_last_kernel(own_ref, rx_ref, ry_ref, out_ref):
    out_ref[...] = narrow(add(own_ref[...], rx_ref[...], ry_ref[...]))


def fold_last(own, rx, ry, us, after=()):
    _, rows, cols = own.shape
    block = pl.BlockSpec((2, rows, cols), lambda i: (i, 0, 0))
    return launch(
        fold_last_kernel, [own, rx, ry], after=after, us=us, grid=(2,),
        in_specs=[block] * 3, out_specs=[block], out_shape=[shaped(own.shape)], flops=2 * own.size,
    )[0]


def widen_kernel(cuts, sum_ref, *outs):
    for out, (row, rows, parts, cols) in zip(outs, cuts):
        for part in range(parts):
            out[part * rows : (part + 1) * rows, :] = sum_ref[
                row : row + rows, part * cols : (part + 1) * cols
            ].astype(F32)


class Scatter:
    def __init__(self, keep, send, where):
        self.where, self.keep = where, keep
        self.come = swap(send, "core")

    def step(self, after, us):
        self.us = us
        self.steps = getattr(self, "steps", 0) + 1
        return (self.core, self.mid, self.last)[self.steps - 1](after)

    def core(self, after):
        low, high, self.px, self.py, self.own = fold_core(self.keep, self.come, self.where, after)
        self.rx, self.ry = swap(low, "x"), swap(high, "y")
        return (self.own,)

    def mid(self, after):
        px, py = fold_mid(self.px, self.py, self.rx, self.ry, after)
        self.one, self.two = swap(px, "x"), swap(py, "y")
        return (px,)

    def last(self, after):
        line = fold_last(self.own, self.one, self.two, self.us, after)
        rows, cols = line.shape[1:]
        self.out = lax.psum_scatter(
            line.reshape(4 * rows, cols), "dp", scatter_dimension=0, axis_index_groups=LINES, tiled=True
        )
        return (line,)

    def widen(self, cuts, after):
        outs = launch(
            partial(widen_kernel, cuts), [self.out], after=after, us=1, grid=(1,),
            in_specs=[whole(self.out.shape)], out_specs=[whole((rows * parts, cols)) for _, rows, parts, cols in cuts],
            out_shape=[shaped((rows * parts, cols), F32) for _, rows, parts, cols in cuts], flops=0,
        )
        return outs


def paired():
    return lax.axis_size("dp") == 16 and lax.axis_size("fsdp") == 2


def gather_plain(block):
    full = lax.all_gather(lax.all_gather(block, "fsdp", axis=1, tiled=True), "dp", axis=0, tiled=True)
    rows, cols = full.shape[0] // 16, full.shape[1]
    cut = full.reshape(16, rows, 2, cols // 2 // COLS, COLS).transpose(0, 2, 3, 1, 4)
    return cut.reshape(16, 2, -1, COLS), 0, rows


def scatter_plain(grad):
    rows = lax.psum_scatter(grad, "dp", scatter_dimension=0, tiled=True)
    return lax.psum_scatter(rows, "fsdp", scatter_dimension=1, tiled=True)


def gather_vectors(vectors):
    if not paired():
        return lax.all_gather(vectors, "fsdp", axis=1, tiled=True).astype(F32)
    other = swap(vectors, "y")
    first = lax.axis_index("fsdp") == 0
    return jnp.concatenate(
        [jnp.where(first, vectors, other), jnp.where(first, other, vectors)], axis=1
    ).astype(F32)


def scatter_vectors(vectors):
    part = vectors.shape[1] // lax.axis_size("fsdp")
    y = lax.axis_index("fsdp")
    if not paired():
        total = lax.psum(vectors, ("dp", "fsdp"))
        return lax.dynamic_slice_in_dim(total, y * part, part, axis=1)
    low, high = vectors[:, :part], vectors[:, part:]
    total = jnp.where(y == 0, low, high) + swap(jnp.where(y == 0, high, low), "y")
    for axis in ("core", "x", "z_low", "z_high"):
        total = total + swap(total, axis)
    return total


def shards(
    tokens,
    incoming,
    document_lengths,
    output_grad,
    token_proj,
    state_proj,
    token_out,
    state_out,
    gate_weight,
    init_state,
    hidden_in,
    hidden_out,
    token_gain,
    state_gain,
    hidden_gain,
    gate_bias,
):
    seg_len, width = tokens.shape
    window = WINDOW
    states = incoming.shape[1]
    where = place()
    segment_id = lax.axis_index(("dp", "fsdp"))
    counts = (document_lengths + seg_len - 1) // seg_len
    ends = jnp.cumsum(counts)
    starts = ends - counts
    inside = (segment_id >= starts) & (segment_id < ends)
    valid_len = jnp.sum(
        jnp.where(
            inside, jnp.minimum(seg_len, document_lengths - (segment_id - starts) * seg_len), 0
        )
    )
    first = jnp.any(segment_id == starts)
    lives = [jnp.where(b * window < valid_len, 1.0, 0.0).astype(F32).reshape(1) for b in range(2)]
    live_keys = [jnp.clip(valid_len - b * window, 0, window).astype(jnp.int32).reshape(1) for b in range(2)]

    gains = gather_vectors(jnp.stack([token_gain, state_gain, hidden_gain, gate_bias]))
    token_gain_f, state_gain_f, hidden_gain_f, gate_bias_f = [gains[i : i + 1] for i in range(4)]
    order = ()

    if paired():
        first_gather, second_gather = Gather([token_proj], where), Gather([state_proj, init_state], where)
        order = first_gather.start(order)
        order = first_gather.near(order)
        order = second_gather.start(order)
        order = first_gather.far(order)
        order = second_gather.near(order)
        opening, *scalars = fence([jnp.where(first, 1.0, 0.0).astype(F32).reshape(1), *lives, *live_keys], order)
        lives, live_keys = scalars[:2], scalars[2:]
        order = (opening,)
        order = first_gather.cross(order)
        (full_token_proj,) = first_gather.whole(order)
        full_hidden_in, full_state_out, full_token_out, full_gate_weight = gather_blocks(
            [hidden_in, state_out, token_out, gate_weight]
        )
        (full_hidden_out,) = gather_blocks([hidden_out])
    else:
        opening = jnp.where(first, 1.0, 0.0).astype(F32).reshape(1)
        (
            full_token_proj, full_state_proj, full_state_out, full_gate_weight, full_init, full_token_out, full_hidden_in,
            full_hidden_out,
        ) = [
            gather_plain(block)
            for block in (
                token_proj, state_proj, state_out, gate_weight, init_state, token_out, hidden_in, hidden_out,
            )
        ]
    normed, projected = norm_project(tokens, token_gain_f, full_token_proj, order)
    order = (projected,)
    if paired():
        order = second_gather.far(order)
    self_out, self_log = self_attention(projected, window, order)
    order = (self_log,)
    if paired():
        order = second_gather.cross(order)
        full_state_proj, full_init = second_gather.whole(order)
    array, row, rows = full_init
    full_init = array[:, :, row : row + rows].transpose(0, 2, 1, 3).reshape(states, width)
    state_0 = jnp.where(opening[0] > 0.0, full_init, incoming[0]).astype(F32)
    normed_0, side_0 = norm_project(state_0, state_gain_f, full_state_proj, order)
    order = (side_0,)
    inner_self_0, inner_cross_0, inner_self_log, inner_cross_log = inner_attention(
        projected, side_0, live_keys[0], 0, order
    )
    order = (inner_self_log,)
    mixed_0, gate_0, state_1 = update_state(
        lives[0], inner_self_0, inner_cross_0, full_state_out, full_gate_weight, gate_bias_f, state_0, order
    )
    order = (mixed_0,)
    normed_1, side_1 = norm_project(state_1, state_gain_f, full_state_proj, order)
    order = (normed_1,)
    cross_out, cross_log_0 = cross_attention(projected, side_0, 0, None, order)
    order = (cross_log_0,)
    cross_out, cross_log_1 = cross_attention(projected, side_1, 1, cross_out, order)
    order = (cross_log_1,)
    middle, hidden_normed = branch(self_out, cross_out, full_token_out, tokens, hidden_gain_f, order)
    order = (hidden_normed,)
    active, slope = hidden(hidden_normed, full_hidden_in, order)
    order = (active,)

    def weight(us, *jobs, extra=None):
        nonlocal order
        if paired():
            keep, send = weight_grad(jobs, where, us, extra, order)
            order = (keep,)
            return Scatter(keep, send, where)
        plain = []
        for lefts, rights, plan, split in jobs:
            if split:
                lefts = [jnp.concatenate(lefts, axis=1)]
            grad = jnp.concatenate(
                [sum(matmul_left_t(lefts[a], rights[b]) for a, b in terms) for terms in plan], axis=1
            )
            plain.append(scatter_plain(narrow(grad)).astype(F32))
        if extra is not None:
            plain.append(scatter_plain(extra).astype(F32))
        return plain

    def sums(scatter, *cuts):
        nonlocal order
        if not paired():
            return scatter
        outs = scatter.widen(cuts, order)
        order = (outs[0],)
        return outs

    def fold(scatter, us=3):
        nonlocal order
        if paired():
            order = scatter.step(order, us)

    one = [[(0, 0)]]
    scatter_hidden_out = weight(14, ([active], [output_grad], one, False))
    result, grad_pre = result_and_pre(active, slope, full_hidden_out, middle, output_grad, order)
    order = (result,)
    fold(scatter_hidden_out)
    scatter_hidden_in = weight(15, ([hidden_normed], [grad_pre], one, False))
    grad_hidden_gain, grad_branch, grad_middle = norm_back_project(
        [grad_pre], full_hidden_in, middle, hidden_gain_f, output_grad, 40, True, after=order
    )
    order = (grad_hidden_gain,)
    fold(scatter_hidden_out)
    fold(scatter_hidden_in)
    grad_attended = spread(grad_branch, full_token_out, order)
    order = (grad_attended,)
    grad_cross, grad_keys_1, grad_values_1 = cross_attention_back(
        projected, side_1, cross_out, cross_log_1, grad_attended, 1, order
    )
    order = (grad_keys_1,)
    no_term = jnp.zeros((states, width), jnp.bfloat16)
    grad_state_gain_1, _, grad_state_1 = norm_back_project(
        [grad_keys_1, grad_values_1], full_state_proj, state_1, state_gain_f, no_term, 9, True,
        offset=2 * width, after=order,
    )
    order = (grad_state_gain_1,)
    fold(scatter_hidden_out)
    fold(scatter_hidden_in)
    grad_gate_low, grad_mixed, grad_inner, grad_direct, grad_gate_bias = gate_back(
        lives[0], grad_state_1, gate_0, state_0, mixed_0, full_gate_weight, full_state_out, order
    )
    order = (grad_gate_bias,)
    scatter_out = weight(
        16,
        ([self_out, cross_out], [grad_branch], one, True),
        ([inner_self_0, inner_cross_0], [grad_mixed], one, True),
        ([mixed_0], [grad_gate_low], one, False),
    )
    parts = state_attention_back(
        projected, side_0, live_keys[0], (cross_out, cross_log_0), (inner_self_0, inner_self_log),
        (inner_cross_0, inner_cross_log), grad_attended, grad_inner, grad_cross, 0, order,
    )
    grad_cross, grads_side_0, extra_keys, extra_values = parts[0], parts[1:5], parts[5], parts[6]
    order = (extra_keys,)
    fold(scatter_hidden_in)
    fold(scatter_out)
    (hidden_out_sum,) = sums(scatter_hidden_out, (0, 256, 1, 512))
    scatter_state_proj = weight(
        13,
        (
            [normed_0, normed_1],
            [*grads_side_0, grad_keys_1, grad_values_1],
            [[(0, 0)], [(0, 1)], [(0, 2), (1, 4)], [(0, 3), (1, 5)]],
            False,
        ),
    )
    grad_state_gain_0, grad_init = norm_back_project(
        grads_side_0, full_state_proj, state_0, state_gain_f, grad_direct, 40, scale=opening, after=order,
    )
    order = (grad_state_gain_0,)
    fold(scatter_out)
    fold(scatter_state_proj)
    grad_self, grad_keys, grad_values = self_attention_back(
        projected, self_out, self_log, grad_attended, extra_keys, extra_values, window, order
    )
    order = (grad_self,)
    fold(scatter_state_proj)
    fold(scatter_out)
    (hidden_in_sum,) = sums(scatter_hidden_in, (0, 64, 1, 2048))
    grads_projected = [grad_self, grad_cross, grad_keys, grad_values]
    scatter_token_proj = weight(
        15, ([normed], grads_projected, [[(0, i)] for i in range(4)], False), extra=grad_init
    )
    fold(scatter_state_proj, 40)
    fold(scatter_token_proj)
    inner_self_1, inner_cross_1, log, _ = inner_attention(projected, side_1, live_keys[1], 1, order)
    order = (log,)
    fold(scatter_token_proj)
    grad_token_gain, tokens_grad = norm_back_project(
        grads_projected, full_token_proj, tokens, token_gain_f, grad_middle, 20, after=order
    )
    order = (grad_token_gain,)
    token_out_sum, state_out_sum, gate_sum = sums(scatter_out, (0, 128, 1, 512), (128, 128, 1, 512), (256, 64, 1, 512))
    fold(scatter_token_proj)
    vectors = jnp.concatenate(
        [grad_token_gain, grad_state_gain_0 + grad_state_gain_1, grad_hidden_gain, grad_gate_bias], axis=0
    )
    vector_grads = scatter_vectors(fence([vectors], order)[0])
    _, _, state_2 = update_state(
        lives[1], inner_self_1, inner_cross_1, full_state_out, full_gate_weight, gate_bias_f, state_1, order
    )
    order = (state_2,)
    (state_proj_sum,) = sums(scatter_state_proj, (0, 64, 1, 2048))
    token_proj_sum, init_sum = sums(scatter_token_proj, (0, 64, 1, 2048), (64, 16, 2, 512))
    matrix_grads = [
        token_proj_sum, state_proj_sum, token_out_sum, state_out_sum, gate_sum, init_sum, hidden_in_sum, hidden_out_sum,
    ]
    return (
        result,
        narrow(state_2)[None],
        tokens_grad,
        *matrix_grads,
        *[vector_grads[i] for i in range(4)],
    )


def solution(mesh):
    return jax.shard_map(
        shards,
        mesh=mesh,
        in_specs=(
            P(("dp", "fsdp"), None),
            P(("dp", "fsdp"), None, None),
            P(),
            P(("dp", "fsdp"), None),
            P("dp", "fsdp"),
            P("dp", "fsdp"),
            P("dp", "fsdp"),
            P("dp", "fsdp"),
            P("dp", "fsdp"),
            P("dp", "fsdp"),
            P("dp", "fsdp"),
            P("dp", "fsdp"),
            P("fsdp"),
            P("fsdp"),
            P("fsdp"),
            P("fsdp"),
        ),
        out_specs=(
            P(("dp", "fsdp"), None),
            P(("dp", "fsdp"), None, None),
            P(("dp", "fsdp"), None),
            P("dp", "fsdp"),
            P("dp", "fsdp"),
            P("dp", "fsdp"),
            P("dp", "fsdp"),
            P("dp", "fsdp"),
            P("dp", "fsdp"),
            P("dp", "fsdp"),
            P("dp", "fsdp"),
            P("fsdp"),
            P("fsdp"),
            P("fsdp"),
            P("fsdp"),
        ),
        check_vma=False,
    )
```
